32 devices in a mesh: groups: 1, ctx: 16 (over z, y, core), tp: 2 (over x), sub: 1.
Axes of the slice: x: 2, y: 2, z: 4, core: 2. Of those that a mesh axis runs over, the one named last changes fastest.
Arguments:
- resid: bfloat16 [1024, 4096], P(('groups', 'ctx'), ('tp', 'sub')), may hold values from -8 to 8
- query: bfloat16 [1024, 4096], P(('groups', 'ctx'), ('tp', 'sub')), may hold values from -6 to 6
- key: bfloat16 [1024, 4096], P(('groups', 'ctx'), ('tp', 'sub')), may hold values from -6 to 6
- value: bfloat16 [1024, 4096], P(('groups', 'ctx'), ('tp', 'sub')), may hold values from -6 to 6
- norm_gain: bfloat16 [4096], P(('tp', 'sub')), may hold values from 0.099609375 to 1.8984375
- routes: int32 [1024, 4], P(('groups', 'ctx')), may hold values from 0 to 7, all different within a row; in each aligned block of 64 rows (0 to 63, 64 to 127, ...) at most 40 rows name the same one
- route_gates: float32 [1024, 4], P(('groups', 'ctx')), may hold values from 0.05 to 1
- segment_ids: int32 [1024], P(('groups', 'ctx')), may hold values from 0 to 31, never falling along the last dimension, each value on 1 to 512 neighbouring positions
- w_gate: bfloat16 [16, 4096, 1024], P('ctx', None, ('tp', 'sub')), may hold values from -0.09375 to 0.09375
- w_up: bfloat16 [16, 4096, 1024], P('ctx', None, ('tp', 'sub')), may hold values from -0.09375 to 0.09375
- w_down: bfloat16 [16, 1024, 4096], P('ctx', None, ('tp', 'sub')), may hold values from -0.125 to 0.125
Outputs:
- layer_out: bfloat16 [1024, 4096], P(('groups', 'ctx'), ('tp', 'sub'))
The draws below stay inside these ranges and needn't reach their ends.
Inputs may be any that keep to these rules, and one draw needn't show every extreme that they name: `routes`: in each aligned block of 64 positions no expert is chosen more than 40 times, a bound that some block reaches; the experts of one position differ. `segment_ids`: segment numbers never fall along the window; one segment has exactly 512 positions.
All inputs are finite; a program needn't handle non-finite values.
Results may differ from the reference program's by a relative error of at most 0.0065.
Values may be sent and summed in bfloat16 or wider, within the bound.
No kernel may reach another device: no remote copies, remote signals or barrier semaphores. Data moves between devices by JAX's collectives and lax.ppermute only.
A program may use at most 64 MiB of HBM per device.

```python
import math
import jax
import jax.numpy as jnp
import numpy as np
from jax import lax

D = 4096
HEADS = 32
HD = 128
FFE = 2048
TOPK = 4
TOK_CTX = 64
LENGTH = 1024
EXPERTS = 8
CAP = 40
ROWS = 640
N_CTX = 16


def draw_resid(key, part):
    base_key = jax.random.fold_in(key, 11)
    first_key, second_key = jax.random.split(base_key, 2)
    column = jnp.arange(D, dtype=jnp.float32) / D
    column_scale = 0.25 * jnp.power(3.0, column) * jax.random.uniform(second_key, (D,), jnp.float32, 0.6, 1.4)
    base = jnp.clip(jax.random.normal(first_key, (LENGTH, D), jnp.float32), -6.0, 6.0)
    return (base * column_scale[None, :]).astype(jnp.bfloat16)


def level_of(key, shape, pieces, least, largest):
    def one(axis_at, blocks):
        draws = jax.random.uniform(jax.random.fold_in(jax.random.fold_in(key, 6), axis_at), (blocks,), jnp.float32, least / len(pieces), largest / len(pieces))
        return jnp.repeat(jnp.exp(draws), shape[axis_at] // blocks).reshape((-1,) + (1,) * (len(shape) - axis_at - 1))

    gain = one(*pieces[0])
    for cut in pieces[1:]:
        gain = gain * one(*cut)
    return gain


def split_up(number_of, total, bound, slope):
    portions = [(1 << 20) // math.isqrt(rank ** slope) + 1 for rank in range(2, number_of + 1)]
    surplus, counts = total - bound - (number_of - 1), [1] * (number_of - 1)
    while surplus > 0:
        candidates = [i for i in range(number_of - 1) if counts[i] < bound]
        whole, left = sum([portions[i] for i in candidates]), surplus
        for i in candidates:
            addition = min(bound - counts[i], max(1, left * portions[i] // whole), surplus)
            counts[i] = counts[i] + addition
            surplus = surplus - addition
    return np.array([bound] + counts)


def uneven_parts(key, number_of, total, most, lean):
    if number_of == 2:
        one = jax.random.randint(key, (), max(1, total - most), min(most, total - 1) + 1)
        return jnp.stack([one, total - one])
    tallies = jnp.asarray(split_up(number_of, total, most, lean), jnp.int32)
    couples = (number_of - 1) // 2
    giver, receiver = tallies[1:1 + 2 * couples:2], tallies[2:2 + 2 * couples:2]
    margin = jnp.minimum(giver - 1, most - receiver)
    shifted = jax.random.randint(jax.random.fold_in(key, 1), (couples,), 0, 1 << 20) % (margin + 1)
    tallies = tallies.at[1:1 + 2 * couples:2].set(giver - shifted).at[2:2 + 2 * couples:2].set(receiver + shifted)
    return tallies[jax.random.permutation(jax.random.fold_in(key, 2), number_of)]


def shared_out(key, own, number, rows, amount, top, reach, skew):
    sequence = jax.random.permutation(key, amount)
    packed, common = shares(amount, rows * top, reach, skew, True), shares(amount, rows * top, reach, skew, False)
    places = jnp.arange(amount)

    def named(lengths, turn):
        used = int((lengths > 0).sum())
        fixed = max(1, used // 4)
        passed = fixed + (places - fixed + turn * (used - fixed)) % max(1, amount - fixed)
        return jnp.zeros((amount,), jnp.int32).at[sequence[jnp.where(places < fixed, places, passed)]].set(jnp.asarray(lengths, jnp.int32))

    lengths = jnp.where(number % 4 == 0, named(packed, number // 4), named(common, number - number // 4 - 1))
    mixed = jax.random.permutation(jax.random.fold_in(own, 3), amount)
    giver, taker = mixed[0:amount // 2 * 2:2], mixed[1:amount // 2 * 2:2]
    slack = jnp.minimum(lengths[giver] - 1, reach - lengths[taker]) // 2
    slack = jnp.where((giver == sequence[0]) | (taker == sequence[0]) | (lengths[taker] == 0), 0, jnp.maximum(slack, 0))
    passed = jax.random.randint(jax.random.fold_in(own, 4), (amount // 2,), 0, 1 << 20) % (slack + 1)
    lengths = lengths.at[giver].add(-passed).at[taker].add(passed)
    items = jnp.searchsorted(jnp.cumsum(lengths), jnp.arange(rows * top), side="right").astype(jnp.int32)
    table = items.reshape(top, rows).T
    table = table[jax.random.permutation(jax.random.fold_in(own, 1), rows)]
    turn = jax.random.randint(jax.random.fold_in(own, 2), (rows, 1), 0, top)
    return jnp.take_along_axis(table, (jnp.arange(top)[None, :] + turn) % top, axis=1)


def shares(number_of, total, limit, lean, full):
    portions = [(1 << 20) // math.isqrt(standing ** lean) + 1 for standing in range(1, number_of + 1)]
    largest = limit if full else min(limit, max(-(-total // number_of), total * portions[0] // sum(portions)))
    least = 1 if total - largest >= number_of - 1 else 0
    holding, rest = [largest] + [least] * (number_of - 1), total - largest - least * (number_of - 1)
    while rest > 0:
        free = [i for i in range(1, number_of) if holding[i] < largest] or [i for i in range(1, number_of) if holding[i] < limit]
        mass, left = sum([portions[i] for i in free]), rest
        for i in free:
            addition = min(limit - holding[i], max(1, left * portions[i] // mass), rest)
            holding[i] = holding[i] + addition
            rest = rest - addition
    return np.array(holding)


def normal_values(rng, dims, spread, reach, cuts=(), held_as=jnp.bfloat16):
    entries = jax.random.normal(rng, dims, jnp.float32) * spread
    if len(cuts) > 0:
        entries = level_of(rng, dims, cuts, -0.22, 0.18) * entries
    return jnp.clip(entries, min=-reach, max=reach).astype(held_as)


def setup_inputs(seed: int = 0, part: int = 0) -> dict:
    key_list = jax.random.split(jax.random.key(seed), 12)
    part_splits = jax.random.split(jax.random.fold_in(key_list[11], part), 12)
    resid = draw_resid(jax.random.fold_in(jax.random.fold_in(key_list[11], part), 71), part)
    query = normal_values(part_splits[1], (LENGTH, D), 1.0, 6.0, ((0, 16), (1, 2)))
    key = normal_values(part_splits[2], (LENGTH, D), 1.0, 6.0, ((0, 16), (1, 2)))
    value = normal_values(part_splits[3], (LENGTH, D), 1.0, 6.0, ((0, 16), (1, 2)))
    norm_gain = jnp.clip(1.0 + 0.18 * jax.random.normal(key_list[4], (D,), jnp.float32), 0.099609375, 1.8984375).astype(jnp.bfloat16)
    routes_keys = jax.random.split(jax.random.fold_in(part_splits[5], 1), LENGTH // TOK_CTX)
    routes_turns = jax.random.permutation(jax.random.fold_in(part_splits[5], 3), LENGTH // TOK_CTX)
    routes = jax.vmap(lambda own, number: shared_out(jax.random.fold_in(part_splits[5], 2), own, number, TOK_CTX, EXPERTS, TOPK, CAP, 2))(routes_keys, routes_turns).reshape((LENGTH, TOPK))
    route_gates = jnp.clip(jnp.exp(math.log(1.0) - 2.9957323 * jax.random.uniform(part_splits[6], (LENGTH, TOPK), jnp.float32) ** level_of(part_splits[6], (LENGTH, TOPK), ((0, 16),), -0.2, 0.2)), 0.05, 1.0)
    segment_ids = jnp.searchsorted(jnp.cumsum(uneven_parts(part_splits[7], 2 * N_CTX, LENGTH, LENGTH // 2, 2)), jnp.arange(LENGTH), side="right").astype(jnp.int32)
    w_gate = normal_values(key_list[8], (2 * EXPERTS, D, FFE // 2), D ** -0.5, 0.09375, ((0, 16), (2, 2)))
    w_up = normal_values(key_list[9], (2 * EXPERTS, D, FFE // 2), D ** -0.5, 0.09375, ((0, 16), (2, 2)))
    w_down = normal_values(key_list[10], (2 * EXPERTS, FFE // 2, D), FFE ** -0.5, 0.125, ((0, 16), (2, 2)))
    return dict(resid=resid, query=query, key=key, value=value, norm_gain=norm_gain, routes=routes, route_gates=route_gates, segment_ids=segment_ids, w_gate=w_gate, w_up=w_up, w_down=w_down)


def attend_all(query, key, value, segment_ids):
    query_heads = query.reshape(LENGTH, HEADS, HD).astype(jnp.float32)
    key_heads = key.reshape(LENGTH, HEADS, HD).astype(jnp.float32)
    value_heads = value.reshape(LENGTH, HEADS, HD).astype(jnp.float32)
    key_pos = jnp.arange(LENGTH, dtype=jnp.int32)
    block_len = math.gcd(LENGTH, 512)
    score_scale = 1.0 / math.sqrt(HD)

    def one_block(first_row):
        query_block = lax.dynamic_slice_in_dim(query_heads, first_row, block_len, 0)
        query_segs = lax.dynamic_slice_in_dim(segment_ids, first_row, block_len, 0)
        query_pos = first_row + jnp.arange(block_len, dtype=jnp.int32)
        visible = jnp.logical_and(segment_ids[None, :] == query_segs[:, None], key_pos[None, :] <= query_pos[:, None]).astype(jnp.float32)
        scores = jnp.einsum('thd,shd->hts', query_block, key_heads) * score_scale
        weights = (jax.nn.silu(scores) * visible[None]).astype(jnp.bfloat16)
        summed = jnp.einsum('hts,shd->thd', weights.astype(jnp.float32), value_heads)
        counted = lax.optimization_barrier(jnp.sum(visible, axis=1))
        return summed.reshape(block_len, D) / jnp.sqrt(counted)[:, None]
    firsts = jnp.arange(LENGTH // block_len, dtype=jnp.int32) * block_len
    return lax.map(one_block, firsts).reshape(LENGTH, D)

def run_expert(operands):
    row_block, gate_w, up_w, down_w = operands
    gate_sum = jnp.dot(row_block, gate_w, preferred_element_type=jnp.float32)
    up_sum = jnp.dot(row_block, up_w, preferred_element_type=jnp.float32)
    hidden = (jax.nn.silu(gate_sum) * up_sum).astype(jnp.bfloat16)
    return jnp.dot(hidden, down_w, preferred_element_type=jnp.float32).astype(jnp.bfloat16)

def reference(resid, query, key, value, norm_gain, routes, route_gates, segment_ids, w_gate, w_up, w_down):
    attended = attend_all(query, key, value, segment_ids)
    hand_state = (resid.astype(jnp.float32) + attended).astype(jnp.bfloat16)
    hand_f32 = hand_state.astype(jnp.float32)
    square_sums = lax.optimization_barrier(jnp.sum(hand_f32 * hand_f32, axis=1))
    normed = (hand_f32 * lax.rsqrt(square_sums / D + 1e-06)[:, None] * norm_gain.astype(jnp.float32)).astype(jnp.bfloat16)
    flat_routes = routes.reshape(-1)
    onehot = (flat_routes[:, None] == jnp.arange(EXPERTS, dtype=jnp.int32)[None, :]).astype(jnp.int32)
    slot_rank = lax.optimization_barrier(jnp.sum((jnp.cumsum(onehot, axis=0) - 1) * onehot, axis=1))
    slot_index = (flat_routes * ROWS + slot_rank).astype(jnp.int32)
    position = (jnp.arange(LENGTH * TOPK, dtype=jnp.int32) // TOPK).astype(jnp.int32)
    slot_source = jnp.full((EXPERTS * ROWS,), LENGTH, jnp.int32).at[slot_index].set(position)
    padded = jnp.concatenate([normed, jnp.zeros((1, D), jnp.bfloat16)], axis=0)
    expert_rows = padded[slot_source].reshape(EXPERTS, ROWS, D)
    doubled = jnp.repeat(expert_rows, 2, axis=0)
    halves = lax.map(run_expert, (doubled, w_gate, w_up, w_down))
    expert_out = lax.optimization_barrier(jnp.sum(halves.reshape(EXPERTS, 2, ROWS, D).astype(jnp.float32), axis=1)).reshape(EXPERTS * ROWS, D)
    picked = expert_out[slot_index].reshape(LENGTH, TOPK, D)
    mixed = hand_f32 + lax.optimization_barrier(jnp.sum(route_gates[:, :, None] * picked, axis=1))
    return mixed.astype(jnp.bfloat16)
```

```python
import functools
import math

import jax
import jax.numpy as jnp
from jax import lax
from jax.experimental import pallas as pl
from jax.experimental.pallas import tpu as pltpu
from jax.sharding import PartitionSpec as P

D = 4096
HD = 128
TOPK = 4
EPS = 1e-06
META = 16
LANES = 128
MIB = 1 << 20


def silu(v):
    return v * (0.5 * jnp.tanh(0.5 * v) + 0.5)


def call(kernel, out_shape, args, smem=0, scratch=(), vmem=24, flops=0, moved=0):
    specs = [pl.BlockSpec(memory_space=pltpu.SMEM)] * smem
    specs += [pl.BlockSpec(memory_space=pltpu.VMEM)] * (len(args) - smem)
    several = isinstance(out_shape, (tuple, list))
    out = pl.BlockSpec(memory_space=pltpu.VMEM)
    return pl.pallas_call(
        kernel,
        out_shape=out_shape,
        in_specs=specs,
        out_specs=tuple(out for _ in out_shape) if several else out,
        scratch_shapes=list(scratch),
        compiler_params=pltpu.CompilerParams(vmem_limit_bytes=vmem * MIB),
        cost_estimate=pl.CostEstimate(flops=flops, bytes_accessed=moved, transcendentals=0),
    )(*args)


def pack_kernel(q_ref, k_ref, v_ref, r_ref, seg_ref, gate_ref, out_ref):
    heads, tok = out_ref.shape[0], q_ref.shape[0]
    row = lax.broadcasted_iota(jnp.int32, (META, LANES), 0)
    seg = jnp.broadcast_to(seg_ref[...], (META, LANES))
    for h in range(heads):
        cols = slice(h * HD, (h + 1) * HD)
        for n, ref in enumerate((q_ref, k_ref, v_ref, r_ref)):
            out_ref[h, n * tok : (n + 1) * tok, :] = ref[:, cols]
        gate = jnp.broadcast_to(gate_ref[h : h + 1, :], (META, LANES))
        high = gate.astype(jnp.bfloat16).astype(jnp.float32)
        middle = (gate - high).astype(jnp.bfloat16).astype(jnp.float32)
        low = gate - high - middle
        meta = jnp.where(
            row == 0, seg, jnp.where(row == 1, high, jnp.where(row == 2, middle, jnp.where(row == 3, low, 0.0)))
        )
        out_ref[h, 4 * tok : 4 * tok + META, :] = meta.astype(jnp.bfloat16)


def attend_kernel(x_ref, even_ref, odd_ref, gate_even_ref, gate_odd_ref):
    blocks = x_ref.shape[0]
    tok = LANES // 2
    scale = 1.0 / math.sqrt(HD)
    lane = lax.broadcasted_iota(jnp.int32, (META, LANES), 1)
    row_at = lax.broadcasted_iota(jnp.int32, (LANES, LANES), 0)
    lane_at = lax.broadcasted_iota(jnp.int32, (LANES, LANES), 1)
    causal = lane_at <= row_at

    def part(n, first, last):
        return x_ref[first:last, n * tok : (n + 1) * tok, :].reshape((last - first) * tok, HD)

    seg_rows = []
    for i in range(blocks // 2):
        meta = jnp.where(
            lane < tok,
            x_ref[2 * i, 4 * tok : 4 * tok + META, :].astype(jnp.float32),
            x_ref[2 * i + 1, 4 * tok : 4 * tok + META, :].astype(jnp.float32),
        )
        seg_rows.append(meta[0:1, :])
        seg_col = jnp.transpose(jnp.broadcast_to(meta[0:1, :], (LANES, LANES)))
        gate_row = meta[1:2, :] + (meta[2:3, :] + meta[3:4, :])
        gate_col = jnp.transpose(jnp.broadcast_to(gate_row, (LANES, LANES)))
        masks = []
        for j in range(i + 1):
            same = seg_col == jnp.broadcast_to(seg_rows[j], (LANES, LANES))
            if j == i:
                same = jnp.logical_and(same, causal)
            masks.append(same.astype(jnp.float32))
        visible = jnp.concatenate(masks, axis=1)
        query = part(0, 2 * i, 2 * i + 2)
        keys = part(1, 0, 2 * i + 2)
        values = part(2, 0, 2 * i + 2)
        scores = (
            lax.dot_general(query, keys, (((1,), (1,)), ((), ())), preferred_element_type=jnp.float32) * scale
        )
        weights = (silu(scores) * visible).astype(jnp.bfloat16)
        summed = jnp.dot(weights, values, preferred_element_type=jnp.float32)
        counted = jnp.sum(visible, axis=1, keepdims=True)
        hand = (part(3, 2 * i, 2 * i + 2).astype(jnp.float32) + summed / jnp.sqrt(counted)).astype(jnp.bfloat16)
        here = slice(i * tok, (i + 1) * tok)
        even_ref[here, :] = hand[:tok, :]
        odd_ref[here, :] = hand[tok:, :]
        gate_even_ref[here, :] = gate_col[:tok, :]
        gate_odd_ref[here, :] = gate_col[tok:, :]


def gate_up_kernel(places, heads, idx_ref, gain_ref, wg_ref, wu_ref, *refs):
    pieces, (hidden_ref, hand_ref, lhs_ref) = refs[: len(places)], refs[len(places) :]
    me, plane = idx_ref[0], idx_ref[1]
    rows = pieces[0].shape[1]
    tok = hand_ref.shape[0]
    tile = min(rows, 128)
    mine = pl.multiple_of(lax.div(me, 2) * tok, tok)
    for ref, entries in zip(pieces, places):
        for k, (other, mask) in enumerate(entries):
            if not other:
                at = pl.multiple_of((me ^ mask) * HD, HD)
                hand_ref[:, pl.ds(at, HD)] = ref[k, pl.ds(mine, tok), :]

    def normalise(r, carry):
        here = pl.ds(pl.multiple_of(r * tile, tile), tile)
        squares = jnp.zeros((tile, HD), jnp.float32)
        for ref, entries in zip(pieces, places):
            for k in range(len(entries)):
                v = ref[k, here, :].astype(jnp.float32)
                squares = squares + v * v
        scale = lax.rsqrt(jnp.sum(squares, axis=1, keepdims=True) / D + EPS)
        for ref, entries in zip(pieces, places):
            for k, (other, mask) in enumerate(entries):
                head = me ^ mask
                at = pl.multiple_of(((plane ^ other) * heads + head) * HD, HD)
                gain = gain_ref[other : other + 1, pl.ds(pl.multiple_of(head * HD, HD), HD)]
                v = ref[k, here, :].astype(jnp.float32) * scale * gain
                lhs_ref[here, pl.ds(at, HD)] = v.astype(jnp.bfloat16)
        return carry

    lax.fori_loop(0, rows // tile, normalise, 0)
    width = min(256, wg_ref.shape[1])

    def project(n, carry):
        cols = pl.ds(pl.multiple_of(n * width, width), width)
        gate = jnp.dot(lhs_ref[...], wg_ref[:, cols], preferred_element_type=jnp.float32)
        up = jnp.dot(lhs_ref[...], wu_ref[:, cols], preferred_element_type=jnp.float32)
        hidden_ref[:, cols] = (silu(gate) * up).astype(jnp.bfloat16)
        return carry

    lax.fori_loop(0, wg_ref.shape[1] // width, project, 0)


def down_kernel(idx_ref, own_ref, peer_ref, wd_ref, out_ref):
    plane = idx_ref[1]
    depth = own_ref.shape[1]
    width = min(512, wd_ref.shape[1])
    own_rows = pl.ds(pl.multiple_of(plane * depth, depth), depth)
    peer_rows = pl.ds(pl.multiple_of((1 - plane) * depth, depth), depth)

    def project(n, carry):
        cols = pl.ds(pl.multiple_of(n * width, width), width)
        total = jnp.dot(own_ref[...], wd_ref[own_rows, cols], preferred_element_type=jnp.float32)
        total = total + jnp.dot(peer_ref[...], wd_ref[peer_rows, cols], preferred_element_type=jnp.float32)
        out_ref[:, cols] = total.astype(jnp.bfloat16)
        return carry

    lax.fori_loop(0, wd_ref.shape[1] // width, project, 0)


def weigh_kernel(idx_ref, own_ref, other_ref, gate_ref, send_ref, keep_ref):
    pair = lax.div(idx_ref[0], 2)
    count, tok, width = send_ref.shape
    for k in range(count):
        for flip, out_ref in ((1, send_ref), (0, keep_ref)):
            here = pl.ds(pl.multiple_of((pair ^ (2 * k + flip)) * tok, tok), tok)
            gate = gate_ref[here, :]
            for n in range(width // LANES):
                cols = slice(n * LANES, (n + 1) * LANES)
                both = own_ref[here, cols].astype(jnp.float32) + other_ref[here, cols].astype(jnp.float32)
                out_ref[k, :, cols] = (both * gate).astype(out_ref.dtype)


def add_kernel(keep_ref, got_ref, own_ref, *send_refs):
    own_ref[...] = keep_ref[0] + got_ref[0].astype(jnp.float32)
    for k, ref in enumerate(send_refs, 1):
        ref[...] = (keep_ref[k] + got_ref[k].astype(jnp.float32)).astype(jnp.bfloat16)


def final_kernel(idx_ref, *refs):
    out_ref = refs[-1]
    per = (len(refs) - 1) // 2
    core = lax.rem(idx_ref[0], 2)
    for n in range(2):
        @pl.when(core == n)
        def _(mine=refs[n * per : (n + 1) * per]):
            total = mine[1][...]
            for ref in mine[2:]:
                total = total + ref[...].astype(jnp.float32)
            out_ref[...] = (mine[0][...].astype(jnp.float32) + total).astype(jnp.bfloat16)


def heads_over_ctx(
    resid, query, key, value, norm_gain, routes, route_gates, segment_ids, w_gate, w_up, w_down
):
    ctx = lax.axis_size("ctx")
    heads, tok, width = ctx, resid.shape[0], resid.shape[1]
    levels = ctx // 4
    experts = ctx // 2
    bf16, f32 = jnp.bfloat16, jnp.float32
    rows = ctx // 2 * tok
    me, plane = lax.axis_index("ctx"), lax.axis_index("tp")
    idx = jnp.stack([me, plane]).astype(jnp.int32)

    def over_ctx(x, mask, core=None):
        return lax.ppermute(x, "ctx", [(c, c ^ mask) for c in range(ctx) if core is None or c % 2 == core])

    def over_tp(x):
        return lax.ppermute(x, "tp", [(0, 1), (1, 0)])

    def to_core(x, core):
        return lax.ppermute(x, "ctx", [(c, c ^ 1) for c in range(ctx) if c % 2 != core])

    wg, wu, wd = w_gate[0], w_up[0], w_down[0]
    chosen = routes[:, :, None] == jnp.arange(experts, dtype=jnp.int32)
    gate_rows = jnp.sum(jnp.where(chosen, route_gates[:, :, None], 0.0), axis=1).T
    gate_rows = jnp.tile(jnp.repeat(gate_rows, 2, axis=0), (1, 2))
    seg_row = jnp.tile(segment_ids.astype(f32)[None, :], (1, 2))
    packed = call(
        pack_kernel,
        jax.ShapeDtypeStruct((ctx, 4 * tok + META, HD), bf16),
        (query, key, value, resid, seg_row, gate_rows),
    )
    arrived = lax.all_to_all(packed, "ctx", split_axis=0, concat_axis=0, tiled=True)
    gain = jnp.stack([norm_gain, over_tp(norm_gain)]).astype(f32)
    hand_even, hand_odd, gates_even, gates_odd = call(
        attend_kernel,
        [jax.ShapeDtypeStruct((rows, HD), t) for t in (bf16, bf16, f32, f32)],
        (arrived,),
    )
    masks = [4 * k for k in range(levels)]
    half = levels // 2
    results = []
    for core, (hand, gates) in enumerate(((hand_even, gates_even), (hand_odd, gates_odd))):
        column = jnp.stack([hand] + [over_ctx(hand, m) for m in masks[1:]])
        by_y, by_x = over_ctx(column, 2), over_tp(column)
        diag_x, diag_y = over_tp(by_y[:half]), over_ctx(by_x[half:], 2)
        pieces = [column, by_y, by_x, diag_x, diag_y]
        places = [
            [(0, m) for m in masks],
            [(0, m ^ 2) for m in masks],
            [(1, m) for m in masks],
            [(1, m ^ 2) for m in masks[:half]],
            [(1, m ^ 2) for m in masks[half:]],
        ]
        pieces += [over_ctx(p, 1) for p in pieces]
        places += [[(t, m ^ 1) for t, m in entry] for entry in places]
        hidden, own_hand = call(
            functools.partial(gate_up_kernel, places, heads),
            [
                jax.ShapeDtypeStruct((rows, wg.shape[1]), bf16),
                jax.ShapeDtypeStruct((tok, width), bf16),
            ],
            (idx, gain, wg, wu, *pieces),
            smem=1,
            scratch=[pltpu.VMEM((rows, D), bf16)],
            vmem=32,
            flops=4 * rows * D * wg.shape[1],
            moved=2 * (rows * D + 2 * D * wg.shape[1]),
        )
        half_out = call(
            down_kernel,
            jax.ShapeDtypeStruct((rows, width), bf16),
            (idx, hidden, over_tp(hidden), wd),
            smem=1,
            flops=2 * rows * wd.shape[0] * width,
            moved=2 * (rows * width + wd.shape[0] * width),
        )
        send, keep = call(
            weigh_kernel,
            [jax.ShapeDtypeStruct((levels, tok, width), t) for t in (bf16, f32)],
            (idx, half_out, to_core(half_out, core), gates),
            smem=1,
        )
        own, *sends = call(
            add_kernel,
            [jax.ShapeDtypeStruct((tok, width), t) for t in [f32] + [bf16] * (levels - 1)],
            (keep, over_ctx(send, 2, core)),
        )
        results += [own_hand, own] + [over_ctx(s, m, core) for s, m in zip(sends, masks[1:])]
    return call(final_kernel, jax.ShapeDtypeStruct((tok, width), bf16), (idx, *results), smem=1)


def general(
    resid, query, key, value, norm_gain, routes, route_gates, segment_ids, w_gate, w_up, w_down
):
    tok_count = resid.shape[0]
    feat_width = resid.shape[1]
    head_count = feat_width // HD
    score_scale = 1.0 / math.sqrt(HD)
    query_pos = lax.axis_index("ctx") * tok_count + jnp.arange(tok_count, dtype=jnp.int32)
    key_segments = lax.all_gather(segment_ids, "ctx", axis=0, tiled=True)
    query_heads = query.reshape(tok_count, head_count, HD)
    start_sums = (
        jnp.zeros((tok_count, feat_width), jnp.float32),
        jnp.zeros((tok_count,), jnp.float32),
    )
    key_piece = lax.all_gather(key, "ctx", axis=0, tiled=True)
    value_piece = lax.all_gather(value, "ctx", axis=0, tiled=True)
    piece_len = key_piece.shape[0]
    block_len = math.gcd(piece_len, 512)
    block_count = piece_len // block_len
    key_blocks = key_piece.reshape(block_count, block_len, head_count, HD)
    value_blocks = value_piece.reshape(block_count, block_len, head_count, HD)

    def advance(state, inputs):
        key_block, value_block, block_id = inputs
        key_first = block_id * block_len

        def compute(current):
            acc_sum, key_total = current
            key_pos = key_first + jnp.arange(block_len, dtype=jnp.int32)
            key_segs = lax.dynamic_slice_in_dim(key_segments, key_first, block_len, 0)
            visible = jnp.logical_and(
                key_segs[None, :] == segment_ids[:, None], key_pos[None, :] <= query_pos[:, None]
            ).astype(jnp.float32)
            scores = (
                jnp.einsum(
                    "thd,shd->hts", query_heads, key_block, preferred_element_type=jnp.float32
                )
                * score_scale
            )
            weights = (jax.nn.silu(scores) * visible[None]).astype(jnp.bfloat16)
            summed = jnp.einsum(
                "hts,shd->thd", weights, value_block, preferred_element_type=jnp.float32
            )
            return (
                acc_sum + summed.reshape(tok_count, feat_width),
                key_total + jnp.sum(visible, axis=1),
            )

        last_key_seg = lax.dynamic_slice_in_dim(key_segments, key_first + block_len - 1, 1, 0)[0]
        reached = jnp.logical_and(key_first <= query_pos[-1], last_key_seg >= segment_ids[0])
        state = lax.cond(reached, compute, lambda current: current, state)
        return (state, None)

    block_ids = jnp.arange(block_count, dtype=jnp.int32)
    result, unused = lax.scan(advance, start_sums, (key_blocks, value_blocks, block_ids))
    acc_sum, key_total = result
    attended = acc_sum / jnp.sqrt(key_total)[:, None]
    hand_state = (resid.astype(jnp.float32) + attended).astype(jnp.bfloat16)
    hand_f32 = hand_state.astype(jnp.float32)
    square_sums = lax.psum(jnp.sum(hand_f32 * hand_f32, axis=1), ("tp", "sub"))
    normed = (
        hand_f32 * lax.rsqrt(square_sums / D + EPS)[:, None] * norm_gain.astype(jnp.float32)
    ).astype(jnp.bfloat16)
    ctx_count = lax.axis_size("ctx")
    expert_count = ctx_count // 2
    capacity = min(tok_count, max(2, tok_count * 10 // ctx_count))
    slot_total = expert_count * capacity
    recv_total = ctx_count * capacity
    flat_routes = routes.reshape(-1)
    onehot = (flat_routes[:, None] == jnp.arange(expert_count, dtype=jnp.int32)[None, :]).astype(
        jnp.int32
    )
    slot_rank = jnp.sum((jnp.cumsum(onehot, axis=0) - 1) * onehot, axis=1)
    slot_index = flat_routes * capacity + slot_rank
    position = jnp.arange(tok_count * TOPK, dtype=jnp.int32) // TOPK
    slot_source = jnp.full((slot_total,), tok_count, jnp.int32).at[slot_index].set(position)
    gate_local = w_gate[0]
    up_local = w_up[0]
    down_local = w_down[0]
    gathered = lax.all_gather(normed, ("tp", "sub"), axis=1, tiled=True)
    padded = jnp.concatenate([gathered, jnp.zeros((1, gathered.shape[1]), gathered.dtype)], axis=0)
    filled = padded[slot_source].reshape(expert_count, capacity, gathered.shape[1])
    arrived = lax.all_to_all(
        jnp.repeat(filled, 2, axis=0), "ctx", split_axis=0, concat_axis=0, tiled=True
    ).reshape(recv_total, gathered.shape[1])
    gate_sum = jnp.dot(arrived, gate_local, preferred_element_type=jnp.float32)
    up_sum = jnp.dot(arrived, up_local, preferred_element_type=jnp.float32)
    hidden = (jax.nn.silu(gate_sum) * up_sum).astype(jnp.bfloat16)
    down_rows_out = jnp.dot(
        lax.all_gather(hidden, ("tp", "sub"), axis=1, tiled=True),
        down_local,
        preferred_element_type=jnp.float32,
    ).astype(jnp.bfloat16)
    returned = lax.all_to_all(
        down_rows_out.reshape(ctx_count, capacity, feat_width),
        "ctx",
        split_axis=0,
        concat_axis=0,
        tiled=True,
    )
    combined = jnp.sum(
        returned.reshape(expert_count, 2, capacity, feat_width).astype(jnp.float32), axis=1
    ).reshape(slot_total, feat_width)
    picked = combined[slot_index].reshape(tok_count, TOPK, feat_width)
    mixed = hand_f32 + jnp.sum(route_gates[:, :, None] * picked, axis=1)
    return mixed.astype(jnp.bfloat16)


def fits(mesh, resid):
    ctx, tp = mesh.shape["ctx"], mesh.shape["tp"]
    heads = resid.shape[1] // tp // HD
    tok = resid.shape[0] // mesh.shape["groups"] // ctx
    return tp == 2 and mesh.shape["sub"] == 1 and heads == ctx and 2 * tok == LANES and ctx >= 8 and ctx & (ctx - 1) == 0


def solution(mesh):
    placed = (
        P(("groups", "ctx"), ("tp", "sub")),
        P(("groups", "ctx"), ("tp", "sub")),
        P(("groups", "ctx"), ("tp", "sub")),
        P(("groups", "ctx"), ("tp", "sub")),
        P(("tp", "sub")),
        P(("groups", "ctx"), None),
        P(("groups", "ctx"), None),
        P(("groups", "ctx")),
        P("ctx", None, ("tp", "sub")),
        P("ctx", None, ("tp", "sub")),
        P("ctx", None, ("tp", "sub")),
    )

    def step(resid, *rest):
        per_device = heads_over_ctx if fits(mesh, resid) else general
        return jax.shard_map(
            per_device,
            mesh=mesh,
            in_specs=placed,
            out_specs=P(("groups", "ctx"), ("tp", "sub")),
            check_vma=False,
        )(resid, *rest)

    return step
```

```python
import functools
import math

import jax
import jax.numpy as jnp
from jax import lax
from jax.experimental import pallas as pl
from jax.experimental.pallas import tpu as pltpu
from jax.sharding import PartitionSpec as P

D = 4096
HD = 128
TOPK = 4
EPS = 1e-06
META = 16
LANES = 128
MIB = 1 << 20


def silu(v):
    return v * (0.5 * jnp.tanh(0.5 * v) + 0.5)


def call(kernel, out_shape, args, smem=0, hbm=(), scratch=(), vmem=16, flops=0, moved=0):
    spaces = [pltpu.SMEM if n < smem else pl.ANY if n in hbm else pltpu.VMEM for n in range(len(args))]
    several = isinstance(out_shape, (tuple, list))
    out = pl.BlockSpec(memory_space=pltpu.VMEM)
    return pl.pallas_call(
        kernel,
        out_shape=out_shape,
        in_specs=[pl.BlockSpec(memory_space=space) for space in spaces],
        out_specs=tuple(out for _ in out_shape) if several else out,
        scratch_shapes=list(scratch),
        compiler_params=pltpu.CompilerParams(vmem_limit_bytes=vmem * MIB),
        cost_estimate=pl.CostEstimate(flops=flops, bytes_accessed=moved, transcendentals=0),
    )(*args)


def pack_kernel(seg_ref, route_ref, gate_ref, q_ref, k_ref, v_ref, r_ref, out_ref, held_ref, sems):
    heads, tok = out_ref.shape[0], q_ref.shape[0]
    copies = [pltpu.make_async_copy(ref, held_ref.at[n], sems.at[n]) for n, ref in enumerate((q_ref, k_ref, v_ref, r_ref))]
    for copy in copies:
        copy.start()
    row = lax.broadcasted_iota(jnp.int32, (META, tok), 0)
    seg = jnp.broadcast_to(seg_ref[...].astype(jnp.float32), (META, tok))
    parts = []
    for e in range(heads // 2):
        gate = jnp.sum(jnp.where(route_ref[...] == e, gate_ref[...], 0.0), axis=0, keepdims=True)
        gate = jnp.broadcast_to(gate, (META, tok))
        high = gate.astype(jnp.bfloat16).astype(jnp.float32)
        middle = (gate - high).astype(jnp.bfloat16).astype(jnp.float32)
        parts.append((high, middle, gate - high - middle))
    out_ref[:, 4 * tok :, :] = jnp.zeros((heads, META, HD), jnp.bfloat16)
    for h in range(heads):
        meta = jnp.where(row == 0, seg, 0.0)
        for n, piece in enumerate(parts[h // 2] + parts[h // 2 ^ 1], 1):
            meta = jnp.where(row == n, piece, meta)
        out_ref[h, 4 * tok :, 0:tok] = meta.astype(jnp.bfloat16)
    for n, copy in enumerate(copies):
        copy.wait()
        for h in range(heads):
            out_ref[h, n * tok : (n + 1) * tok, :] = held_ref[n, :, h * HD : (h + 1) * HD]


def attend_kernel(capacity, x_ref, even_ref, odd_ref, pick_even_ref, pick_odd_ref, gate_even_ref, gate_odd_ref):
    blocks = x_ref.shape[0]
    tok = LANES // 2
    levels = blocks // 4
    scale = 1.0 / math.sqrt(HD)
    lane = lax.broadcasted_iota(jnp.int32, (META, LANES), 1)
    row_at = lax.broadcasted_iota(jnp.int32, (LANES, LANES), 0)
    lane_at = lax.broadcasted_iota(jnp.int32, (LANES, LANES), 1)
    causal = lane_at <= row_at
    span = levels * tok
    slots = levels * capacity
    earlier_at = lax.broadcasted_iota(jnp.int32, (span, span), 0)
    later_at = lax.broadcasted_iota(jnp.int32, (span, span), 1)
    earlier = jnp.logical_and(earlier_at < later_at, earlier_at // tok == later_at // tok)
    earlier = earlier.astype(jnp.float32).astype(jnp.bfloat16)
    slot_at = lax.broadcasted_iota(jnp.int32, (slots, span), 0).astype(jnp.float32)
    base = (lax.broadcasted_iota(jnp.int32, (1, span), 1) // tok * capacity).astype(jnp.float32)

    def part(n, first, last):
        return x_ref[first:last, n * tok : (n + 1) * tok, :].reshape((last - first) * tok, HD)

    def scalars(first, second):
        left = x_ref[first, 4 * tok :, :].astype(jnp.float32)
        right = pltpu.roll(x_ref[second, 4 * tok :, :].astype(jnp.float32), tok, 1)
        return jnp.where(lane < tok, left, right)

    def gate_of(meta, which):
        first = 1 + 3 * which
        return meta[first : first + 1, :] + (meta[first + 1 : first + 2, :] + meta[first + 2 : first + 3, :])

    def down_rows(row):
        return jnp.transpose(jnp.broadcast_to(row, (LANES, LANES)))

    for y in range(2):
        for odd, (pick_ref, gate_ref) in enumerate(((pick_even_ref, gate_even_ref), (pick_odd_ref, gate_odd_ref))):
            metas = [scalars(4 * z + 2 * y + odd, 4 * z + 4 + 2 * y + odd) for z in range(0, levels, 2)]
            for which in range(2):
                rows = [gate_of(meta, which) for meta in metas]
                for n, row in enumerate(rows):
                    gate_ref[which, y * span + n * LANES : y * span + (n + 1) * LANES, :] = down_rows(row)
                named = (jnp.concatenate(rows, axis=1) > 0.0).astype(jnp.float32)
                rank = jnp.dot(
                    jnp.broadcast_to(named, (META, span)).astype(jnp.bfloat16),
                    earlier,
                    preferred_element_type=jnp.float32,
                )[0:1, :]
                target = jnp.broadcast_to(jnp.where(named > 0.0, base + rank, -1.0), (slots, span))
                pick = (slot_at == target).astype(jnp.float32).astype(jnp.bfloat16)
                pick_ref[which, y * slots : (y + 1) * slots, :] = pick

    seg_rows = []
    for i in range(blocks // 2):
        seg_rows.append(scalars(2 * i, 2 * i + 1)[0:1, :])
        seg_col = down_rows(seg_rows[i])
        masks = []
        for j in range(i + 1):
            same = seg_col == jnp.broadcast_to(seg_rows[j], (LANES, LANES))
            if j == i:
                same = jnp.logical_and(same, causal)
            masks.append(same.astype(jnp.float32))
        visible = jnp.concatenate(masks, axis=1)
        query = part(0, 2 * i, 2 * i + 2)
        keys = part(1, 0, 2 * i + 2)
        values = part(2, 0, 2 * i + 2)
        scores = (
            lax.dot_general(query, keys, (((1,), (1,)), ((), ())), preferred_element_type=jnp.float32) * scale
        )
        weights = (silu(scores) * visible).astype(jnp.bfloat16)
        summed = jnp.dot(weights, values, preferred_element_type=jnp.float32)
        counted = jnp.sum(visible, axis=1, keepdims=True)
        hand = (part(3, 2 * i, 2 * i + 2).astype(jnp.float32) + summed / jnp.sqrt(counted)).astype(jnp.bfloat16)
        at = (i % 2 * levels + i // 2) * tok
        even_ref[at : at + tok, :] = hand[:tok, :]
        odd_ref[at : at + tok, :] = hand[tok:, :]


def compact_kernel(idx_ref, pick_ref, *refs):
    pieces, (mine_ref, theirs_ref) = refs[:-2], refs[-2:]
    me = idx_ref[0]
    levels = len(pieces)
    slots, span = pick_ref.shape[1] // 2, pick_ref.shape[2]
    tok = span // levels
    z, y = lax.div(me, 4), lax.rem(lax.div(me, 2), 2)
    for group in range(2):
        block = jnp.concatenate([p[group * span : (group + 1) * span, :] for p in pieces], axis=1)
        for which, out_ref in enumerate((mine_ref, theirs_ref)):
            here = slice(group * slots, (group + 1) * slots)
            rows = jnp.dot(pick_ref[which, here, :], block, preferred_element_type=jnp.float32).astype(jnp.bfloat16)
            for k in range(levels):
                out_ref[k, here, :] = rows[:, k * HD : (k + 1) * HD]
    for which, out_ref in enumerate((mine_ref, theirs_ref)):
        own = pl.ds(pl.multiple_of(((y ^ which) * levels + z) * tok, tok), tok)
        for k in range(levels):
            out_ref[k, 2 * slots :, :] = pieces[k][own, :]


def gate_up_kernel(places, heads, idx_ref, wg_ref, wu_ref, gain_ref, *refs):
    pieces, (hidden_ref, hand_ref, lhs_ref, wg_held, wu_held, sems) = refs[: len(places)], refs[len(places) :]
    me, plane = idx_ref[0], idx_ref[1]
    rows, tok = hidden_ref.shape[0], hand_ref.shape[0]
    width = min(256, wg_ref.shape[1])
    steps = wg_ref.shape[1] // width
    copies = []
    for n in range(steps):
        cols = slice(n * width, (n + 1) * width)
        for m, (ref, held) in enumerate(((wg_ref, wg_held), (wu_ref, wu_held))):
            copies.append(pltpu.make_async_copy(ref.at[:, cols], held.at[:, cols], sems.at[2 * n + m]))
            copies[-1].start()
    tile = rows // 2
    for ref, entries in zip(pieces, places):
        for k, (other, mask) in enumerate(entries):
            if not other:
                at = pl.multiple_of((me ^ mask) * HD, HD)
                hand_ref[:, pl.ds(at, HD)] = ref[k, rows : rows + tok, :]

    def normalise(r, carry):
        here = pl.ds(pl.multiple_of(r * tile, tile), tile)
        squares = jnp.zeros((tile, HD), jnp.float32)
        for ref, entries in zip(pieces, places):
            for k in range(len(entries)):
                v = ref[k, here, :].astype(jnp.float32)
                squares = squares + v * v
        scale = lax.rsqrt(jnp.sum(squares, axis=1, keepdims=True) / D + EPS)
        for ref, entries in zip(pieces, places):
            for k, (other, mask) in enumerate(entries):
                head = me ^ mask
                at = pl.multiple_of(((plane ^ other) * heads + head) * HD, HD)
                gain = gain_ref[other : other + 1, pl.ds(pl.multiple_of(head * HD, HD), HD)]
                v = ref[k, here, :].astype(jnp.float32) * scale * gain
                lhs_ref[here, pl.ds(at, HD)] = v.astype(jnp.bfloat16)
        return carry

    lax.fori_loop(0, rows // tile, normalise, 0)
    for n in range(steps):
        cols = slice(n * width, (n + 1) * width)
        copies[2 * n].wait()
        gate = jnp.dot(lhs_ref[...], wg_held[:, cols], preferred_element_type=jnp.float32)
        copies[2 * n + 1].wait()
        up = jnp.dot(lhs_ref[...], wu_held[:, cols], preferred_element_type=jnp.float32)
        hidden_ref[:, cols] = (silu(gate) * up).astype(jnp.bfloat16)


def down_kernel(idx_ref, wd_ref, own_ref, peer_ref, out_ref, wd_held, sems):
    plane = idx_ref[1]
    depth = own_ref.shape[1]
    width = min(512, wd_ref.shape[1])
    steps = wd_ref.shape[1] // width
    copies = []
    for n in range(steps):
        cols = slice(n * width, (n + 1) * width)
        copies.append(pltpu.make_async_copy(wd_ref.at[:, cols], wd_held.at[:, cols], sems.at[n]))
        copies[-1].start()
    own_rows = pl.ds(pl.multiple_of(plane * depth, depth), depth)
    peer_rows = pl.ds(pl.multiple_of((1 - plane) * depth, depth), depth)
    for n in range(steps):
        cols = slice(n * width, (n + 1) * width)
        copies[n].wait()
        total = jnp.dot(own_ref[...], wd_held[own_rows, cols], preferred_element_type=jnp.float32)
        total = total + jnp.dot(peer_ref[...], wd_held[peer_rows, cols], preferred_element_type=jnp.float32)
        out_ref[:, cols] = total.astype(jnp.bfloat16)


def pair_kernel(idx_ref, own_ref, other_ref, send_ref):
    slots = send_ref.shape[0]
    y = lax.rem(lax.div(idx_ref[0], 2), 2)
    theirs = pl.ds(pl.multiple_of((1 - y) * slots, slots), slots)
    both = own_ref[theirs, :].astype(jnp.float32) + other_ref[theirs, :].astype(jnp.float32)
    send_ref[...] = both.astype(jnp.bfloat16)


def spread(pick, rows):
    return lax.dot_general(pick, rows, (((0,), (0,)), ((), ())), preferred_element_type=jnp.float32)


def weigh_kernel(idx_ref, pick_ref, gate_ref, own_ref, other_ref, keep_ref):
    slots, span = pick_ref.shape[1] // 2, pick_ref.shape[2]
    y = lax.rem(lax.div(idx_ref[0], 2), 2)
    mine = pl.ds(pl.multiple_of(y * slots, slots), slots)
    gate = gate_ref[0, pl.ds(pl.multiple_of(y * span, span), span), :]
    pick = pick_ref[0, mine, :]
    width = 4 * LANES
    for n in range(own_ref.shape[1] // width):
        cols = slice(n * width, (n + 1) * width)
        total = spread(pick, own_ref[mine, cols]) + spread(pick, other_ref[mine, cols])
        keep_ref[:, cols] = total * jnp.concatenate([gate] * (width // LANES), axis=1)


def add_kernel(idx_ref, pick_ref, gate_ref, keep_ref, got_ref, own_ref, *refs):
    send_refs, total_ref = refs[:-1], refs[-1]
    slots, span = pick_ref.shape[1] // 2, pick_ref.shape[2]
    tok = own_ref.shape[0]
    z, y = lax.div(idx_ref[0], 4), lax.rem(lax.div(idx_ref[0], 2), 2)
    gate = gate_ref[1, pl.ds(pl.multiple_of(y * span, span), span), :]
    pick = pick_ref[1, pl.ds(pl.multiple_of(y * slots, slots), slots), :]
    width = 4 * LANES
    for n in range(got_ref.shape[1] // width):
        cols = slice(n * width, (n + 1) * width)
        more = spread(pick, got_ref[:, cols]) * jnp.concatenate([gate] * (width // LANES), axis=1)
        total_ref[:, cols] = keep_ref[:, cols] + more
    own_ref[...] = total_ref[pl.ds(pl.multiple_of(z * tok, tok), tok), :]
    for k, ref in enumerate(send_refs, 1):
        ref[...] = total_ref[pl.ds(pl.multiple_of((z ^ k) * tok, tok), tok), :].astype(jnp.bfloat16)


def final_kernel(idx_ref, *refs):
    out_ref = refs[-1]
    per = (len(refs) - 1) // 2
    core = lax.rem(idx_ref[0], 2)
    for n in range(2):
        @pl.when(core == n)
        def _(mine=refs[n * per : (n + 1) * per]):
            total = mine[1][...]
            for ref in mine[2:]:
                total = total + ref[...].astype(jnp.float32)
            out_ref[...] = (mine[0][...].astype(jnp.float32) + total).astype(jnp.bfloat16)


def heads_over_ctx(
    resid, query, key, value, norm_gain, routes, route_gates, segment_ids, w_gate, w_up, w_down
):
    ctx = lax.axis_size("ctx")
    heads, tok, width = ctx, resid.shape[0], resid.shape[1]
    levels = ctx // 4
    bf16, f32 = jnp.bfloat16, jnp.float32
    rows = ctx // 2 * tok
    span, slots = levels * tok, levels * block_slots(ctx, tok)
    me, plane = lax.axis_index("ctx"), lax.axis_index("tp")
    idx = jnp.stack([me, plane]).astype(jnp.int32)

    def shape(*dims, dtype=bf16):
        return jax.ShapeDtypeStruct(dims, dtype)

    def over_ctx(x, mask, core=None):
        return lax.ppermute(x, "ctx", [(c, c ^ mask) for c in range(ctx) if core is None or c % 2 == core])

    def over_tp(x):
        return lax.ppermute(x, "tp", [(0, 1), (1, 0)])

    def to_core(x, core):
        return lax.ppermute(x, "ctx", [(c, c ^ 1) for c in range(ctx) if c % 2 != core])

    wg, wu, wd = w_gate[0], w_up[0], w_down[0]
    hidden_width = wg.shape[1]
    packed = call(
        pack_kernel,
        shape(ctx, 4 * tok + META, HD),
        (segment_ids[None, :], routes.T, route_gates.T, query, key, value, resid),
        hbm=(3, 4, 5, 6),
        scratch=[pltpu.VMEM((4, tok, width), bf16), pltpu.SemaphoreType.DMA((4,))],
    )
    gain = over_tp(norm_gain)
    arrived = lax.all_to_all(packed, "ctx", split_axis=0, concat_axis=0, tiled=True)
    arrived, gain = lax.optimization_barrier((arrived, gain))
    gain = jnp.stack([norm_gain, gain]).astype(f32)
    hands = call(
        functools.partial(attend_kernel, block_slots(ctx, tok)),
        [shape(rows, HD)] * 2 + [shape(2, 2 * slots, span)] * 2 + [shape(2, 2 * span, LANES, dtype=f32)] * 2,
        (arrived,),
    )
    masks = [4 * k for k in range(levels)]
    results = []
    for core in range(2):
        hand, pick, gates = hands[core::2]
        column = [hand] + [over_ctx(hand, m) for m in masks[1:]]
        mine, theirs = call(compact_kernel, [shape(levels, 2 * slots + tok, HD)] * 2, (idx, pick, *column), smem=1)
        by_y = over_ctx(theirs, 2)
        pieces = [mine, by_y, over_tp(mine[:, : 2 * slots]), over_tp(by_y[:, : 2 * slots])]
        places = [[(t, m ^ f) for m in masks] for t, f in ((0, 0), (0, 2), (1, 0), (1, 2))]
        pieces += [over_ctx(p, 1) for p in pieces]
        places += [[(t, m ^ 1) for t, m in entry] for entry in places]
        hidden, own_hand = call(
            functools.partial(gate_up_kernel, places, heads),
            [shape(2 * slots, hidden_width), shape(tok, width)],
            (idx, wg, wu, gain, *pieces),
            smem=1,
            hbm=(1, 2),
            scratch=[pltpu.VMEM((2 * slots, D), bf16), pltpu.VMEM(wg.shape, bf16), pltpu.VMEM(wu.shape, bf16)]
            + [pltpu.SemaphoreType.DMA((2 * (hidden_width // min(256, hidden_width)),))],
            vmem=32,
            flops=8 * slots * D * hidden_width,
            moved=2 * (2 * slots * D + 2 * D * hidden_width),
        )
        half_out = call(
            down_kernel,
            shape(2 * slots, width),
            (idx, wd, hidden, over_tp(hidden)),
            smem=1,
            hbm=(1,),
            scratch=[pltpu.VMEM(wd.shape, bf16), pltpu.SemaphoreType.DMA((width // min(512, width),))],
            flops=4 * slots * wd.shape[0] * width,
            moved=2 * (2 * slots * width + wd.shape[0] * width),
        )
        other = to_core(half_out, core)
        got = over_ctx(call(pair_kernel, shape(slots, width), (idx, half_out, other), smem=1), 2, core)
        keep = call(weigh_kernel, shape(span, width, dtype=f32), (idx, pick, gates, half_out, other), smem=1)
        own, *sends = call(
            add_kernel,
            [shape(tok, width, dtype=f32)] + [shape(tok, width)] * (levels - 1),
            (idx, pick, gates, keep, got),
            smem=1,
            scratch=[pltpu.VMEM((span, width), f32)],
        )
        results += [own_hand, own] + [over_ctx(s, m, core) for s, m in zip(sends, masks[1:])]
    return call(final_kernel, shape(tok, width), (idx, *results), smem=1)


def general(
    resid, query, key, value, norm_gain, routes, route_gates, segment_ids, w_gate, w_up, w_down
):
    tok_count = resid.shape[0]
    feat_width = resid.shape[1]
    head_count = feat_width // HD
    score_scale = 1.0 / math.sqrt(HD)
    query_pos = lax.axis_index("ctx") * tok_count + jnp.arange(tok_count, dtype=jnp.int32)
    key_segments = lax.all_gather(segment_ids, "ctx", axis=0, tiled=True)
    query_heads = query.reshape(tok_count, head_count, HD)
    start_sums = (
        jnp.zeros((tok_count, feat_width), jnp.float32),
        jnp.zeros((tok_count,), jnp.float32),
    )
    key_piece = lax.all_gather(key, "ctx", axis=0, tiled=True)
    value_piece = lax.all_gather(value, "ctx", axis=0, tiled=True)
    piece_len = key_piece.shape[0]
    block_len = math.gcd(piece_len, 512)
    block_count = piece_len // block_len
    key_blocks = key_piece.reshape(block_count, block_len, head_count, HD)
    value_blocks = value_piece.reshape(block_count, block_len, head_count, HD)

    def advance(state, inputs):
        key_block, value_block, block_id = inputs
        key_first = block_id * block_len

        def compute(current):
            acc_sum, key_total = current
            key_pos = key_first + jnp.arange(block_len, dtype=jnp.int32)
            key_segs = lax.dynamic_slice_in_dim(key_segments, key_first, block_len, 0)
            visible = jnp.logical_and(
                key_segs[None, :] == segment_ids[:, None], key_pos[None, :] <= query_pos[:, None]
            ).astype(jnp.float32)
            scores = (
                jnp.einsum(
                    "thd,shd->hts", query_heads, key_block, preferred_element_type=jnp.float32
                )
                * score_scale
            )
            weights = (jax.nn.silu(scores) * visible[None]).astype(jnp.bfloat16)
            summed = jnp.einsum(
                "hts,shd->thd", weights, value_block, preferred_element_type=jnp.float32
            )
            return (
                acc_sum + summed.reshape(tok_count, feat_width),
                key_total + jnp.sum(visible, axis=1),
            )

        last_key_seg = lax.dynamic_slice_in_dim(key_segments, key_first + block_len - 1, 1, 0)[0]
        reached = jnp.logical_and(key_first <= query_pos[-1], last_key_seg >= segment_ids[0])
        state = lax.cond(reached, compute, lambda current: current, state)
        return (state, None)

    block_ids = jnp.arange(block_count, dtype=jnp.int32)
    result, unused = lax.scan(advance, start_sums, (key_blocks, value_blocks, block_ids))
    acc_sum, key_total = result
    attended = acc_sum / jnp.sqrt(key_total)[:, None]
    hand_state = (resid.astype(jnp.float32) + attended).astype(jnp.bfloat16)
    hand_f32 = hand_state.astype(jnp.float32)
    square_sums = lax.psum(jnp.sum(hand_f32 * hand_f32, axis=1), ("tp", "sub"))
    normed = (
        hand_f32 * lax.rsqrt(square_sums / D + EPS)[:, None] * norm_gain.astype(jnp.float32)
    ).astype(jnp.bfloat16)
    ctx_count = lax.axis_size("ctx")
    expert_count = ctx_count // 2
    capacity = block_slots(ctx_count, tok_count)
    slot_total = expert_count * capacity
    recv_total = ctx_count * capacity
    flat_routes = routes.reshape(-1)
    onehot = (flat_routes[:, None] == jnp.arange(expert_count, dtype=jnp.int32)[None, :]).astype(
        jnp.int32
    )
    slot_rank = jnp.sum((jnp.cumsum(onehot, axis=0) - 1) * onehot, axis=1)
    slot_index = flat_routes * capacity + slot_rank
    position = jnp.arange(tok_count * TOPK, dtype=jnp.int32) // TOPK
    slot_source = jnp.full((slot_total,), tok_count, jnp.int32).at[slot_index].set(position)
    gate_local = w_gate[0]
    up_local = w_up[0]
    down_local = w_down[0]
    gathered = lax.all_gather(normed, ("tp", "sub"), axis=1, tiled=True)
    padded = jnp.concatenate([gathered, jnp.zeros((1, gathered.shape[1]), gathered.dtype)], axis=0)
    filled = padded[slot_source].reshape(expert_count, capacity, gathered.shape[1])
    arrived = lax.all_to_all(
        jnp.repeat(filled, 2, axis=0), "ctx", split_axis=0, concat_axis=0, tiled=True
    ).reshape(recv_total, gathered.shape[1])
    gate_sum = jnp.dot(arrived, gate_local, preferred_element_type=jnp.float32)
    up_sum = jnp.dot(arrived, up_local, preferred_element_type=jnp.float32)
    hidden = (jax.nn.silu(gate_sum) * up_sum).astype(jnp.bfloat16)
    down_rows_out = jnp.dot(
        lax.all_gather(hidden, ("tp", "sub"), axis=1, tiled=True),
        down_local,
        preferred_element_type=jnp.float32,
    ).astype(jnp.bfloat16)
    returned = lax.all_to_all(
        down_rows_out.reshape(ctx_count, capacity, feat_width),
        "ctx",
        split_axis=0,
        concat_axis=0,
        tiled=True,
    )
    combined = jnp.sum(
        returned.reshape(expert_count, 2, capacity, feat_width).astype(jnp.float32), axis=1
    ).reshape(slot_total, feat_width)
    picked = combined[slot_index].reshape(tok_count, TOPK, feat_width)
    mixed = hand_f32 + jnp.sum(route_gates[:, :, None] * picked, axis=1)
    return mixed.astype(jnp.bfloat16)


def block_slots(ctx, tok):
    return min(tok, max(2, tok * 10 // ctx))


def fits(mesh, resid):
    ctx, tp = mesh.shape["ctx"], mesh.shape["tp"]
    heads = resid.shape[1] // tp // HD
    tok = resid.shape[0] // mesh.shape["groups"] // ctx
    slots = ctx // 4 * block_slots(ctx, tok)
    whole = heads == ctx and 2 * tok == LANES and slots % 16 == 0
    return tp == 2 and mesh.shape["sub"] == 1 and whole and ctx >= 8 and ctx & (ctx - 1) == 0


def solution(mesh):
    placed = (
        P(("groups", "ctx"), ("tp", "sub")),
        P(("groups", "ctx"), ("tp", "sub")),
        P(("groups", "ctx"), ("tp", "sub")),
        P(("groups", "ctx"), ("tp", "sub")),
        P(("tp", "sub")),
        P(("groups", "ctx"), None),
        P(("groups", "ctx"), None),
        P(("groups", "ctx")),
        P("ctx", None, ("tp", "sub")),
        P("ctx", None, ("tp", "sub")),
        P("ctx", None, ("tp", "sub")),
    )

    def step(resid, *rest):
        per_device = heads_over_ctx if fits(mesh, resid) else general
        return jax.shard_map(
            per_device,
            mesh=mesh,
            in_specs=placed,
            out_specs=P(("groups", "ctx"), ("tp", "sub")),
            check_vma=False,
        )(resid, *rest)

    return step
```

```python
import functools
import math

import jax
import jax.numpy as jnp
from jax import lax
from jax.experimental import pallas as pl
from jax.experimental.pallas import tpu as pltpu
from jax.sharding import PartitionSpec as P

D = 4096
HD = 128
TOPK = 4
EPS = 1e-06
META = 16
LANES = 128
MIB = 1 << 20


def silu(v):
    return v * (0.5 * jnp.tanh(0.5 * v) + 0.5)


def call(kernel, out_shape, args, smem=0, hbm=(), scratch=(), vmem=16, flops=0, moved=0):
    spaces = [pltpu.SMEM if n < smem else pltpu.HBM if n in hbm else pltpu.VMEM for n in range(len(args))]
    several = isinstance(out_shape, (tuple, list))
    out = pl.BlockSpec(memory_space=pltpu.VMEM)
    return pl.pallas_call(
        kernel,
        out_shape=out_shape,
        in_specs=[pl.BlockSpec(memory_space=space) for space in spaces],
        out_specs=tuple(out for _ in out_shape) if several else out,
        scratch_shapes=list(scratch),
        compiler_params=pltpu.CompilerParams(vmem_limit_bytes=vmem * MIB),
    )(*args)


def pack_kernel(seg_ref, route_ref, gate_ref, q_ref, k_ref, v_ref, r_ref, out_ref, held_ref, sems):
    heads, tok = out_ref.shape[0], q_ref.shape[0]
    copies = [pltpu.make_async_copy(ref, held_ref.at[n], sems.at[n]) for n, ref in enumerate((q_ref, k_ref, v_ref, r_ref))]
    for copy in copies:
        copy.start()
    row = lax.broadcasted_iota(jnp.int32, (META, tok), 0)
    seg = jnp.broadcast_to(seg_ref[...].astype(jnp.float32), (META, tok))
    parts = []
    for e in range(heads // 2):
        gate = jnp.sum(jnp.where(route_ref[...] == e, gate_ref[...], 0.0), axis=0, keepdims=True)
        gate = jnp.broadcast_to(gate, (META, tok))
        high = gate.astype(jnp.bfloat16).astype(jnp.float32)
        middle = (gate - high).astype(jnp.bfloat16).astype(jnp.float32)
        parts.append((high, middle, gate - high - middle))
    out_ref[:, 4 * tok :, :] = jnp.zeros((heads, META, HD), jnp.bfloat16)
    for h in range(heads):
        meta = jnp.where(row == 0, seg, 0.0)
        for n, piece in enumerate(parts[h // 2] + parts[h // 2 ^ 1], 1):
            meta = jnp.where(row == n, piece, meta)
        out_ref[h, 4 * tok :, 0:tok] = meta.astype(jnp.bfloat16)
    for n, copy in enumerate(copies):
        copy.wait()
        for h in range(heads):
            out_ref[h, n * tok : (n + 1) * tok, :] = held_ref[n, :, h * HD : (h + 1) * HD]


def attend_kernel(capacity, x_ref, even_ref, odd_ref, pick_even_ref, pick_odd_ref, gate_even_ref, gate_odd_ref):
    blocks = x_ref.shape[0]
    tok = LANES // 2
    levels = blocks // 4
    scale = 1.0 / math.sqrt(HD)
    lane = lax.broadcasted_iota(jnp.int32, (META, LANES), 1)
    row_at = lax.broadcasted_iota(jnp.int32, (LANES, LANES), 0)
    lane_at = lax.broadcasted_iota(jnp.int32, (LANES, LANES), 1)
    causal = lane_at <= row_at
    span = levels * tok
    slots = levels * capacity
    earlier_at = lax.broadcasted_iota(jnp.int32, (span, span), 0)
    later_at = lax.broadcasted_iota(jnp.int32, (span, span), 1)
    earlier = jnp.logical_and(earlier_at < later_at, earlier_at // tok == later_at // tok)
    earlier = earlier.astype(jnp.float32).astype(jnp.bfloat16)
    slot_at = lax.broadcasted_iota(jnp.int32, (slots, span), 0).astype(jnp.float32)
    base = (lax.broadcasted_iota(jnp.int32, (1, span), 1) // tok * capacity).astype(jnp.float32)

    def part(n, first, last):
        return x_ref[first:last, n * tok : (n + 1) * tok, :].reshape((last - first) * tok, HD)

    def scalars(first, second):
        left = x_ref[first, 4 * tok :, :].astype(jnp.float32)
        right = pltpu.roll(x_ref[second, 4 * tok :, :].astype(jnp.float32), tok, 1)
        return jnp.where(lane < tok, left, right)

    def gate_of(meta, which):
        first = 1 + 3 * which
        return meta[first : first + 1, :] + (meta[first + 1 : first + 2, :] + meta[first + 2 : first + 3, :])

    def down_rows(row):
        return jnp.transpose(jnp.broadcast_to(row, (LANES, LANES)))

    for y in range(2):
        for odd, (pick_ref, gate_ref) in enumerate(((pick_even_ref, gate_even_ref), (pick_odd_ref, gate_odd_ref))):
            metas = [scalars(4 * z + 2 * y + odd, 4 * z + 4 + 2 * y + odd) for z in range(0, levels, 2)]
            for which in range(2):
                rows = [gate_of(meta, which) for meta in metas]
                for n, row in enumerate(rows):
                    gate_ref[which, y * span + n * LANES : y * span + (n + 1) * LANES, :] = down_rows(row)
                named = (jnp.concatenate(rows, axis=1) > 0.0).astype(jnp.float32)
                rank = jnp.dot(
                    jnp.broadcast_to(named, (META, span)).astype(jnp.bfloat16),
                    earlier,
                    preferred_element_type=jnp.float32,
                )[0:1, :]
                target = jnp.broadcast_to(jnp.where(named > 0.0, base + rank, -1.0), (slots, span))
                pick = (slot_at == target).astype(jnp.float32).astype(jnp.bfloat16)
                pick_ref[which, y * slots : (y + 1) * slots, :] = pick

    seg_rows = []
    for i in range(blocks // 2):
        seg_rows.append(scalars(2 * i, 2 * i + 1)[0:1, :])
        seg_col = down_rows(seg_rows[i])
        masks = []
        for j in range(i + 1):
            same = seg_col == jnp.broadcast_to(seg_rows[j], (LANES, LANES))
            if j == i:
                same = jnp.logical_and(same, causal)
            masks.append(same.astype(jnp.float32))
        visible = jnp.concatenate(masks, axis=1)
        query = part(0, 2 * i, 2 * i + 2)
        keys = part(1, 0, 2 * i + 2)
        values = part(2, 0, 2 * i + 2)
        scores = (
            lax.dot_general(query, keys, (((1,), (1,)), ((), ())), preferred_element_type=jnp.float32) * scale
        )
        weights = (silu(scores) * visible).astype(jnp.bfloat16)
        summed = jnp.dot(weights, values, preferred_element_type=jnp.float32)
        counted = jnp.sum(visible, axis=1, keepdims=True)
        hand = (part(3, 2 * i, 2 * i + 2).astype(jnp.float32) + summed / jnp.sqrt(counted)).astype(jnp.bfloat16)
        at = (i % 2 * levels + i // 2) * tok
        even_ref[at : at + tok, :] = hand[:tok, :]
        odd_ref[at : at + tok, :] = hand[tok:, :]


def compact_kernel(idx_ref, pick_ref, *refs):
    pieces, (mine_ref, theirs_ref) = refs[:-2], refs[-2:]
    me = idx_ref[0]
    levels = len(pieces)
    slots, span = pick_ref.shape[1] // 2, pick_ref.shape[2]
    tok = span // levels
    z, y = lax.div(me, 4), lax.rem(lax.div(me, 2), 2)
    for group in range(2):
        block = jnp.concatenate([p[group * span : (group + 1) * span, :] for p in pieces], axis=1)
        for which, out_ref in enumerate((mine_ref, theirs_ref)):
            here = slice(group * slots, (group + 1) * slots)
            rows = jnp.dot(pick_ref[which, here, :], block, preferred_element_type=jnp.float32).astype(jnp.bfloat16)
            for k in range(levels):
                out_ref[k, here, :] = rows[:, k * HD : (k + 1) * HD]
    for which, out_ref in enumerate((mine_ref, theirs_ref)):
        own = pl.ds(pl.multiple_of(((y ^ which) * levels + z) * tok, tok), tok)
        for k in range(levels):
            out_ref[k, 2 * slots :, :] = pieces[k][own, :]


def gate_up_kernel(places, heads, idx_ref, wg_ref, wu_ref, gain_ref, *refs):
    pieces, (hidden_ref, hand_ref, lhs_ref) = refs[: len(places)], refs[len(places) :]
    me, plane = idx_ref[0], idx_ref[1]
    rows, tok = hidden_ref.shape[0], hand_ref.shape[0]
    width = min(256, wg_ref.shape[1])
    tile = rows // 2
    for ref, entries in zip(pieces, places):
        for k, (other, mask) in enumerate(entries):
            if not other:
                at = pl.multiple_of((me ^ mask) * HD, HD)
                hand_ref[:, pl.ds(at, HD)] = ref[k, rows : rows + tok, :]

    def normalise(r, carry):
        here = pl.ds(pl.multiple_of(r * tile, tile), tile)
        squares = jnp.zeros((tile, HD), jnp.float32)
        for ref, entries in zip(pieces, places):
            for k in range(len(entries)):
                v = ref[k, here, :].astype(jnp.float32)
                squares = squares + v * v
        scale = lax.rsqrt(jnp.sum(squares, axis=1, keepdims=True) / D + EPS)
        for ref, entries in zip(pieces, places):
            for k, (other, mask) in enumerate(entries):
                head = me ^ mask
                at = pl.multiple_of(((plane ^ other) * heads + head) * HD, HD)
                gain = gain_ref[other : other + 1, pl.ds(pl.multiple_of(head * HD, HD), HD)]
                v = ref[k, here, :].astype(jnp.float32) * scale * gain
                lhs_ref[here, pl.ds(at, HD)] = v.astype(jnp.bfloat16)
        return carry

    lax.fori_loop(0, rows // tile, normalise, 0)
    for n in range(wg_ref.shape[1] // width):
        cols = slice(n * width, (n + 1) * width)
        gate = jnp.dot(lhs_ref[...], wg_ref[:, cols], preferred_element_type=jnp.float32)
        up = jnp.dot(lhs_ref[...], wu_ref[:, cols], preferred_element_type=jnp.float32)
        hidden_ref[:, cols] = (silu(gate) * up).astype(jnp.bfloat16)


def down_kernel(flip, idx_ref, wd_ref, own_ref, peer_ref, out_ref):
    core, plane = lax.rem(idx_ref[0], 2), idx_ref[1]
    depth, total_width = own_ref.shape[1], out_ref.shape[1]
    width = min(512, total_width)
    first = (core ^ flip) * total_width
    own_rows = pl.ds(pl.multiple_of(plane * depth, depth), depth)
    peer_rows = pl.ds(pl.multiple_of((1 - plane) * depth, depth), depth)
    for n in range(total_width // width):
        cols = pl.ds(pl.multiple_of(first + n * width, width), width)
        total = jnp.dot(own_ref[...], wd_ref[own_rows, cols], preferred_element_type=jnp.float32)
        total = total + jnp.dot(peer_ref[...], wd_ref[peer_rows, cols], preferred_element_type=jnp.float32)
        out_ref[:, n * width : (n + 1) * width] = total.astype(jnp.bfloat16)


def pair_kernel(idx_ref, own_ref, other_ref, send_ref):
    slots = send_ref.shape[0]
    y = lax.rem(lax.div(idx_ref[0], 2), 2)
    theirs = pl.ds(pl.multiple_of((1 - y) * slots, slots), slots)
    both = own_ref[theirs, :].astype(jnp.float32) + other_ref[theirs, :].astype(jnp.float32)
    send_ref[...] = both.astype(jnp.bfloat16)


def spread(pick, rows):
    return lax.dot_general(pick, rows, (((0,), (0,)), ((), ())), preferred_element_type=jnp.float32)


def weigh_kernel(idx_ref, pick_ref, gate_ref, own_ref, other_ref, keep_ref):
    slots, span = pick_ref.shape[1] // 2, pick_ref.shape[2]
    y = lax.rem(lax.div(idx_ref[0], 2), 2)
    mine = pl.ds(pl.multiple_of(y * slots, slots), slots)
    gate = gate_ref[0, pl.ds(pl.multiple_of(y * span, span), span), :]
    pick = pick_ref[0, mine, :]
    width = 4 * LANES
    for n in range(own_ref.shape[1] // width):
        cols = slice(n * width, (n + 1) * width)
        total = spread(pick, own_ref[mine, cols]) + spread(pick, other_ref[mine, cols])
        keep_ref[:, cols] = total * jnp.concatenate([gate] * (width // LANES), axis=1)


def add_kernel(idx_ref, pick_ref, gate_ref, keep_ref, got_ref, own_ref, *refs):
    send_refs, total_ref = refs[:-1], refs[-1]
    slots, span = pick_ref.shape[1] // 2, pick_ref.shape[2]
    tok = own_ref.shape[0]
    z, y = lax.div(idx_ref[0], 4), lax.rem(lax.div(idx_ref[0], 2), 2)
    gate = gate_ref[1, pl.ds(pl.multiple_of(y * span, span), span), :]
    pick = pick_ref[1, pl.ds(pl.multiple_of(y * slots, slots), slots), :]
    width = 4 * LANES
    for n in range(got_ref.shape[1] // width):
        cols = slice(n * width, (n + 1) * width)
        more = spread(pick, got_ref[:, cols]) * jnp.concatenate([gate] * (width // LANES), axis=1)
        total_ref[:, cols] = keep_ref[:, cols] + more
    own_ref[...] = total_ref[pl.ds(pl.multiple_of(z * tok, tok), tok), :]
    for k, ref in enumerate(send_refs, 1):
        ref[...] = total_ref[pl.ds(pl.multiple_of((z ^ k) * tok, tok), tok), :].astype(jnp.bfloat16)


def sum_kernel(own_ref, *refs):
    total = own_ref[...]
    for ref in refs[:-1]:
        total = total + ref[...].astype(jnp.float32)
    refs[-1][...] = total.astype(refs[-1].dtype)


def final_kernel(idx_ref, *refs):
    out_ref = refs[-1]
    core = lax.rem(idx_ref[0], 2)
    for n in range(2):
        hand_ref, own_ref, other_ref = refs[3 * n : 3 * n + 3]
        half = own_ref.shape[1]

        @pl.when(core == n)
        def _(hand_ref=hand_ref, halves=(own_ref, other_ref) if n == 0 else (other_ref, own_ref)):
            for m, ref in enumerate(halves):
                cols = slice(m * half, (m + 1) * half)
                out_ref[:, cols] = (hand_ref[:, cols].astype(jnp.float32) + ref[...].astype(jnp.float32)).astype(
                    jnp.bfloat16
                )


def heads_over_ctx(
    resid, query, key, value, norm_gain, routes, route_gates, segment_ids, w_gate, w_up, w_down
):
    ctx = lax.axis_size("ctx")
    heads, tok, width = ctx, resid.shape[0], resid.shape[1]
    levels = ctx // 4
    bf16, f32 = jnp.bfloat16, jnp.float32
    rows = ctx // 2 * tok
    span, slots = levels * tok, levels * block_slots(ctx, tok)
    me, plane = lax.axis_index("ctx"), lax.axis_index("tp")
    idx = jnp.stack([me, plane]).astype(jnp.int32)

    def shape(*dims, dtype=bf16):
        return jax.ShapeDtypeStruct(dims, dtype)

    def over_ctx(x, mask, core=None):
        return lax.ppermute(x, "ctx", [(c, c ^ mask) for c in range(ctx) if core is None or c % 2 == core])

    def over_tp(x):
        return lax.ppermute(x, "tp", [(0, 1), (1, 0)])

    def across(x):
        pairs = [(2 * c + t, 2 * (c ^ 2) + (t ^ 1)) for c in range(ctx) for t in range(2)]
        return lax.ppermute(x, ("ctx", "tp"), pairs)

    def to_core(x, core):
        return lax.ppermute(x, "ctx", [(c, c ^ 1) for c in range(ctx) if c % 2 != core])

    packed = call(
        pack_kernel,
        shape(ctx, 4 * tok + META, HD),
        (segment_ids[None, :], routes.T, route_gates.T, query, key, value, resid),
        hbm=(3, 4, 5, 6),
        scratch=[pltpu.VMEM((4, tok, width), bf16), pltpu.SemaphoreType.DMA((4,))],
        vmem=60,
    )
    gain = over_tp(norm_gain)
    arrived = lax.all_to_all(packed, "ctx", split_axis=0, concat_axis=0, tiled=True)
    wg, wu, wd = w_gate[0], w_up[0], w_down[0]
    hidden_width = wg.shape[1]
    arrived, gain = lax.optimization_barrier((arrived, gain))
    gain = jnp.stack([norm_gain, gain]).astype(f32)
    hands = call(
        functools.partial(attend_kernel, block_slots(ctx, tok)),
        [shape(rows, HD)] * 2 + [shape(2, 2 * slots, span)] * 2 + [shape(2, 2 * span, LANES, dtype=f32)] * 2,
        (arrived,),
    )
    masks = [4 * k for k in range(levels)]
    half = width // 2
    results, waited = [], None
    for core in range(2):
        hand, pick, gates = hands[core::2]
        if waited is not None:
            hand, waited = lax.optimization_barrier((hand, waited))
        column = [hand] + [over_ctx(hand, m) for m in masks[1:]]
        if waited is None:
            column[:-1] = lax.optimization_barrier(column[:-1])
            waited = column[0]
        mine, theirs = call(compact_kernel, [shape(levels, 2 * slots + tok, HD)] * 2, (idx, pick, *column), smem=1)
        pieces = [over_ctx(theirs, 2), over_tp(mine[:, : 2 * slots]), across(theirs[:, : 2 * slots])]
        pieces = [mine] + pieces
        if core:
            *pieces, hidden = lax.optimization_barrier((*pieces, hidden))
        places = [[(t, m ^ f) for m in masks] for t, f in ((0, 0), (0, 2), (1, 0), (1, 2))]
        pieces += [over_ctx(p, 1) for p in pieces]
        places += [[(t, m ^ 1) for t, m in entry] for entry in places]
        hidden, own_hand = call(
            functools.partial(gate_up_kernel, places, heads),
            [shape(2 * slots, hidden_width), shape(tok, width)],
            (idx, wg, wu, gain, *pieces),
            smem=1,
            scratch=[pltpu.VMEM((2 * slots, D), bf16)],
            flops=8 * slots * D * hidden_width,
            moved=2 * (2 * slots * D + 2 * D * hidden_width),
        )
        peer = over_tp(hidden)

        def down(flip):
            return call(
                functools.partial(down_kernel, flip),
                shape(2 * slots, half),
                (idx, wd, hidden, peer),
                smem=1,
                flops=4 * slots * wd.shape[0] * half,
                moved=2 * (2 * slots * half + wd.shape[0] * half),
            )

        other = over_ctx(down(1), 1)
        half_out = down(0)
        got = over_ctx(call(pair_kernel, shape(slots, half), (idx, half_out, other), smem=1), 2)
        keep = call(weigh_kernel, shape(span, half, dtype=f32), (idx, pick, gates, half_out, other), smem=1)
        own, *sends = call(
            add_kernel,
            [shape(tok, half, dtype=f32)] + [shape(tok, half)] * (levels - 1),
            (idx, pick, gates, keep, got),
            smem=1,
            scratch=[pltpu.VMEM((span, half), f32)],
        )
        summed = call(sum_kernel, shape(tok, half), (own, *[over_ctx(s, m) for s, m in zip(sends, masks[1:])]))
        results += [own_hand, summed, to_core(summed, core)]
    return call(final_kernel, shape(tok, width), (idx, *results), smem=1)


def general(
    resid, query, key, value, norm_gain, routes, route_gates, segment_ids, w_gate, w_up, w_down
):
    tok_count = resid.shape[0]
    feat_width = resid.shape[1]
    head_count = feat_width // HD
    score_scale = 1.0 / math.sqrt(HD)
    query_pos = lax.axis_index("ctx") * tok_count + jnp.arange(tok_count, dtype=jnp.int32)
    key_segments = lax.all_gather(segment_ids, "ctx", axis=0, tiled=True)
    query_heads = query.reshape(tok_count, head_count, HD)
    start_sums = (
        jnp.zeros((tok_count, feat_width), jnp.float32),
        jnp.zeros((tok_count,), jnp.float32),
    )
    key_piece = lax.all_gather(key, "ctx", axis=0, tiled=True)
    value_piece = lax.all_gather(value, "ctx", axis=0, tiled=True)
    piece_len = key_piece.shape[0]
    block_len = math.gcd(piece_len, 512)
    block_count = piece_len // block_len
    key_blocks = key_piece.reshape(block_count, block_len, head_count, HD)
    value_blocks = value_piece.reshape(block_count, block_len, head_count, HD)

    def advance(state, inputs):
        key_block, value_block, block_id = inputs
        key_first = block_id * block_len

        def compute(current):
            acc_sum, key_total = current
            key_pos = key_first + jnp.arange(block_len, dtype=jnp.int32)
            key_segs = lax.dynamic_slice_in_dim(key_segments, key_first, block_len, 0)
            visible = jnp.logical_and(
                key_segs[None, :] == segment_ids[:, None], key_pos[None, :] <= query_pos[:, None]
            ).astype(jnp.float32)
            scores = (
                jnp.einsum(
                    "thd,shd->hts", query_heads, key_block, preferred_element_type=jnp.float32
                )
                * score_scale
            )
            weights = (jax.nn.silu(scores) * visible[None]).astype(jnp.bfloat16)
            summed = jnp.einsum(
                "hts,shd->thd", weights, value_block, preferred_element_type=jnp.float32
            )
            return (
                acc_sum + summed.reshape(tok_count, feat_width),
                key_total + jnp.sum(visible, axis=1),
            )

        last_key_seg = lax.dynamic_slice_in_dim(key_segments, key_first + block_len - 1, 1, 0)[0]
        reached = jnp.logical_and(key_first <= query_pos[-1], last_key_seg >= segment_ids[0])
        state = lax.cond(reached, compute, lambda current: current, state)
        return (state, None)

    block_ids = jnp.arange(block_count, dtype=jnp.int32)
    result, unused = lax.scan(advance, start_sums, (key_blocks, value_blocks, block_ids))
    acc_sum, key_total = result
    attended = acc_sum / jnp.sqrt(key_total)[:, None]
    hand_state = (resid.astype(jnp.float32) + attended).astype(jnp.bfloat16)
    hand_f32 = hand_state.astype(jnp.float32)
    square_sums = lax.psum(jnp.sum(hand_f32 * hand_f32, axis=1), ("tp", "sub"))
    normed = (
        hand_f32 * lax.rsqrt(square_sums / D + EPS)[:, None] * norm_gain.astype(jnp.float32)
    ).astype(jnp.bfloat16)
    ctx_count = lax.axis_size("ctx")
    expert_count = ctx_count // 2
    capacity = block_slots(ctx_count, tok_count)
    slot_total = expert_count * capacity
    recv_total = ctx_count * capacity
    flat_routes = routes.reshape(-1)
    onehot = (flat_routes[:, None] == jnp.arange(expert_count, dtype=jnp.int32)[None, :]).astype(
        jnp.int32
    )
    slot_rank = jnp.sum((jnp.cumsum(onehot, axis=0) - 1) * onehot, axis=1)
    slot_index = flat_routes * capacity + slot_rank
    position = jnp.arange(tok_count * TOPK, dtype=jnp.int32) // TOPK
    slot_source = jnp.full((slot_total,), tok_count, jnp.int32).at[slot_index].set(position)
    gate_local = w_gate[0]
    up_local = w_up[0]
    down_local = w_down[0]
    gathered = lax.all_gather(normed, ("tp", "sub"), axis=1, tiled=True)
    padded = jnp.concatenate([gathered, jnp.zeros((1, gathered.shape[1]), gathered.dtype)], axis=0)
    filled = padded[slot_source].reshape(expert_count, capacity, gathered.shape[1])
    arrived = lax.all_to_all(
        jnp.repeat(filled, 2, axis=0), "ctx", split_axis=0, concat_axis=0, tiled=True
    ).reshape(recv_total, gathered.shape[1])
    gate_sum = jnp.dot(arrived, gate_local, preferred_element_type=jnp.float32)
    up_sum = jnp.dot(arrived, up_local, preferred_element_type=jnp.float32)
    hidden = (jax.nn.silu(gate_sum) * up_sum).astype(jnp.bfloat16)
    down_rows_out = jnp.dot(
        lax.all_gather(hidden, ("tp", "sub"), axis=1, tiled=True),
        down_local,
        preferred_element_type=jnp.float32,
    ).astype(jnp.bfloat16)
    returned = lax.all_to_all(
        down_rows_out.reshape(ctx_count, capacity, feat_width),
        "ctx",
        split_axis=0,
        concat_axis=0,
        tiled=True,
    )
    combined = jnp.sum(
        returned.reshape(expert_count, 2, capacity, feat_width).astype(jnp.float32), axis=1
    ).reshape(slot_total, feat_width)
    picked = combined[slot_index].reshape(tok_count, TOPK, feat_width)
    mixed = hand_f32 + jnp.sum(route_gates[:, :, None] * picked, axis=1)
    return mixed.astype(jnp.bfloat16)


def block_slots(ctx, tok):
    return min(tok, max(2, tok * 10 // ctx))


def fits(mesh, resid):
    ctx, tp = mesh.shape["ctx"], mesh.shape["tp"]
    heads = resid.shape[1] // tp // HD
    tok = resid.shape[0] // mesh.shape["groups"] // ctx
    slots = ctx // 4 * block_slots(ctx, tok)
    whole = heads == ctx and 2 * tok == LANES and slots % 16 == 0
    return tp == 2 and mesh.shape["sub"] == 1 and whole and ctx >= 8 and ctx & (ctx - 1) == 0


def solution(mesh):
    placed = (
        P(("groups", "ctx"), ("tp", "sub")),
        P(("groups", "ctx"), ("tp", "sub")),
        P(("groups", "ctx"), ("tp", "sub")),
        P(("groups", "ctx"), ("tp", "sub")),
        P(("tp", "sub")),
        P(("groups", "ctx"), None),
        P(("groups", "ctx"), None),
        P(("groups", "ctx")),
        P("ctx", None, ("tp", "sub")),
        P("ctx", None, ("tp", "sub")),
        P("ctx", None, ("tp", "sub")),
    )

    def step(resid, *rest):
        per_device = heads_over_ctx if fits(mesh, resid) else general
        return jax.shard_map(
            per_device,
            mesh=mesh,
            in_specs=placed,
            out_specs=P(("groups", "ctx"), ("tp", "sub")),
            check_vma=False,
        )(resid, *rest)

    return step
```

```python
import functools
import math

import jax
import jax.numpy as jnp
from jax import lax
from jax.experimental import pallas as pl
from jax.experimental.pallas import tpu as pltpu
from jax.sharding import PartitionSpec as P

D = 4096
HD = 128
TOPK = 4
EPS = 1e-06
META = 16
LANES = 128
MIB = 1 << 20
PARTS = 4


def silu(v):
    return v * (0.5 * jnp.tanh(0.5 * v) + 0.5)


def call(kernel, out_shape, args, smem=0, hbm=(), scratch=(), vmem=8, flops=0, moved=0):
    spaces = [pltpu.SMEM if n < smem else pltpu.HBM if n in hbm else pltpu.VMEM for n in range(len(args))]
    several = isinstance(out_shape, (tuple, list))
    out = pl.BlockSpec(memory_space=pltpu.VMEM)
    return pl.pallas_call(
        kernel,
        out_shape=out_shape,
        in_specs=[pl.BlockSpec(memory_space=space) for space in spaces],
        out_specs=tuple(out for _ in out_shape) if several else out,
        scratch_shapes=list(scratch),
        compiler_params=pltpu.CompilerParams(vmem_limit_bytes=vmem * MIB),
    )(*args)


def pack_kernel(seg_ref, route_ref, gate_ref, q_ref, k_ref, v_ref, r_ref, out_ref, held_ref, sems):
    heads, tok = out_ref.shape[0], q_ref.shape[0]
    copies = [pltpu.make_async_copy(ref, held_ref.at[n], sems.at[n]) for n, ref in enumerate((q_ref, k_ref, v_ref, r_ref))]
    for copy in copies:
        copy.start()
    row = lax.broadcasted_iota(jnp.int32, (META, tok), 0)
    seg = jnp.broadcast_to(seg_ref[...].astype(jnp.float32), (META, tok))
    parts = []
    for e in range(heads // 2):
        gate = jnp.sum(jnp.where(route_ref[...] == e, gate_ref[...], 0.0), axis=0, keepdims=True)
        gate = jnp.broadcast_to(gate, (META, tok))
        high = gate.astype(jnp.bfloat16).astype(jnp.float32)
        middle = (gate - high).astype(jnp.bfloat16).astype(jnp.float32)
        parts.append((high, middle, gate - high - middle))
    out_ref[:, 4 * tok :, :] = jnp.zeros((heads, META, HD), jnp.bfloat16)
    for h in range(heads):
        meta = jnp.where(row == 0, seg, 0.0)
        for n, piece in enumerate(parts[h // 2] + parts[h // 2 ^ 1], 1):
            meta = jnp.where(row == n, piece, meta)
        out_ref[h, 4 * tok :, 0:tok] = meta.astype(jnp.bfloat16)
    for n, copy in enumerate(copies):
        copy.wait()
        for h in range(heads):
            out_ref[h, n * tok : (n + 1) * tok, :] = held_ref[n, :, h * HD : (h + 1) * HD]


def attend_kernel(capacity, x_ref, even_ref, odd_ref, pick_even_ref, pick_odd_ref, gate_even_ref, gate_odd_ref):
    blocks = x_ref.shape[0]
    tok = LANES // 2
    levels = blocks // 4
    scale = 1.0 / math.sqrt(HD)
    lane = lax.broadcasted_iota(jnp.int32, (META, LANES), 1)
    row_at = lax.broadcasted_iota(jnp.int32, (LANES, LANES), 0)
    lane_at = lax.broadcasted_iota(jnp.int32, (LANES, LANES), 1)
    causal = lane_at <= row_at
    span = levels * tok
    slots = levels * capacity
    earlier_at = lax.broadcasted_iota(jnp.int32, (span, span), 0)
    later_at = lax.broadcasted_iota(jnp.int32, (span, span), 1)
    earlier = jnp.logical_and(earlier_at < later_at, earlier_at // tok == later_at // tok)
    earlier = earlier.astype(jnp.float32).astype(jnp.bfloat16)
    slot_at = lax.broadcasted_iota(jnp.int32, (slots, span), 0).astype(jnp.float32)
    base = (lax.broadcasted_iota(jnp.int32, (1, span), 1) // tok * capacity).astype(jnp.float32)

    def part(n, first, last):
        return x_ref[first:last, n * tok : (n + 1) * tok, :].reshape((last - first) * tok, HD)

    def scalars(first, second):
        left = x_ref[first, 4 * tok :, :].astype(jnp.float32)
        right = pltpu.roll(x_ref[second, 4 * tok :, :].astype(jnp.float32), tok, 1)
        return jnp.where(lane < tok, left, right)

    def gate_of(meta, which):
        first = 1 + 3 * which
        return meta[first : first + 1, :] + (meta[first + 1 : first + 2, :] + meta[first + 2 : first + 3, :])

    def down_rows(row):
        return jnp.transpose(jnp.broadcast_to(row, (LANES, LANES)))

    for y in range(2):
        for odd, (pick_ref, gate_ref) in enumerate(((pick_even_ref, gate_even_ref), (pick_odd_ref, gate_odd_ref))):
            metas = [scalars(4 * z + 2 * y + odd, 4 * z + 4 + 2 * y + odd) for z in range(0, levels, 2)]
            for which in range(2):
                rows = [gate_of(meta, which) for meta in metas]
                for n, row in enumerate(rows):
                    gate_ref[which, y * span + n * LANES : y * span + (n + 1) * LANES, :] = down_rows(row)
                named = (jnp.concatenate(rows, axis=1) > 0.0).astype(jnp.float32)
                rank = jnp.dot(
                    jnp.broadcast_to(named, (META, span)).astype(jnp.bfloat16),
                    earlier,
                    preferred_element_type=jnp.float32,
                )[0:1, :]
                target = jnp.broadcast_to(jnp.where(named > 0.0, base + rank, -1.0), (slots, span))
                pick = (slot_at == target).astype(jnp.float32).astype(jnp.bfloat16)
                pick_ref[which, y * slots : (y + 1) * slots, :] = pick

    seg_rows = []
    for i in range(blocks // 2):
        seg_rows.append(scalars(2 * i, 2 * i + 1)[0:1, :])
        seg_col = down_rows(seg_rows[i])
        masks = []
        for j in range(i + 1):
            same = seg_col == jnp.broadcast_to(seg_rows[j], (LANES, LANES))
            if j == i:
                same = jnp.logical_and(same, causal)
            masks.append(same.astype(jnp.float32))
        visible = jnp.concatenate(masks, axis=1)
        query = part(0, 2 * i, 2 * i + 2)
        keys = part(1, 0, 2 * i + 2)
        values = part(2, 0, 2 * i + 2)
        scores = (
            lax.dot_general(query, keys, (((1,), (1,)), ((), ())), preferred_element_type=jnp.float32) * scale
        )
        weights = (silu(scores) * visible).astype(jnp.bfloat16)
        summed = jnp.dot(weights, values, preferred_element_type=jnp.float32)
        counted = jnp.sum(visible, axis=1, keepdims=True)
        hand = (part(3, 2 * i, 2 * i + 2).astype(jnp.float32) + summed / jnp.sqrt(counted)).astype(jnp.bfloat16)
        at = (i % 2 * levels + i // 2) * tok
        even_ref[at : at + tok, :] = hand[:tok, :]
        odd_ref[at : at + tok, :] = hand[tok:, :]


def compact_kernel(idx_ref, pick_ref, *refs):
    mine_ref, theirs_ref = refs[-2:]
    me = idx_ref[0]
    levels = mine_ref.shape[0]
    pieces = refs[:levels]
    slots, span = pick_ref.shape[1] // 2, pick_ref.shape[2]
    tok = span // levels
    z, y = lax.div(me, 4), lax.rem(lax.div(me, 2), 2)
    for group in range(2):
        block = jnp.concatenate([p[group * span : (group + 1) * span, :] for p in pieces], axis=1)
        for which, out_ref in enumerate((mine_ref, theirs_ref)):
            here = slice(group * slots, (group + 1) * slots)
            rows = jnp.dot(pick_ref[which, here, :], block, preferred_element_type=jnp.float32).astype(jnp.bfloat16)
            for k in range(levels):
                out_ref[k, here, :] = rows[:, k * HD : (k + 1) * HD]
    for which, out_ref in enumerate((mine_ref, theirs_ref)):
        own = pl.ds(pl.multiple_of(((y ^ which) * levels + z) * tok, tok), tok)
        for k in range(levels):
            out_ref[k, 2 * slots :, :] = pieces[k][own, :]


def thirds(value):
    high = value.astype(jnp.bfloat16)
    rest = value - high.astype(jnp.float32)
    middle = rest.astype(jnp.bfloat16)
    return high, middle, (rest - middle.astype(jnp.float32)).astype(jnp.bfloat16)


def scale_kernel(places, idx_ref, gain_ref, *refs):
    pieces, out_ref = refs[: len(places)], refs[-1]
    me = idx_ref[0]
    heads = gain_ref.shape[1] // HD
    rows, tok = pieces[-1].shape[1], pieces[0].shape[1] - pieces[-1].shape[1]
    width = sum(map(len, places)) * HD
    tile = rows // 2
    for r in range(rows // tile):
        here = slice(r * tile, (r + 1) * tile)
        squares = jnp.zeros((tile, HD), jnp.float32)
        n = 0
        for ref, entries in zip(pieces, places):
            for k, (other, low, back) in enumerate(entries):
                head = lax.rem((me ^ low) + heads - 4 * back, heads)
                gain = gain_ref[other : other + 1, pl.ds(pl.multiple_of(head * HD, HD), HD)]
                v = ref[k, here, :].astype(jnp.float32)
                squares = squares + v * v
                out_ref[here, n : n + HD] = (v * gain).astype(jnp.bfloat16)
                if not other and r == 0:
                    out_ref[rows:, n : n + HD] = ref[k, rows : rows + tok, :]
                n += HD
        lane = lax.broadcasted_iota(jnp.int32, (tile, HD), 1)
        high, middle, low = thirds(jnp.broadcast_to(jnp.sum(squares, axis=1, keepdims=True), (tile, HD)))
        parts = jnp.where(lane == 0, high, jnp.where(lane == 1, middle, jnp.where(lane == 2, low, 0)))
        out_ref[here, width:] = parts.astype(jnp.bfloat16)


def row_offsets(places, heads, me, plane, flip):
    found = []
    for other, low, back in (entry for entries in places for entry in entries):
        head = lax.rem((me ^ low ^ flip) + heads - 4 * back, heads)
        found.append((other, pl.multiple_of(head * HD, HD), pl.multiple_of(((plane ^ other) * heads + head) * HD, HD)))
    return found


def half_projection(lhs, offsets, weight_ref, cols):
    weights = jnp.concatenate([weight_ref[pl.ds(at, HD), cols] for *_, at in offsets], axis=0)
    return jnp.dot(lhs, weights, preferred_element_type=jnp.float32)


def first_kernel(places, heads, idx_ref, wg_ref, wu_ref, lhs_ref, gate_ref, up_ref):
    rows = gate_ref.shape[0]
    offsets = row_offsets(places, heads, idx_ref[0], idx_ref[1], 0)
    width = min(256, wg_ref.shape[1])
    for n in range(wg_ref.shape[1] // width):
        cols = slice(n * width, (n + 1) * width)
        lhs = lhs_ref[0:rows, 0 : len(offsets) * HD]
        gate_ref[:, cols] = half_projection(lhs, offsets, wg_ref, cols)
        up_ref[:, cols] = half_projection(lhs, offsets, wu_ref, cols)


def second_kernel(places, heads, idx_ref, wg_ref, wu_ref, own_ref, lhs_ref, gate_ref, up_ref, hidden_ref, hand_ref):
    rows = gate_ref.shape[0]
    me, plane = idx_ref[0], idx_ref[1]
    for flip, ref in enumerate((own_ref, lhs_ref)):
        for n, (other, at, _) in enumerate(row_offsets(places, heads, me, plane, flip)):
            if not other:
                hand_ref[:, pl.ds(at, HD)] = ref[rows:, n * HD : (n + 1) * HD]
    offsets = row_offsets(places, heads, me, plane, 1)
    last = len(offsets) * HD
    squares = own_ref[0:rows, last:].astype(jnp.float32) + lhs_ref[0:rows, last:].astype(jnp.float32)
    scale = lax.rsqrt(jnp.sum(squares, axis=1, keepdims=True) / D + EPS)
    width = min(256, wg_ref.shape[1])
    for n in range(wg_ref.shape[1] // width):
        cols = slice(n * width, (n + 1) * width)
        lhs = lhs_ref[0:rows, 0:last]
        gate = (gate_ref[:, cols] + half_projection(lhs, offsets, wg_ref, cols)) * scale
        up = (up_ref[:, cols] + half_projection(lhs, offsets, wu_ref, cols)) * scale
        hidden_ref[:, cols] = (silu(gate) * up).astype(jnp.bfloat16)


def down_kernel(flip, parts, idx_ref, wd_ref, own_ref, peer_ref, *refs):
    out_refs = refs[-parts:]
    core, plane = lax.rem(idx_ref[0], 2), idx_ref[1]
    depth, width = own_ref.shape[1], out_refs[0].shape[1]
    total_width = parts * width
    first = (core ^ flip) * total_width
    own_rows = pl.ds(pl.multiple_of(plane * depth, depth), depth)
    peer_rows = pl.ds(pl.multiple_of((1 - plane) * depth, depth), depth)
    for n, out_ref in enumerate(out_refs):
        cols = pl.ds(pl.multiple_of(first + n * width, width), width)
        total = jnp.dot(own_ref[...], wd_ref[own_rows, cols], preferred_element_type=jnp.float32)
        total = total + jnp.dot(peer_ref[...], wd_ref[peer_rows, cols], preferred_element_type=jnp.float32)
        out_ref[...] = total.astype(jnp.bfloat16)


def pair_kernel(parts, idx_ref, *refs):
    send_ref = refs[-1]
    slots = send_ref.shape[0]
    y = lax.rem(lax.div(idx_ref[0], 2), 2)
    theirs = pl.ds(pl.multiple_of((1 - y) * slots, slots), slots)
    width = refs[0].shape[1]
    for n in range(parts):
        both = refs[n][theirs, :].astype(jnp.float32) + refs[parts + n][theirs, :].astype(jnp.float32)
        send_ref[:, n * width : (n + 1) * width] = both.astype(jnp.bfloat16)


def spread(pick, rows):
    return lax.dot_general(pick, rows, (((0,), (0,)), ((), ())), preferred_element_type=jnp.float32)


def weigh_kernel(parts, idx_ref, pick_ref, gate_ref, *refs):
    slots, span = pick_ref.shape[1] // 2, pick_ref.shape[2]
    y = lax.rem(lax.div(idx_ref[0], 2), 2)
    mine = pl.ds(pl.multiple_of(y * slots, slots), slots)
    gate = gate_ref[0, pl.ds(pl.multiple_of(y * span, span), span), :]
    pick = pick_ref[0, mine, :]
    width = refs[0].shape[1]
    for n in range(parts):
        cols = slice(n * width, (n + 1) * width)
        total = spread(pick, refs[n][mine, :]) + spread(pick, refs[parts + n][mine, :])
        refs[-1][:, cols] = total * jnp.concatenate([gate] * (width // LANES), axis=1)


def add_kernel(idx_ref, pick_ref, gate_ref, keep_ref, got_ref, own_ref, *refs):
    send_refs, total_ref = refs[:-1], refs[-1]
    slots, span = pick_ref.shape[1] // 2, pick_ref.shape[2]
    tok = own_ref.shape[0]
    z, y = lax.div(idx_ref[0], 4), lax.rem(lax.div(idx_ref[0], 2), 2)
    gate = gate_ref[1, pl.ds(pl.multiple_of(y * span, span), span), :]
    pick = pick_ref[1, pl.ds(pl.multiple_of(y * slots, slots), slots), :]
    width = 4 * LANES
    for n in range(got_ref.shape[1] // width):
        cols = slice(n * width, (n + 1) * width)
        more = spread(pick, got_ref[:, cols]) * jnp.concatenate([gate] * (width // LANES), axis=1)
        total_ref[:, cols] = keep_ref[:, cols] + more
    own_ref[...] = total_ref[pl.ds(pl.multiple_of(z * tok, tok), tok), :]
    for k, ref in enumerate(send_refs, 1):
        there = lax.rem(z + k, len(send_refs) + 1)
        ref[...] = total_ref[pl.ds(pl.multiple_of(there * tok, tok), tok), :].astype(jnp.bfloat16)


def sum_kernel(own_ref, *refs):
    total = own_ref[...]
    for ref in refs[:-1]:
        total = total + ref[...].astype(jnp.float32)
    refs[-1][...] = total.astype(refs[-1].dtype)


def final_kernel(idx_ref, *refs):
    out_ref = refs[-1]
    core = lax.rem(idx_ref[0], 2)
    for n in range(2):
        hand_ref, own_ref, other_ref = refs[3 * n : 3 * n + 3]
        half = own_ref.shape[1]

        @pl.when(core == n)
        def _(hand_ref=hand_ref, halves=(own_ref, other_ref) if n == 0 else (other_ref, own_ref)):
            for m, ref in enumerate(halves):
                cols = slice(m * half, (m + 1) * half)
                out_ref[:, cols] = (hand_ref[:, cols].astype(jnp.float32) + ref[...].astype(jnp.float32)).astype(
                    jnp.bfloat16
                )


def heads_over_ctx(
    resid, query, key, value, norm_gain, routes, route_gates, segment_ids, w_gate, w_up, w_down
):
    ctx = lax.axis_size("ctx")
    heads, tok, width = ctx, resid.shape[0], resid.shape[1]
    levels = ctx // 4
    bf16, f32 = jnp.bfloat16, jnp.float32
    rows = ctx // 2 * tok
    span, slots = levels * tok, levels * block_slots(ctx, tok)
    me, plane = lax.axis_index("ctx"), lax.axis_index("tp")
    idx = jnp.stack([me, plane]).astype(jnp.int32)

    def shape(*dims, dtype=bf16):
        return jax.ShapeDtypeStruct(dims, dtype)

    def over_ctx(x, mask, core=None):
        return lax.ppermute(x, "ctx", [(c, c ^ mask) for c in range(ctx) if core is None or c % 2 == core])

    def along_z(x, steps):
        return lax.ppermute(x, "ctx", [(c, (c + 4 * steps) % ctx) for c in range(ctx)])

    def over_tp(x):
        return lax.ppermute(x, "tp", [(0, 1), (1, 0)])

    def across(x):
        pairs = [(2 * c + t, 2 * (c ^ 2) + (t ^ 1)) for c in range(ctx) for t in range(2)]
        return lax.ppermute(x, ("ctx", "tp"), pairs)

    def to_core(x, core):
        return lax.ppermute(x, "ctx", [(c, c ^ 1) for c in range(ctx) if c % 2 != core])

    packed = call(
        pack_kernel,
        shape(ctx, 4 * tok + META, HD),
        (segment_ids[None, :], routes.T, route_gates.T, query, key, value, resid),
        hbm=(3, 4, 5, 6),
        scratch=[pltpu.VMEM((4, tok, width), bf16), pltpu.SemaphoreType.DMA((4,))],
        vmem=60,
    )
    gain = over_tp(norm_gain)
    arrived = lax.all_to_all(packed, "ctx", split_axis=0, concat_axis=0, tiled=True)
    wg, wu, wd = w_gate[0], w_up[0], w_down[0]
    hidden_width = wg.shape[1]
    arrived, gain = lax.optimization_barrier((arrived, gain))
    gain = jnp.stack([norm_gain, gain]).astype(f32)
    hands = call(
        functools.partial(attend_kernel, block_slots(ctx, tok)),
        [shape(rows, HD)] * 2 + [shape(2, 2 * slots, span)] * 2 + [shape(2, 2 * span, LANES, dtype=f32)] * 2,
        (arrived,),
    )
    half = width // 2
    columns = []
    for hand in hands[:2]:
        if columns:
            hand, columns[0][1] = lax.optimization_barrier((hand, columns[0][1]))
        columns.append([hand] + [along_z(hand, k) for k in range(1, levels)])
    places = [[(t, f, k) for k in range(levels)] for t, f in ((0, 0), (0, 2), (1, 0), (1, 2))]
    pieces, compacted = [], []
    for pick, column in zip(hands[2:4], columns):
        mine, theirs = call(
            compact_kernel, [shape(levels, 2 * slots + tok, HD)] * 2, (idx, pick, *column, *compacted), smem=1
        )
        compacted = [theirs]
        pieces.append([mine, over_ctx(theirs, 2), over_tp(mine[:, : 2 * slots]), across(theirs[:, : 2 * slots])])
    fronts, after = [], pieces[1][0]
    for got in pieces:
        mixed = call(
            functools.partial(scale_kernel, places),
            shape(2 * slots + tok, (4 * levels + 1) * HD),
            (idx, gain, *got, after),
            smem=1,
        )
        sums = call(
            functools.partial(first_kernel, places, heads),
            [shape(2 * slots, hidden_width, dtype=f32)] * 2,
            (idx, wg, wu, mixed),
            smem=1,
        )
        hidden, own_hand = call(
            functools.partial(second_kernel, places, heads),
            [shape(2 * slots, hidden_width), shape(tok, width)],
            (idx, wg, wu, mixed, over_ctx(mixed, 1), *sums),
            smem=1,
        )
        fronts.append((hidden, over_tp(hidden), own_hand))
        after = hidden
    half = width // 2
    results, after, added = [], [fronts[1][0]], [fronts[1][1]]

    def down(flip, *args):
        return call(
            functools.partial(down_kernel, flip, PARTS),
            [shape(2 * slots, half // PARTS)] * PARTS,
            (idx, wd, *args),
            smem=1,
        )

    for core, (hidden, peer, own_hand) in enumerate(fronts):
        pick, gates = hands[2 + core], hands[4 + core]
        other = [over_ctx(part, 1) for part in down(1, hidden, peer, *after)]
        half_out = down(0, hidden, peer)
        send = call(
            functools.partial(pair_kernel, PARTS), shape(slots, half), (idx, *half_out, *other, *added), smem=1
        )
        after = [send]
        got = over_ctx(send, 2)
        keep = call(
            functools.partial(weigh_kernel, PARTS),
            shape(span, half, dtype=f32),
            (idx, pick, gates, *half_out, *other),
            smem=1,
        )
        own, *sends = call(
            add_kernel,
            [shape(tok, half, dtype=f32)] + [shape(tok, half)] * (levels - 1),
            (idx, pick, gates, keep, got),
            smem=1,
            scratch=[pltpu.VMEM((span, half), f32)],
        )
        added = [own]
        summed = call(sum_kernel, shape(tok, half, dtype=f32), (own, *[along_z(s, k) for k, s in enumerate(sends, 1)]))
        results += [own_hand, summed, to_core(summed, core)]
    return call(final_kernel, shape(tok, width), (idx, *results), smem=1)


def general(
    resid, query, key, value, norm_gain, routes, route_gates, segment_ids, w_gate, w_up, w_down
):
    tok_count = resid.shape[0]
    feat_width = resid.shape[1]
    head_count = feat_width // HD
    score_scale = 1.0 / math.sqrt(HD)
    query_pos = lax.axis_index("ctx") * tok_count + jnp.arange(tok_count, dtype=jnp.int32)
    key_segments = lax.all_gather(segment_ids, "ctx", axis=0, tiled=True)
    query_heads = query.reshape(tok_count, head_count, HD)
    start_sums = (
        jnp.zeros((tok_count, feat_width), jnp.float32),
        jnp.zeros((tok_count,), jnp.float32),
    )
    key_piece = lax.all_gather(key, "ctx", axis=0, tiled=True)
    value_piece = lax.all_gather(value, "ctx", axis=0, tiled=True)
    piece_len = key_piece.shape[0]
    block_len = math.gcd(piece_len, 512)
    block_count = piece_len // block_len
    key_blocks = key_piece.reshape(block_count, block_len, head_count, HD)
    value_blocks = value_piece.reshape(block_count, block_len, head_count, HD)

    def advance(state, inputs):
        key_block, value_block, block_id = inputs
        key_first = block_id * block_len

        def compute(current):
            acc_sum, key_total = current
            key_pos = key_first + jnp.arange(block_len, dtype=jnp.int32)
            key_segs = lax.dynamic_slice_in_dim(key_segments, key_first, block_len, 0)
            visible = jnp.logical_and(
                key_segs[None, :] == segment_ids[:, None], key_pos[None, :] <= query_pos[:, None]
            ).astype(jnp.float32)
            scores = (
                jnp.einsum(
                    "thd,shd->hts", query_heads, key_block, preferred_element_type=jnp.float32
                )
                * score_scale
            )
            weights = (jax.nn.silu(scores) * visible[None]).astype(jnp.bfloat16)
            summed = jnp.einsum(
                "hts,shd->thd", weights, value_block, preferred_element_type=jnp.float32
            )
            return (
                acc_sum + summed.reshape(tok_count, feat_width),
                key_total + jnp.sum(visible, axis=1),
            )

        last_key_seg = lax.dynamic_slice_in_dim(key_segments, key_first + block_len - 1, 1, 0)[0]
        reached = jnp.logical_and(key_first <= query_pos[-1], last_key_seg >= segment_ids[0])
        state = lax.cond(reached, compute, lambda current: current, state)
        return (state, None)

    block_ids = jnp.arange(block_count, dtype=jnp.int32)
    result, unused = lax.scan(advance, start_sums, (key_blocks, value_blocks, block_ids))
    acc_sum, key_total = result
    attended = acc_sum / jnp.sqrt(key_total)[:, None]
    hand_state = (resid.astype(jnp.float32) + attended).astype(jnp.bfloat16)
    hand_f32 = hand_state.astype(jnp.float32)
    square_sums = lax.psum(jnp.sum(hand_f32 * hand_f32, axis=1), ("tp", "sub"))
    normed = (
        hand_f32 * lax.rsqrt(square_sums / D + EPS)[:, None] * norm_gain.astype(jnp.float32)
    ).astype(jnp.bfloat16)
    ctx_count = lax.axis_size("ctx")
    expert_count = ctx_count // 2
    capacity = block_slots(ctx_count, tok_count)
    slot_total = expert_count * capacity
    recv_total = ctx_count * capacity
    flat_routes = routes.reshape(-1)
    onehot = (flat_routes[:, None] == jnp.arange(expert_count, dtype=jnp.int32)[None, :]).astype(
        jnp.int32
    )
    slot_rank = jnp.sum((jnp.cumsum(onehot, axis=0) - 1) * onehot, axis=1)
    slot_index = flat_routes * capacity + slot_rank
    position = jnp.arange(tok_count * TOPK, dtype=jnp.int32) // TOPK
    slot_source = jnp.full((slot_total,), tok_count, jnp.int32).at[slot_index].set(position)
    gate_local = w_gate[0]
    up_local = w_up[0]
    down_local = w_down[0]
    gathered = lax.all_gather(normed, ("tp", "sub"), axis=1, tiled=True)
    padded = jnp.concatenate([gathered, jnp.zeros((1, gathered.shape[1]), gathered.dtype)], axis=0)
    filled = padded[slot_source].reshape(expert_count, capacity, gathered.shape[1])
    arrived = lax.all_to_all(
        jnp.repeat(filled, 2, axis=0), "ctx", split_axis=0, concat_axis=0, tiled=True
    ).reshape(recv_total, gathered.shape[1])
    gate_sum = jnp.dot(arrived, gate_local, preferred_element_type=jnp.float32)
    up_sum = jnp.dot(arrived, up_local, preferred_element_type=jnp.float32)
    hidden = (jax.nn.silu(gate_sum) * up_sum).astype(jnp.bfloat16)
    down_rows_out = jnp.dot(
        lax.all_gather(hidden, ("tp", "sub"), axis=1, tiled=True),
        down_local,
        preferred_element_type=jnp.float32,
    ).astype(jnp.bfloat16)
    returned = lax.all_to_all(
        down_rows_out.reshape(ctx_count, capacity, feat_width),
        "ctx",
        split_axis=0,
        concat_axis=0,
        tiled=True,
    )
    combined = jnp.sum(
        returned.reshape(expert_count, 2, capacity, feat_width).astype(jnp.float32), axis=1
    ).reshape(slot_total, feat_width)
    picked = combined[slot_index].reshape(tok_count, TOPK, feat_width)
    mixed = hand_f32 + jnp.sum(route_gates[:, :, None] * picked, axis=1)
    return mixed.astype(jnp.bfloat16)


def block_slots(ctx, tok):
    return min(tok, max(2, tok * 10 // ctx))


def fits(mesh, resid):
    ctx, tp = mesh.shape["ctx"], mesh.shape["tp"]
    heads = resid.shape[1] // tp // HD
    tok = resid.shape[0] // mesh.shape["groups"] // ctx
    slots = ctx // 4 * block_slots(ctx, tok)
    whole = heads == ctx and 2 * tok == LANES and slots % 16 == 0
    return tp == 2 and mesh.shape["sub"] == 1 and whole and ctx >= 8 and ctx & (ctx - 1) == 0


def solution(mesh):
    placed = (
        P(("groups", "ctx"), ("tp", "sub")),
        P(("groups", "ctx"), ("tp", "sub")),
        P(("groups", "ctx"), ("tp", "sub")),
        P(("groups", "ctx"), ("tp", "sub")),
        P(("tp", "sub")),
        P(("groups", "ctx"), None),
        P(("groups", "ctx"), None),
        P(("groups", "ctx")),
        P("ctx", None, ("tp", "sub")),
        P("ctx", None, ("tp", "sub")),
        P("ctx", None, ("tp", "sub")),
    )

    def step(resid, *rest):
        per_device = heads_over_ctx if fits(mesh, resid) else general
        return jax.shard_map(
            per_device,
            mesh=mesh,
            in_specs=placed,
            out_specs=P(("groups", "ctx"), ("tp", "sub")),
            check_vma=False,
        )(resid, *rest)

    return step
```

```python
import functools
import math

import jax
import jax.numpy as jnp
from jax import lax
from jax.experimental import pallas as pl
from jax.experimental.pallas import tpu as pltpu
from jax.sharding import PartitionSpec as P

D = 4096
HD = 128
TOPK = 4
EPS = 1e-06
META = 16
LANES = 128
MIB = 1 << 20
PARTS = 4


def silu(v):
    return v * (0.5 * jnp.tanh(0.5 * v) + 0.5)


def call(kernel, out_shape, args, smem=0, hbm=(), scratch=(), vmem=8, flops=0, moved=0):
    spaces = [pltpu.SMEM if n < smem else pltpu.HBM if n in hbm else pltpu.VMEM for n in range(len(args))]
    several = isinstance(out_shape, (tuple, list))
    out = pl.BlockSpec(memory_space=pltpu.VMEM)
    return pl.pallas_call(
        kernel,
        out_shape=out_shape,
        in_specs=[pl.BlockSpec(memory_space=space) for space in spaces],
        out_specs=tuple(out for _ in out_shape) if several else out,
        scratch_shapes=list(scratch),
        compiler_params=pltpu.CompilerParams(vmem_limit_bytes=vmem * MIB),
    )(*args)


def pack_kernel(seg_ref, route_ref, gate_ref, q_ref, k_ref, v_ref, r_ref, out_ref, held_ref, sems):
    heads, tok = out_ref.shape[0], q_ref.shape[0]
    copies = [pltpu.make_async_copy(ref, held_ref.at[n], sems.at[n]) for n, ref in enumerate((q_ref, k_ref, v_ref, r_ref))]
    for copy in copies:
        copy.start()
    row = lax.broadcasted_iota(jnp.int32, (META, tok), 0)
    seg = jnp.broadcast_to(seg_ref[...].astype(jnp.float32), (META, tok))
    parts = []
    for e in range(heads // 2):
        gate = jnp.sum(jnp.where(route_ref[...] == e, gate_ref[...], 0.0), axis=0, keepdims=True)
        gate = jnp.broadcast_to(gate, (META, tok))
        high = gate.astype(jnp.bfloat16).astype(jnp.float32)
        middle = (gate - high).astype(jnp.bfloat16).astype(jnp.float32)
        parts.append((high, middle, gate - high - middle))
    out_ref[:, 4 * tok :, :] = jnp.zeros((heads, META, HD), jnp.bfloat16)
    for h in range(heads):
        meta = jnp.where(row == 0, seg, 0.0)
        for n, piece in enumerate(parts[h // 2] + parts[h // 2 ^ 1], 1):
            meta = jnp.where(row == n, piece, meta)
        out_ref[h, 4 * tok :, 0:tok] = meta.astype(jnp.bfloat16)
    for n, copy in enumerate(copies):
        copy.wait()
        for h in range(heads):
            out_ref[h, n * tok : (n + 1) * tok, :] = held_ref[n, :, h * HD : (h + 1) * HD]


def attend_kernel(capacity, x_ref, even_ref, odd_ref, pick_even_ref, pick_odd_ref, gate_even_ref, gate_odd_ref):
    blocks = x_ref.shape[0]
    tok = LANES // 2
    levels = blocks // 4
    scale = 1.0 / math.sqrt(HD)
    lane = lax.broadcasted_iota(jnp.int32, (META, LANES), 1)
    row_at = lax.broadcasted_iota(jnp.int32, (LANES, LANES), 0)
    lane_at = lax.broadcasted_iota(jnp.int32, (LANES, LANES), 1)
    causal = lane_at <= row_at
    span = levels * tok
    slots = levels * capacity
    earlier_at = lax.broadcasted_iota(jnp.int32, (span, span), 0)
    later_at = lax.broadcasted_iota(jnp.int32, (span, span), 1)
    earlier = jnp.logical_and(earlier_at < later_at, earlier_at // tok == later_at // tok)
    earlier = earlier.astype(jnp.float32).astype(jnp.bfloat16)
    slot_at = lax.broadcasted_iota(jnp.int32, (slots, span), 0).astype(jnp.float32)
    base = (lax.broadcasted_iota(jnp.int32, (1, span), 1) // tok * capacity).astype(jnp.float32)

    def part(n, first, last):
        return x_ref[first:last, n * tok : (n + 1) * tok, :].reshape((last - first) * tok, HD)

    def scalars(first, second):
        left = x_ref[first, 4 * tok :, :].astype(jnp.float32)
        right = pltpu.roll(x_ref[second, 4 * tok :, :].astype(jnp.float32), tok, 1)
        return jnp.where(lane < tok, left, right)

    def gate_of(meta, which):
        first = 1 + 3 * which
        return meta[first : first + 1, :] + (meta[first + 1 : first + 2, :] + meta[first + 2 : first + 3, :])

    def down_rows(row):
        return jnp.transpose(jnp.broadcast_to(row, (LANES, LANES)))

    for y in range(2):
        for odd, (pick_ref, gate_ref) in enumerate(((pick_even_ref, gate_even_ref), (pick_odd_ref, gate_odd_ref))):
            metas = [scalars(4 * z + 2 * y + odd, 4 * z + 4 + 2 * y + odd) for z in range(0, levels, 2)]
            for which in range(2):
                rows = [gate_of(meta, which) for meta in metas]
                for n, row in enumerate(rows):
                    gate_ref[which, y * span + n * LANES : y * span + (n + 1) * LANES, :] = down_rows(row)
                named = (jnp.concatenate(rows, axis=1) > 0.0).astype(jnp.float32)
                rank = jnp.dot(
                    jnp.broadcast_to(named, (META, span)).astype(jnp.bfloat16),
                    earlier,
                    preferred_element_type=jnp.float32,
                )[0:1, :]
                target = jnp.broadcast_to(jnp.where(named > 0.0, base + rank, -1.0), (slots, span))
                pick = (slot_at == target).astype(jnp.float32).astype(jnp.bfloat16)
                pick_ref[which, y * slots : (y + 1) * slots, :] = pick

    seg_rows = []
    for i in range(blocks // 2):
        seg_rows.append(scalars(2 * i, 2 * i + 1)[0:1, :])
        seg_col = down_rows(seg_rows[i])
        masks = []
        for j in range(i + 1):
            same = seg_col == jnp.broadcast_to(seg_rows[j], (LANES, LANES))
            if j == i:
                same = jnp.logical_and(same, causal)
            masks.append(same.astype(jnp.float32))
        visible = jnp.concatenate(masks, axis=1)
        query = part(0, 2 * i, 2 * i + 2)
        keys = part(1, 0, 2 * i + 2)
        values = part(2, 0, 2 * i + 2)
        scores = (
            lax.dot_general(query, keys, (((1,), (1,)), ((), ())), preferred_element_type=jnp.float32) * scale
        )
        weights = (silu(scores) * visible).astype(jnp.bfloat16)
        summed = jnp.dot(weights, values, preferred_element_type=jnp.float32)
        counted = jnp.sum(visible, axis=1, keepdims=True)
        hand = (part(3, 2 * i, 2 * i + 2).astype(jnp.float32) + summed / jnp.sqrt(counted)).astype(jnp.bfloat16)
        at = (i % 2 * levels + i // 2) * tok
        even_ref[at : at + tok, :] = hand[:tok, :]
        odd_ref[at : at + tok, :] = hand[tok:, :]


def near_kernel(pick_even_ref, pick_odd_ref, even_ref, odd_ref, mine_ref, theirs_ref):
    slots, span = pick_even_ref.shape[1] // 2, pick_even_ref.shape[2]
    for n, (pick_ref, ref) in enumerate(((pick_even_ref, even_ref), (pick_odd_ref, odd_ref))):
        for group in range(2):
            here = slice(group * slots, (group + 1) * slots)
            block = ref[group * span : (group + 1) * span, :]
            for which, out_ref in enumerate((mine_ref, theirs_ref)):
                rows = jnp.dot(pick_ref[which, here, :], block, preferred_element_type=jnp.float32)
                out_ref[n, here, :] = rows.astype(jnp.bfloat16)


def compact_kernel(idx_ref, pick_ref, *refs):
    *out_refs, mine_own_ref, theirs_own_ref = refs[-4:]
    me = idx_ref[0]
    levels, tok = mine_own_ref.shape[:2]
    pieces = refs[:levels]
    slots, span = pick_ref.shape[1] // 2, pick_ref.shape[2]
    z, y = lax.div(me, 4), lax.rem(lax.div(me, 2), 2)
    for group in range(2):
        block = jnp.concatenate([p[group * span : (group + 1) * span, :] for p in pieces], axis=1)
        for which, out_ref in enumerate(out_refs):
            here = slice(group * slots, (group + 1) * slots)
            rows = jnp.dot(pick_ref[which, here, :], block, preferred_element_type=jnp.float32).astype(jnp.bfloat16)
            for k in range(levels):
                out_ref[k, here, :] = rows[:, k * HD : (k + 1) * HD]
    for which, out_ref in enumerate((mine_own_ref, theirs_own_ref)):
        own = pl.ds(pl.multiple_of(((y ^ which) * levels + z) * tok, tok), tok)
        for k in range(levels):
            out_ref[k, :, :] = pieces[k][own, :]


def gather_kernel(*refs):
    out_ref = refs[-1]
    for n in range(out_ref.shape[0]):
        out_ref[n] = refs[n][...]


def own_rows_kernel(idx_ref, even_ref, odd_ref, by_y_ref, keep_ref, send_ref):
    core = lax.rem(idx_ref[0], 2)
    levels = even_ref.shape[0]
    for n, ref in enumerate((even_ref, odd_ref)):
        for same, out_ref in ((True, keep_ref), (False, send_ref)):
            @pl.when((core == n) == same)
            def _(ref=ref, out_ref=out_ref, n=n):
                out_ref[:levels] = ref[...]
                out_ref[levels:] = by_y_ref[n]


def thirds(value):
    high = value.astype(jnp.bfloat16)
    rest = value - high.astype(jnp.float32)
    middle = rest.astype(jnp.bfloat16)
    return high, middle, (rest - middle.astype(jnp.float32)).astype(jnp.bfloat16)


def scale_kernel(places, idx_ref, gain_ref, *refs):
    pieces, out_ref = refs[: len(places)], refs[-1]
    me = idx_ref[0]
    heads = gain_ref.shape[1] // HD
    rows = out_ref.shape[0]
    width = sum(map(len, places)) * HD
    tile = rows // 2
    for r in range(rows // tile):
        here = slice(r * tile, (r + 1) * tile)
        squares = jnp.zeros((tile, HD), jnp.float32)
        n = 0
        for ref, entries in zip(pieces, places):
            for k, other, low, back in entries:
                head = lax.rem((me ^ low) + heads - 4 * back, heads)
                gain = gain_ref[other : other + 1, pl.ds(pl.multiple_of(head * HD, HD), HD)]
                v = ref[k, here, :].astype(jnp.float32)
                squares = squares + v * v
                out_ref[here, n : n + HD] = (v * gain).astype(jnp.bfloat16)
                n += HD
        lane = lax.broadcasted_iota(jnp.int32, (tile, HD), 1)
        high, middle, low = thirds(jnp.broadcast_to(jnp.sum(squares, axis=1, keepdims=True), (tile, HD)))
        parts = jnp.where(lane == 0, high, jnp.where(lane == 1, middle, jnp.where(lane == 2, low, 0)))
        out_ref[here, width:] = parts.astype(jnp.bfloat16)


def row_offsets(places, heads, me, plane, flip):
    found = []
    for _, other, low, back in (entry for entries in places for entry in entries):
        head = lax.rem((me ^ low ^ flip) + heads - 4 * back, heads)
        found.append(pl.multiple_of(((plane ^ other) * heads + head) * HD, HD))
    return found


def half_projection(lhs, offsets, weight_ref, cols):
    weights = jnp.concatenate([weight_ref[pl.ds(at, HD), cols] for at in offsets], axis=0)
    return jnp.dot(lhs, weights, preferred_element_type=jnp.float32)


def first_kernel(places, heads, idx_ref, wg_ref, wu_ref, lhs_ref, gate_ref, up_ref):
    rows = gate_ref.shape[0]
    offsets = row_offsets(places, heads, idx_ref[0], idx_ref[1], 0)
    width = min(256, wg_ref.shape[1])
    for n in range(wg_ref.shape[1] // width):
        cols = slice(n * width, (n + 1) * width)
        lhs = lhs_ref[0:rows, 0 : len(offsets) * HD]
        gate_ref[:, cols] = half_projection(lhs, offsets, wg_ref, cols)
        up_ref[:, cols] = half_projection(lhs, offsets, wu_ref, cols)


def second_kernel(places, heads, idx_ref, wg_ref, wu_ref, own_ref, lhs_ref, gate_ref, up_ref, hidden_ref):
    rows = gate_ref.shape[0]
    me, plane = idx_ref[0], idx_ref[1]
    offsets = row_offsets(places, heads, me, plane, 1)
    last = len(offsets) * HD
    squares = own_ref[0:rows, last:].astype(jnp.float32) + lhs_ref[0:rows, last:].astype(jnp.float32)
    scale = lax.rsqrt(jnp.sum(squares, axis=1, keepdims=True) / D + EPS)
    width = min(256, wg_ref.shape[1])
    for n in range(wg_ref.shape[1] // width):
        cols = slice(n * width, (n + 1) * width)
        lhs = lhs_ref[0:rows, 0:last]
        gate = (gate_ref[:, cols] + half_projection(lhs, offsets, wg_ref, cols)) * scale
        up = (up_ref[:, cols] + half_projection(lhs, offsets, wu_ref, cols)) * scale
        hidden_ref[:, cols] = (silu(gate) * up).astype(jnp.bfloat16)


def down_kernel(flip, parts, idx_ref, wd_ref, own_ref, peer_ref, *refs):
    out_refs = refs[-parts:]
    core, plane = lax.rem(idx_ref[0], 2), idx_ref[1]
    depth, width = own_ref.shape[1], out_refs[0].shape[1]
    total_width = parts * width
    first = (core ^ flip) * total_width
    own_rows = pl.ds(pl.multiple_of(plane * depth, depth), depth)
    peer_rows = pl.ds(pl.multiple_of((1 - plane) * depth, depth), depth)
    for n, out_ref in enumerate(out_refs):
        cols = pl.ds(pl.multiple_of(first + n * width, width), width)
        total = jnp.dot(own_ref[...], wd_ref[own_rows, cols], preferred_element_type=jnp.float32)
        total = total + jnp.dot(peer_ref[...], wd_ref[peer_rows, cols], preferred_element_type=jnp.float32)
        out_ref[...] = total.astype(jnp.bfloat16)


def pair_kernel(parts, idx_ref, *refs):
    send_ref = refs[-1]
    slots = send_ref.shape[0]
    y = lax.rem(lax.div(idx_ref[0], 2), 2)
    theirs = pl.ds(pl.multiple_of((1 - y) * slots, slots), slots)
    width = refs[0].shape[1]
    for n in range(parts):
        both = refs[n][theirs, :].astype(jnp.float32) + refs[parts + n][theirs, :].astype(jnp.float32)
        send_ref[:, n * width : (n + 1) * width] = both.astype(jnp.bfloat16)


def spread(pick, rows):
    return lax.dot_general(pick, rows, (((0,), (0,)), ((), ())), preferred_element_type=jnp.float32)


def weigh_kernel(parts, idx_ref, pick_ref, gate_ref, *refs):
    slots, span = pick_ref.shape[1] // 2, pick_ref.shape[2]
    y = lax.rem(lax.div(idx_ref[0], 2), 2)
    mine = pl.ds(pl.multiple_of(y * slots, slots), slots)
    gate = gate_ref[0, pl.ds(pl.multiple_of(y * span, span), span), :]
    pick = pick_ref[0, mine, :]
    width = refs[0].shape[1]
    for n in range(parts):
        cols = slice(n * width, (n + 1) * width)
        total = spread(pick, refs[n][mine, :]) + spread(pick, refs[parts + n][mine, :])
        refs[-1][:, cols] = total * jnp.concatenate([gate] * (width // LANES), axis=1)


def add_kernel(idx_ref, pick_ref, gate_ref, keep_ref, got_ref, own_ref, *refs):
    send_refs, total_ref = refs[:-1], refs[-1]
    slots, span = pick_ref.shape[1] // 2, pick_ref.shape[2]
    tok = own_ref.shape[0]
    z, y = lax.div(idx_ref[0], 4), lax.rem(lax.div(idx_ref[0], 2), 2)
    gate = gate_ref[1, pl.ds(pl.multiple_of(y * span, span), span), :]
    pick = pick_ref[1, pl.ds(pl.multiple_of(y * slots, slots), slots), :]
    width = 4 * LANES
    for n in range(got_ref.shape[1] // width):
        cols = slice(n * width, (n + 1) * width)
        more = spread(pick, got_ref[:, cols]) * jnp.concatenate([gate] * (width // LANES), axis=1)
        total_ref[:, cols] = keep_ref[:, cols] + more
    own_ref[...] = total_ref[pl.ds(pl.multiple_of(z * tok, tok), tok), :]
    for k, ref in enumerate(send_refs, 1):
        there = lax.rem(z + k, len(send_refs) + 1)
        ref[...] = total_ref[pl.ds(pl.multiple_of(there * tok, tok), tok), :].astype(jnp.bfloat16)


def sum_kernel(own_ref, *refs):
    total = own_ref[...]
    for ref in refs[:-1]:
        total = total + ref[...].astype(jnp.float32)
    refs[-1][...] = total.astype(refs[-1].dtype)


def final_kernel(idx_ref, *refs):
    hand_refs, sum_refs, out_ref = refs[:2], refs[2:-1], refs[-1]
    me = idx_ref[0]
    core = lax.rem(me, 2)
    levels = hand_refs[0].shape[0] // 2
    heads = out_ref.shape[1] // HD
    for n in range(2):
        own_ref, other_ref = sum_refs[2 * n : 2 * n + 2]
        half = own_ref.shape[1]

        @pl.when(core == n)
        def _(halves=(own_ref, other_ref) if n == 0 else (other_ref, own_ref)):
            for flip, hand_ref in enumerate(hand_refs):
                for low in range(2):
                    for back in range(levels):
                        head = lax.rem((me ^ (2 * low) ^ flip) + heads - 4 * back, heads)
                        hand = hand_ref[low * levels + back].astype(jnp.float32)
                        at = pl.multiple_of(head * HD, HD)
                        inside = pl.multiple_of(lax.rem(head, heads // 2) * HD, HD)
                        first = halves[0][:, pl.ds(inside, HD)].astype(jnp.float32)
                        second = halves[1][:, pl.ds(inside, HD)].astype(jnp.float32)
                        total = hand + jnp.where(head < heads // 2, first, second)
                        out_ref[:, pl.ds(at, HD)] = total.astype(jnp.bfloat16)


def heads_over_ctx(
    resid, query, key, value, norm_gain, routes, route_gates, segment_ids, w_gate, w_up, w_down
):
    ctx = lax.axis_size("ctx")
    heads, tok, width = ctx, resid.shape[0], resid.shape[1]
    levels = ctx // 4
    bf16, f32 = jnp.bfloat16, jnp.float32
    rows = ctx // 2 * tok
    span, slots = levels * tok, levels * block_slots(ctx, tok)
    me, plane = lax.axis_index("ctx"), lax.axis_index("tp")
    idx = jnp.stack([me, plane]).astype(jnp.int32)

    def shape(*dims, dtype=bf16):
        return jax.ShapeDtypeStruct(dims, dtype)

    def over_ctx(x, mask, core=None):
        return lax.ppermute(x, "ctx", [(c, c ^ mask) for c in range(ctx) if core is None or c % 2 == core])

    def along_z(x, steps):
        return lax.ppermute(x, "ctx", [(c, (c + 4 * steps) % ctx) for c in range(ctx)])

    def over_tp(x):
        return lax.ppermute(x, "tp", [(0, 1), (1, 0)])

    def across(x):
        pairs = [(2 * c + t, 2 * (c ^ 2) + (t ^ 1)) for c in range(ctx) for t in range(2)]
        return lax.ppermute(x, ("ctx", "tp"), pairs)

    def to_core(x, core):
        return lax.ppermute(x, "ctx", [(c, c ^ 1) for c in range(ctx) if c % 2 != core])

    packed = call(
        pack_kernel,
        shape(ctx, 4 * tok + META, HD),
        (segment_ids[None, :], routes.T, route_gates.T, query, key, value, resid),
        hbm=(3, 4, 5, 6),
        scratch=[pltpu.VMEM((4, tok, width), bf16), pltpu.SemaphoreType.DMA((4,))],
        vmem=60,
    )
    gain = over_tp(norm_gain)
    arrived = lax.all_to_all(packed, "ctx", split_axis=0, concat_axis=0, tiled=True)
    wg, wu, wd = w_gate[0], w_up[0], w_down[0]
    hidden_width = wg.shape[1]
    arrived, gain = lax.optimization_barrier((arrived, gain))
    gain = jnp.stack([norm_gain, gain]).astype(f32)
    hands = call(
        functools.partial(attend_kernel, block_slots(ctx, tok)),
        [shape(rows, HD)] * 2 + [shape(2, 2 * slots, span)] * 2 + [shape(2, 2 * span, LANES, dtype=f32)] * 2,
        (arrived,),
    )
    half = width // 2
    columns = []
    for hand in hands[:2]:
        if columns:
            hand, columns[0][1] = lax.optimization_barrier((hand, columns[0][1]))
        columns.append([hand] + [along_z(hand, k) for k in range(1, levels)])
    near = call(near_kernel, [shape(2, 2 * slots, HD)] * 2, (*hands[2:4], *hands[:2]))
    near = [over_tp(near[0]), across(near[1])]
    pieces, places, blocks, compacted = [], [], [], near
    for core, (pick, column) in enumerate(zip(hands[2:4], columns)):
        mine, theirs, *own_rows = call(
            compact_kernel,
            [shape(levels, 2 * slots, HD)] * 2 + [shape(levels, tok, HD)] * 2,
            (idx, pick, *column, *compacted),
            smem=1,
        )
        blocks.append(own_rows)
        compacted = [theirs]
        far = [over_tp(mine[1:]), across(theirs[1:])]
        pieces.append([mine, over_ctx(theirs, 2), *far, *near])
        places.append(
            [[(k, 0, f, k) for k in range(levels)] for f in (0, 2)]
            + [[(k - 1, 1, f, k) for k in range(1, levels)] for f in (0, 2)]
            + [[(core, 1, f, 0)] for f in (0, 2)]
        )
    fronts, after = [], pieces[1][0]
    for got, where in zip(pieces, places):
        mixed = call(
            functools.partial(scale_kernel, where),
            shape(2 * slots, (4 * levels + 1) * HD),
            (idx, gain, *got, after),
            smem=1,
        )
        sums = call(
            functools.partial(first_kernel, where, heads),
            [shape(2 * slots, hidden_width, dtype=f32)] * 2,
            (idx, wg, wu, mixed),
            smem=1,
        )
        hidden = call(
            functools.partial(second_kernel, where, heads),
            shape(2 * slots, hidden_width),
            (idx, wg, wu, mixed, over_ctx(mixed, 1), *sums),
            smem=1,
        )
        fronts.append((hidden, over_tp(hidden)))
        after = hidden
    half = width // 2
    results, after, added = [], [fronts[1][0]], [fronts[1][1]]

    def down(flip, *args):
        return call(
            functools.partial(down_kernel, flip, PARTS),
            [shape(2 * slots, half // PARTS)] * PARTS,
            (idx, wd, *args),
            smem=1,
        )

    by_y = call(gather_kernel, shape(2, levels, tok, HD), (blocks[0][1], blocks[1][1], fronts[1][0]))
    keep_rows, send_rows = call(
        own_rows_kernel,
        [shape(2 * levels, tok, HD)] * 2,
        (idx, blocks[0][0], blocks[1][0], over_ctx(by_y, 2)),
        smem=1,
    )
    for core, (hidden, peer) in enumerate(fronts):
        pick, gates = hands[2 + core], hands[4 + core]
        other = [over_ctx(part, 1) for part in down(1, hidden, peer, *after)]
        half_out = down(0, hidden, peer)
        send = call(
            functools.partial(pair_kernel, PARTS), shape(slots, half), (idx, *half_out, *other, *added), smem=1
        )
        after = [send]
        got = over_ctx(send, 2)
        keep = call(
            functools.partial(weigh_kernel, PARTS),
            shape(span, half, dtype=f32),
            (idx, pick, gates, *half_out, *other),
            smem=1,
        )
        own, *sends = call(
            add_kernel,
            [shape(tok, half, dtype=f32)] + [shape(tok, half)] * (levels - 1),
            (idx, pick, gates, keep, got),
            smem=1,
            scratch=[pltpu.VMEM((span, half), f32)],
        )
        added = [own]
        summed = call(sum_kernel, shape(tok, half, dtype=f32), (own, *[along_z(s, k) for k, s in enumerate(sends, 1)]))
        results += [summed, to_core(summed, core)]
    return call(final_kernel, shape(tok, width), (idx, keep_rows, over_ctx(send_rows, 1), *results), smem=1)


def general(
    resid, query, key, value, norm_gain, routes, route_gates, segment_ids, w_gate, w_up, w_down
):
    tok_count = resid.shape[0]
    feat_width = resid.shape[1]
    head_count = feat_width // HD
    score_scale = 1.0 / math.sqrt(HD)
    query_pos = lax.axis_index("ctx") * tok_count + jnp.arange(tok_count, dtype=jnp.int32)
    key_segments = lax.all_gather(segment_ids, "ctx", axis=0, tiled=True)
    query_heads = query.reshape(tok_count, head_count, HD)
    start_sums = (
        jnp.zeros((tok_count, feat_width), jnp.float32),
        jnp.zeros((tok_count,), jnp.float32),
    )
    key_piece = lax.all_gather(key, "ctx", axis=0, tiled=True)
    value_piece = lax.all_gather(value, "ctx", axis=0, tiled=True)
    piece_len = key_piece.shape[0]
    block_len = math.gcd(piece_len, 512)
    block_count = piece_len // block_len
    key_blocks = key_piece.reshape(block_count, block_len, head_count, HD)
    value_blocks = value_piece.reshape(block_count, block_len, head_count, HD)

    def advance(state, inputs):
        key_block, value_block, block_id = inputs
        key_first = block_id * block_len

        def compute(current):
            acc_sum, key_total = current
            key_pos = key_first + jnp.arange(block_len, dtype=jnp.int32)
            key_segs = lax.dynamic_slice_in_dim(key_segments, key_first, block_len, 0)
            visible = jnp.logical_and(
                key_segs[None, :] == segment_ids[:, None], key_pos[None, :] <= query_pos[:, None]
            ).astype(jnp.float32)
            scores = (
                jnp.einsum(
                    "thd,shd->hts", query_heads, key_block, preferred_element_type=jnp.float32
                )
                * score_scale
            )
            weights = (jax.nn.silu(scores) * visible[None]).astype(jnp.bfloat16)
            summed = jnp.einsum(
                "hts,shd->thd", weights, value_block, preferred_element_type=jnp.float32
            )
            return (
                acc_sum + summed.reshape(tok_count, feat_width),
                key_total + jnp.sum(visible, axis=1),
            )

        last_key_seg = lax.dynamic_slice_in_dim(key_segments, key_first + block_len - 1, 1, 0)[0]
        reached = jnp.logical_and(key_first <= query_pos[-1], last_key_seg >= segment_ids[0])
        state = lax.cond(reached, compute, lambda current: current, state)
        return (state, None)

    block_ids = jnp.arange(block_count, dtype=jnp.int32)
    result, unused = lax.scan(advance, start_sums, (key_blocks, value_blocks, block_ids))
    acc_sum, key_total = result
    attended = acc_sum / jnp.sqrt(key_total)[:, None]
    hand_state = (resid.astype(jnp.float32) + attended).astype(jnp.bfloat16)
    hand_f32 = hand_state.astype(jnp.float32)
    square_sums = lax.psum(jnp.sum(hand_f32 * hand_f32, axis=1), ("tp", "sub"))
    normed = (
        hand_f32 * lax.rsqrt(square_sums / D + EPS)[:, None] * norm_gain.astype(jnp.float32)
    ).astype(jnp.bfloat16)
    ctx_count = lax.axis_size("ctx")
    expert_count = ctx_count // 2
    capacity = block_slots(ctx_count, tok_count)
    slot_total = expert_count * capacity
    recv_total = ctx_count * capacity
    flat_routes = routes.reshape(-1)
    onehot = (flat_routes[:, None] == jnp.arange(expert_count, dtype=jnp.int32)[None, :]).astype(
        jnp.int32
    )
    slot_rank = jnp.sum((jnp.cumsum(onehot, axis=0) - 1) * onehot, axis=1)
    slot_index = flat_routes * capacity + slot_rank
    position = jnp.arange(tok_count * TOPK, dtype=jnp.int32) // TOPK
    slot_source = jnp.full((slot_total,), tok_count, jnp.int32).at[slot_index].set(position)
    gate_local = w_gate[0]
    up_local = w_up[0]
    down_local = w_down[0]
    gathered = lax.all_gather(normed, ("tp", "sub"), axis=1, tiled=True)
    padded = jnp.concatenate([gathered, jnp.zeros((1, gathered.shape[1]), gathered.dtype)], axis=0)
    filled = padded[slot_source].reshape(expert_count, capacity, gathered.shape[1])
    arrived = lax.all_to_all(
        jnp.repeat(filled, 2, axis=0), "ctx", split_axis=0, concat_axis=0, tiled=True
    ).reshape(recv_total, gathered.shape[1])
    gate_sum = jnp.dot(arrived, gate_local, preferred_element_type=jnp.float32)
    up_sum = jnp.dot(arrived, up_local, preferred_element_type=jnp.float32)
    hidden = (jax.nn.silu(gate_sum) * up_sum).astype(jnp.bfloat16)
    down_rows_out = jnp.dot(
        lax.all_gather(hidden, ("tp", "sub"), axis=1, tiled=True),
        down_local,
        preferred_element_type=jnp.float32,
    ).astype(jnp.bfloat16)
    returned = lax.all_to_all(
        down_rows_out.reshape(ctx_count, capacity, feat_width),
        "ctx",
        split_axis=0,
        concat_axis=0,
        tiled=True,
    )
    combined = jnp.sum(
        returned.reshape(expert_count, 2, capacity, feat_width).astype(jnp.float32), axis=1
    ).reshape(slot_total, feat_width)
    picked = combined[slot_index].reshape(tok_count, TOPK, feat_width)
    mixed = hand_f32 + jnp.sum(route_gates[:, :, None] * picked, axis=1)
    return mixed.astype(jnp.bfloat16)


def block_slots(ctx, tok):
    return min(tok, max(2, tok * 10 // ctx))


def fits(mesh, resid):
    ctx, tp = mesh.shape["ctx"], mesh.shape["tp"]
    heads = resid.shape[1] // tp // HD
    tok = resid.shape[0] // mesh.shape["groups"] // ctx
    slots = ctx // 4 * block_slots(ctx, tok)
    whole = heads == ctx and 2 * tok == LANES and slots % 16 == 0
    return tp == 2 and mesh.shape["sub"] == 1 and whole and ctx >= 8 and ctx & (ctx - 1) == 0


def solution(mesh):
    placed = (
        P(("groups", "ctx"), ("tp", "sub")),
        P(("groups", "ctx"), ("tp", "sub")),
        P(("groups", "ctx"), ("tp", "sub")),
        P(("groups", "ctx"), ("tp", "sub")),
        P(("tp", "sub")),
        P(("groups", "ctx"), None),
        P(("groups", "ctx"), None),
        P(("groups", "ctx")),
        P("ctx", None, ("tp", "sub")),
        P("ctx", None, ("tp", "sub")),
        P("ctx", None, ("tp", "sub")),
    )

    def step(resid, *rest):
        per_device = heads_over_ctx if fits(mesh, resid) else general
        return jax.shard_map(
            per_device,
            mesh=mesh,
            in_specs=placed,
            out_specs=P(("groups", "ctx"), ("tp", "sub")),
            check_vma=False,
        )(resid, *rest)

    return step
```

```python
import functools
import math

import jax
import jax.numpy as jnp
from jax import lax
from jax.experimental import pallas as pl
from jax.experimental.pallas import tpu as pltpu
from jax.sharding import PartitionSpec as P

D = 4096
HD = 128
TOPK = 4
EPS = 1e-06
META = 16
LANES = 128
MIB = 1 << 20
PARTS = 4
GROUPS = (((0, 1, 2, 3, 4, 5),), ((0, 2, 4), (1, 3, 5)))


def silu(v):
    return v * (0.5 * jnp.tanh(0.5 * v) + 0.5)


def call(kernel, out_shape, args, smem=0, hbm=(), scratch=(), vmem=8, flops=0, moved=0):
    spaces = [pltpu.SMEM if n < smem else pltpu.HBM if n in hbm else pltpu.VMEM for n in range(len(args))]
    several = isinstance(out_shape, (tuple, list))
    out = pl.BlockSpec(memory_space=pltpu.VMEM)
    return pl.pallas_call(
        kernel,
        out_shape=out_shape,
        in_specs=[pl.BlockSpec(memory_space=space) for space in spaces],
        out_specs=tuple(out for _ in out_shape) if several else out,
        scratch_shapes=list(scratch),
        compiler_params=pltpu.CompilerParams(vmem_limit_bytes=vmem * MIB),
    )(*args)


def pack_kernel(seg_ref, route_ref, gate_ref, q_ref, k_ref, v_ref, r_ref, out_ref, held_ref, sems):
    heads, tok = out_ref.shape[0], q_ref.shape[0]
    copies = [pltpu.make_async_copy(ref, held_ref.at[n], sems.at[n]) for n, ref in enumerate((q_ref, k_ref, v_ref, r_ref))]
    for copy in copies:
        copy.start()
    row = lax.broadcasted_iota(jnp.int32, (META, tok), 0)
    seg = jnp.broadcast_to(seg_ref[...].astype(jnp.float32), (META, tok))
    parts = []
    for e in range(heads // 2):
        gate = jnp.sum(jnp.where(route_ref[...] == e, gate_ref[...], 0.0), axis=0, keepdims=True)
        gate = jnp.broadcast_to(gate, (META, tok))
        high = gate.astype(jnp.bfloat16).astype(jnp.float32)
        middle = (gate - high).astype(jnp.bfloat16).astype(jnp.float32)
        parts.append((high, middle, gate - high - middle))
    out_ref[:, 4 * tok :, :] = jnp.zeros((heads, META, HD), jnp.bfloat16)
    for h in range(heads):
        meta = jnp.where(row == 0, seg, 0.0)
        for n, piece in enumerate(parts[h // 2] + parts[h // 2 ^ 1], 1):
            meta = jnp.where(row == n, piece, meta)
        out_ref[h, 4 * tok :, 0:tok] = meta.astype(jnp.bfloat16)
    for n, copy in enumerate(copies):
        copy.wait()
        for h in range(heads):
            out_ref[h, n * tok : (n + 1) * tok, :] = held_ref[n, :, h * HD : (h + 1) * HD]


def attend_kernel(capacity, x_ref, even_ref, odd_ref, pick_even_ref, pick_odd_ref, gate_even_ref, gate_odd_ref):
    blocks = x_ref.shape[0]
    tok = LANES // 2
    levels = blocks // 4
    scale = 1.0 / math.sqrt(HD)
    lane = lax.broadcasted_iota(jnp.int32, (META, LANES), 1)
    row_at = lax.broadcasted_iota(jnp.int32, (LANES, LANES), 0)
    lane_at = lax.broadcasted_iota(jnp.int32, (LANES, LANES), 1)
    causal = lane_at <= row_at
    span = levels * tok
    slots = levels * capacity
    earlier_at = lax.broadcasted_iota(jnp.int32, (span, span), 0)
    later_at = lax.broadcasted_iota(jnp.int32, (span, span), 1)
    earlier = jnp.logical_and(earlier_at < later_at, earlier_at // tok == later_at // tok)
    earlier = earlier.astype(jnp.float32).astype(jnp.bfloat16)
    slot_at = lax.broadcasted_iota(jnp.int32, (slots, span), 0).astype(jnp.float32)
    base = (lax.broadcasted_iota(jnp.int32, (1, span), 1) // tok * capacity).astype(jnp.float32)

    def part(n, first, last):
        return x_ref[first:last, n * tok : (n + 1) * tok, :].reshape((last - first) * tok, HD)

    def scalars(first, second):
        left = x_ref[first, 4 * tok :, :].astype(jnp.float32)
        right = pltpu.roll(x_ref[second, 4 * tok :, :].astype(jnp.float32), tok, 1)
        return jnp.where(lane < tok, left, right)

    def gate_of(meta, which):
        first = 1 + 3 * which
        return meta[first : first + 1, :] + (meta[first + 1 : first + 2, :] + meta[first + 2 : first + 3, :])

    def down_rows(row):
        return jnp.transpose(jnp.broadcast_to(row, (LANES, LANES)))

    for y in range(2):
        for odd, (pick_ref, gate_ref) in enumerate(((pick_even_ref, gate_even_ref), (pick_odd_ref, gate_odd_ref))):
            metas = [scalars(4 * z + 2 * y + odd, 4 * z + 4 + 2 * y + odd) for z in range(0, levels, 2)]
            for which in range(2):
                rows = [gate_of(meta, which) for meta in metas]
                for n, row in enumerate(rows):
                    gate_ref[which, y * span + n * LANES : y * span + (n + 1) * LANES, :] = down_rows(row)
                named = (jnp.concatenate(rows, axis=1) > 0.0).astype(jnp.float32)
                rank = jnp.dot(
                    jnp.broadcast_to(named, (META, span)).astype(jnp.bfloat16),
                    earlier,
                    preferred_element_type=jnp.float32,
                )[0:1, :]
                target = jnp.broadcast_to(jnp.where(named > 0.0, base + rank, -1.0), (slots, span))
                pick = (slot_at == target).astype(jnp.float32).astype(jnp.bfloat16)
                pick_ref[which, y * slots : (y + 1) * slots, :] = pick

    seg_rows = []
    for i in range(blocks // 2):
        seg_rows.append(scalars(2 * i, 2 * i + 1)[0:1, :])
        seg_col = down_rows(seg_rows[i])
        masks = []
        for j in range(i + 1):
            same = seg_col == jnp.broadcast_to(seg_rows[j], (LANES, LANES))
            if j == i:
                same = jnp.logical_and(same, causal)
            masks.append(same.astype(jnp.float32))
        visible = jnp.concatenate(masks, axis=1)
        query = part(0, 2 * i, 2 * i + 2)
        keys = part(1, 0, 2 * i + 2)
        values = part(2, 0, 2 * i + 2)
        scores = (
            lax.dot_general(query, keys, (((1,), (1,)), ((), ())), preferred_element_type=jnp.float32) * scale
        )
        weights = (silu(scores) * visible).astype(jnp.bfloat16)
        summed = jnp.dot(weights, values, preferred_element_type=jnp.float32)
        counted = jnp.sum(visible, axis=1, keepdims=True)
        hand = (part(3, 2 * i, 2 * i + 2).astype(jnp.float32) + summed / jnp.sqrt(counted)).astype(jnp.bfloat16)
        at = (i % 2 * levels + i // 2) * tok
        even_ref[at : at + tok, :] = hand[:tok, :]
        odd_ref[at : at + tok, :] = hand[tok:, :]


def near_kernel(pick_even_ref, pick_odd_ref, even_ref, odd_ref, mine_ref, theirs_ref):
    slots, span = pick_even_ref.shape[1] // 2, pick_even_ref.shape[2]
    for n, (pick_ref, ref) in enumerate(((pick_even_ref, even_ref), (pick_odd_ref, odd_ref))):
        for group in range(2):
            here = slice(group * slots, (group + 1) * slots)
            block = ref[group * span : (group + 1) * span, :]
            for which, out_ref in enumerate((mine_ref, theirs_ref)):
                rows = jnp.dot(pick_ref[which, here, :], block, preferred_element_type=jnp.float32)
                out_ref[n, here, :] = rows.astype(jnp.bfloat16)


def compact_kernel(idx_ref, pick_ref, *refs):
    *out_refs, mine_own_ref, theirs_own_ref = refs[-4:]
    me = idx_ref[0]
    levels, tok = mine_own_ref.shape[:2]
    pieces = refs[:levels]
    slots, span = pick_ref.shape[1] // 2, pick_ref.shape[2]
    z, y = lax.div(me, 4), lax.rem(lax.div(me, 2), 2)
    for group in range(2):
        block = jnp.concatenate([p[group * span : (group + 1) * span, :] for p in pieces], axis=1)
        for which, out_ref in enumerate(out_refs):
            here = slice(group * slots, (group + 1) * slots)
            rows = jnp.dot(pick_ref[which, here, :], block, preferred_element_type=jnp.float32).astype(jnp.bfloat16)
            for k in range(levels):
                out_ref[k, here, :] = rows[:, k * HD : (k + 1) * HD]
    for which, out_ref in enumerate((mine_own_ref, theirs_own_ref)):
        own = pl.ds(pl.multiple_of(((y ^ which) * levels + z) * tok, tok), tok)
        for k in range(levels):
            out_ref[k, :, :] = pieces[k][own, :]


def gather_kernel(*refs):
    out_ref = refs[-1]
    for n in range(out_ref.shape[0]):
        out_ref[n] = refs[n][...]


def own_rows_kernel(idx_ref, even_ref, odd_ref, by_y_ref, keep_ref, send_ref):
    core = lax.rem(idx_ref[0], 2)
    levels = even_ref.shape[0]
    for n, ref in enumerate((even_ref, odd_ref)):
        for same, out_ref in ((True, keep_ref), (False, send_ref)):
            @pl.when((core == n) == same)
            def _(ref=ref, out_ref=out_ref, n=n):
                out_ref[:levels] = ref[...]
                out_ref[levels:] = by_y_ref[n]


def thirds(value):
    high = value.astype(jnp.bfloat16)
    rest = value - high.astype(jnp.float32)
    middle = rest.astype(jnp.bfloat16)
    return high, middle, (rest - middle.astype(jnp.float32)).astype(jnp.bfloat16)


def scale_kernel(places, idx_ref, gain_ref, *refs):
    pieces, out_ref = refs[: len(places)], refs[-1]
    me = idx_ref[0]
    heads = gain_ref.shape[1] // HD
    rows = out_ref.shape[0]
    width = sum(map(len, places)) * HD
    tile = rows // 2
    for r in range(rows // tile):
        here = slice(r * tile, (r + 1) * tile)
        squares = jnp.zeros((tile, HD), jnp.float32)
        n = 0
        for ref, entries in zip(pieces, places):
            for k, other, low, back in entries:
                head = lax.rem((me ^ low) + heads - 4 * back, heads)
                gain = gain_ref[other : other + 1, pl.ds(pl.multiple_of(head * HD, HD), HD)]
                v = ref[k, here, :].astype(jnp.float32)
                squares = squares + v * v
                out_ref[here, n : n + HD] = (v * gain).astype(jnp.bfloat16)
                n += HD
        lane = lax.broadcasted_iota(jnp.int32, (tile, HD), 1)
        high, middle, low = thirds(jnp.broadcast_to(jnp.sum(squares, axis=1, keepdims=True), (tile, HD)))
        parts = jnp.where(lane == 0, high, jnp.where(lane == 1, middle, jnp.where(lane == 2, low, 0)))
        out_ref[here, width:] = parts.astype(jnp.bfloat16)


def row_offsets(places, heads, me, plane, flip):
    found = []
    for _, other, low, back in (entry for entries in places for entry in entries):
        head = lax.rem((me ^ low ^ flip) + heads - 4 * back, heads)
        found.append(pl.multiple_of(((plane ^ other) * heads + head) * HD, HD))
    return found


def half_projection(lhs, offsets, weight_ref, cols):
    weights = jnp.concatenate([weight_ref[pl.ds(at, HD), cols] for at in offsets], axis=0)
    return jnp.dot(lhs, weights, preferred_element_type=jnp.float32)


def project_kernel(places, heads, flip, idx_ref, wg_ref, wu_ref, lhs_ref, *refs):
    *before, gate_ref, up_ref = refs
    rows = gate_ref.shape[0]
    offsets = row_offsets(places, heads, idx_ref[0], idx_ref[1], flip)
    width = min(256, wg_ref.shape[1])
    for n in range(wg_ref.shape[1] // width):
        cols = slice(n * width, (n + 1) * width)
        lhs = lhs_ref[0:rows, 0 : len(offsets) * HD]
        for m, (weight_ref, out_ref) in enumerate(((wg_ref, gate_ref), (wu_ref, up_ref))):
            total = half_projection(lhs, offsets, weight_ref, cols)
            out_ref[:, cols] = before[m][:, cols] + total if before else total


def hidden_kernel(places, heads, idx_ref, wg_ref, wu_ref, gate_ref, up_ref, lhs_ref, *refs):
    hidden_ref = refs[-1]
    rows = gate_ref.shape[0]
    offsets = row_offsets(places, heads, idx_ref[0], idx_ref[1], 1)
    squares = jnp.zeros((rows, HD), jnp.float32)
    for ref in (lhs_ref, *refs[:-1]):
        squares = squares + ref[:, ref.shape[1] - HD :].astype(jnp.float32)
    scale = lax.rsqrt(jnp.sum(squares, axis=1, keepdims=True) / D + EPS)
    width = min(256, wg_ref.shape[1])
    for n in range(wg_ref.shape[1] // width):
        cols = slice(n * width, (n + 1) * width)
        lhs = lhs_ref[0:rows, 0 : len(offsets) * HD]
        gate = (gate_ref[:, cols] + half_projection(lhs, offsets, wg_ref, cols)) * scale
        up = (up_ref[:, cols] + half_projection(lhs, offsets, wu_ref, cols)) * scale
        hidden_ref[:, cols] = (silu(gate) * up).astype(jnp.bfloat16)


def down_kernel(flip, parts, idx_ref, wd_ref, own_ref, peer_ref, *refs):
    out_refs = refs[-parts:]
    core, plane = lax.rem(idx_ref[0], 2), idx_ref[1]
    depth, width = own_ref.shape[1], out_refs[0].shape[1]
    total_width = parts * width
    first = (core ^ flip) * total_width
    own_rows = pl.ds(pl.multiple_of(plane * depth, depth), depth)
    peer_rows = pl.ds(pl.multiple_of((1 - plane) * depth, depth), depth)
    for n, out_ref in enumerate(out_refs):
        cols = pl.ds(pl.multiple_of(first + n * width, width), width)
        total = jnp.dot(own_ref[...], wd_ref[own_rows, cols], preferred_element_type=jnp.float32)
        total = total + jnp.dot(peer_ref[...], wd_ref[peer_rows, cols], preferred_element_type=jnp.float32)
        out_ref[...] = total.astype(jnp.bfloat16)


def pair_kernel(parts, idx_ref, *refs):
    send_ref = refs[-1]
    slots = send_ref.shape[0]
    y = lax.rem(lax.div(idx_ref[0], 2), 2)
    theirs = pl.ds(pl.multiple_of((1 - y) * slots, slots), slots)
    width = refs[0].shape[1]
    for n in range(parts):
        both = refs[n][theirs, :].astype(jnp.float32) + refs[parts + n][theirs, :].astype(jnp.float32)
        send_ref[:, n * width : (n + 1) * width] = both.astype(jnp.bfloat16)


def spread(pick, rows):
    return lax.dot_general(pick, rows, (((0,), (0,)), ((), ())), preferred_element_type=jnp.float32)


def weigh_kernel(parts, idx_ref, pick_ref, gate_ref, *refs):
    slots, span = pick_ref.shape[1] // 2, pick_ref.shape[2]
    y = lax.rem(lax.div(idx_ref[0], 2), 2)
    mine = pl.ds(pl.multiple_of(y * slots, slots), slots)
    gate = gate_ref[0, pl.ds(pl.multiple_of(y * span, span), span), :]
    pick = pick_ref[0, mine, :]
    width = refs[0].shape[1]
    for n in range(parts):
        cols = slice(n * width, (n + 1) * width)
        total = spread(pick, refs[n][mine, :]) + spread(pick, refs[parts + n][mine, :])
        refs[-1][:, cols] = total * jnp.concatenate([gate] * (width // LANES), axis=1)


def add_kernel(idx_ref, pick_ref, gate_ref, keep_ref, got_ref, own_ref, *refs):
    send_refs, total_ref = refs[:-1], refs[-1]
    slots, span = pick_ref.shape[1] // 2, pick_ref.shape[2]
    tok = own_ref.shape[0]
    z, y = lax.div(idx_ref[0], 4), lax.rem(lax.div(idx_ref[0], 2), 2)
    gate = gate_ref[1, pl.ds(pl.multiple_of(y * span, span), span), :]
    pick = pick_ref[1, pl.ds(pl.multiple_of(y * slots, slots), slots), :]
    width = 4 * LANES
    for n in range(got_ref.shape[1] // width):
        cols = slice(n * width, (n + 1) * width)
        more = spread(pick, got_ref[:, cols]) * jnp.concatenate([gate] * (width // LANES), axis=1)
        total_ref[:, cols] = keep_ref[:, cols] + more
    own_ref[...] = total_ref[pl.ds(pl.multiple_of(z * tok, tok), tok), :]
    for k, ref in enumerate(send_refs, 1):
        there = lax.rem(z + k, len(send_refs) + 1)
        ref[...] = total_ref[pl.ds(pl.multiple_of(there * tok, tok), tok), :].astype(jnp.bfloat16)


def sum_kernel(own_ref, *refs):
    total = own_ref[...]
    for ref in refs[:-1]:
        total = total + ref[...].astype(jnp.float32)
    refs[-1][...] = total.astype(refs[-1].dtype)


def final_kernel(idx_ref, *refs):
    hand_refs, sum_refs, out_ref = refs[:2], refs[2:-1], refs[-1]
    me = idx_ref[0]
    core = lax.rem(me, 2)
    levels = hand_refs[0].shape[0] // 2
    heads = out_ref.shape[1] // HD
    for n in range(2):
        own_ref, other_ref = sum_refs[2 * n : 2 * n + 2]
        half = own_ref.shape[1]

        @pl.when(core == n)
        def _(halves=(own_ref, other_ref) if n == 0 else (other_ref, own_ref)):
            for flip, hand_ref in enumerate(hand_refs):
                for low in range(2):
                    for back in range(levels):
                        head = lax.rem((me ^ (2 * low) ^ flip) + heads - 4 * back, heads)
                        hand = hand_ref[low * levels + back].astype(jnp.float32)
                        at = pl.multiple_of(head * HD, HD)
                        inside = pl.multiple_of(lax.rem(head, heads // 2) * HD, HD)
                        first = halves[0][:, pl.ds(inside, HD)].astype(jnp.float32)
                        second = halves[1][:, pl.ds(inside, HD)].astype(jnp.float32)
                        total = hand + jnp.where(head < heads // 2, first, second)
                        out_ref[:, pl.ds(at, HD)] = total.astype(jnp.bfloat16)


def heads_over_ctx(
    resid, query, key, value, norm_gain, routes, route_gates, segment_ids, w_gate, w_up, w_down
):
    ctx = lax.axis_size("ctx")
    heads, tok, width = ctx, resid.shape[0], resid.shape[1]
    levels = ctx // 4
    bf16, f32 = jnp.bfloat16, jnp.float32
    rows = ctx // 2 * tok
    span, slots = levels * tok, levels * block_slots(ctx, tok)
    me, plane = lax.axis_index("ctx"), lax.axis_index("tp")
    idx = jnp.stack([me, plane]).astype(jnp.int32)

    def shape(*dims, dtype=bf16):
        return jax.ShapeDtypeStruct(dims, dtype)

    def over_ctx(x, mask, core=None):
        return lax.ppermute(x, "ctx", [(c, c ^ mask) for c in range(ctx) if core is None or c % 2 == core])

    def along_z(x, steps):
        return lax.ppermute(x, "ctx", [(c, (c + 4 * steps) % ctx) for c in range(ctx)])

    def over_tp(x):
        return lax.ppermute(x, "tp", [(0, 1), (1, 0)])

    def across(x):
        pairs = [(2 * c + t, 2 * (c ^ 2) + (t ^ 1)) for c in range(ctx) for t in range(2)]
        return lax.ppermute(x, ("ctx", "tp"), pairs)

    def to_core(x, core):
        return lax.ppermute(x, "ctx", [(c, c ^ 1) for c in range(ctx) if c % 2 != core])

    packed = call(
        pack_kernel,
        shape(ctx, 4 * tok + META, HD),
        (segment_ids[None, :], routes.T, route_gates.T, query, key, value, resid),
        hbm=(3, 4, 5, 6),
        scratch=[pltpu.VMEM((4, tok, width), bf16), pltpu.SemaphoreType.DMA((4,))],
        vmem=60,
    )
    gain = over_tp(norm_gain)
    arrived = lax.all_to_all(packed, "ctx", split_axis=0, concat_axis=0, tiled=True)
    wg, wu, wd = w_gate[0], w_up[0], w_down[0]
    hidden_width = wg.shape[1]
    arrived, gain = lax.optimization_barrier((arrived, gain))
    gain = jnp.stack([norm_gain, gain]).astype(f32)
    hands = call(
        functools.partial(attend_kernel, block_slots(ctx, tok)),
        [shape(rows, HD)] * 2 + [shape(2, 2 * slots, span)] * 2 + [shape(2, 2 * span, LANES, dtype=f32)] * 2,
        (arrived,),
    )
    half = width // 2
    columns = []
    for hand in hands[:2]:
        if columns:
            hand, columns[0][1] = lax.optimization_barrier((hand, columns[0][1]))
        columns.append([hand] + [along_z(hand, k) for k in range(1, levels)])
    near = call(near_kernel, [shape(2, 2 * slots, HD)] * 2, (*hands[2:4], *hands[:2]))
    near = [over_tp(near[0]), across(near[1])]
    pieces, places, blocks, compacted = [], [], [], near
    for core, (pick, column) in enumerate(zip(hands[2:4], columns)):
        mine, theirs, *own_rows = call(
            compact_kernel,
            [shape(levels, 2 * slots, HD)] * 2 + [shape(levels, tok, HD)] * 2,
            (idx, pick, *column, *compacted),
            smem=1,
        )
        blocks.append(own_rows)
        far = [over_tp(mine[1:]), across(theirs[1:])]
        pieces.append([mine, over_ctx(theirs, 2), *far, *near])
        compacted = pieces[0][1:4]
        places.append(
            [[(k, 0, f, k) for k in range(levels)] for f in (0, 2)]
            + [[(k - 1, 1, f, k) for k in range(1, levels)] for f in (0, 2)]
            + [[(core, 1, f, 0)] for f in (0, 2)]
        )
    fronts, after = [], pieces[1][0]
    for groups, got, where in zip(GROUPS, pieces, places):
        sums, swapped = [], []
        for group in groups:
            chosen = [where[n] for n in group]
            mixed = call(
                functools.partial(scale_kernel, chosen),
                shape(2 * slots, (sum(map(len, chosen)) + 1) * HD),
                (idx, gain, *[got[n] for n in group], after),
                smem=1,
            )
            sums = call(
                functools.partial(project_kernel, chosen, heads, 0),
                [shape(2 * slots, hidden_width, dtype=f32)] * 2,
                (idx, wg, wu, mixed, *sums),
                smem=1,
            )
            other = over_ctx(mixed, 1)
            swapped += [mixed, other]
            if group is not groups[-1]:
                sums = call(
                    functools.partial(project_kernel, chosen, heads, 1),
                    [shape(2 * slots, hidden_width, dtype=f32)] * 2,
                    (idx, wg, wu, other, *sums),
                    smem=1,
                )
        hidden = call(
            functools.partial(hidden_kernel, chosen, heads),
            shape(2 * slots, hidden_width),
            (idx, wg, wu, *sums, swapped[-1], *swapped[:-1]),
            smem=1,
        )
        fronts.append((hidden, over_tp(hidden)))
        after = hidden
    half = width // 2
    results, after, added = [], [fronts[1][0]], [fronts[1][1]]

    def down(flip, *args):
        return call(
            functools.partial(down_kernel, flip, PARTS),
            [shape(2 * slots, half // PARTS)] * PARTS,
            (idx, wd, *args),
            smem=1,
        )

    by_y = call(gather_kernel, shape(2, levels, tok, HD), (blocks[0][1], blocks[1][1], fronts[1][0]))
    keep_rows, send_rows = call(
        own_rows_kernel,
        [shape(2 * levels, tok, HD)] * 2,
        (idx, blocks[0][0], blocks[1][0], over_ctx(by_y, 2)),
        smem=1,
    )
    for core, (hidden, peer) in enumerate(fronts):
        pick, gates = hands[2 + core], hands[4 + core]
        other = [over_ctx(part, 1) for part in down(1, hidden, peer, *after)]
        half_out = down(0, hidden, peer)
        send = call(
            functools.partial(pair_kernel, PARTS), shape(slots, half), (idx, *half_out, *other, *added), smem=1
        )
        after = [send]
        got = over_ctx(send, 2)
        keep = call(
            functools.partial(weigh_kernel, PARTS),
            shape(span, half, dtype=f32),
            (idx, pick, gates, *half_out, *other),
            smem=1,
        )
        own, *sends = call(
            add_kernel,
            [shape(tok, half, dtype=f32)] + [shape(tok, half)] * (levels - 1),
            (idx, pick, gates, keep, got),
            smem=1,
            scratch=[pltpu.VMEM((span, half), f32)],
        )
        added = [own]
        summed = call(sum_kernel, shape(tok, half, dtype=f32), (own, *[along_z(s, k) for k, s in enumerate(sends, 1)]))
        results += [summed, to_core(summed, core)]
    return call(final_kernel, shape(tok, width), (idx, keep_rows, over_ctx(send_rows, 1), *results), smem=1)


def general(
    resid, query, key, value, norm_gain, routes, route_gates, segment_ids, w_gate, w_up, w_down
):
    tok_count = resid.shape[0]
    feat_width = resid.shape[1]
    head_count = feat_width // HD
    score_scale = 1.0 / math.sqrt(HD)
    query_pos = lax.axis_index("ctx") * tok_count + jnp.arange(tok_count, dtype=jnp.int32)
    key_segments = lax.all_gather(segment_ids, "ctx", axis=0, tiled=True)
    query_heads = query.reshape(tok_count, head_count, HD)
    start_sums = (
        jnp.zeros((tok_count, feat_width), jnp.float32),
        jnp.zeros((tok_count,), jnp.float32),
    )
    key_piece = lax.all_gather(key, "ctx", axis=0, tiled=True)
    value_piece = lax.all_gather(value, "ctx", axis=0, tiled=True)
    piece_len = key_piece.shape[0]
    block_len = math.gcd(piece_len, 512)
    block_count = piece_len // block_len
    key_blocks = key_piece.reshape(block_count, block_len, head_count, HD)
    value_blocks = value_piece.reshape(block_count, block_len, head_count, HD)

    def advance(state, inputs):
        key_block, value_block, block_id = inputs
        key_first = block_id * block_len

        def compute(current):
            acc_sum, key_total = current
            key_pos = key_first + jnp.arange(block_len, dtype=jnp.int32)
            key_segs = lax.dynamic_slice_in_dim(key_segments, key_first, block_len, 0)
            visible = jnp.logical_and(
                key_segs[None, :] == segment_ids[:, None], key_pos[None, :] <= query_pos[:, None]
            ).astype(jnp.float32)
            scores = (
                jnp.einsum(
                    "thd,shd->hts", query_heads, key_block, preferred_element_type=jnp.float32
                )
                * score_scale
            )
            weights = (jax.nn.silu(scores) * visible[None]).astype(jnp.bfloat16)
            summed = jnp.einsum(
                "hts,shd->thd", weights, value_block, preferred_element_type=jnp.float32
            )
            return (
                acc_sum + summed.reshape(tok_count, feat_width),
                key_total + jnp.sum(visible, axis=1),
            )

        last_key_seg = lax.dynamic_slice_in_dim(key_segments, key_first + block_len - 1, 1, 0)[0]
        reached = jnp.logical_and(key_first <= query_pos[-1], last_key_seg >= segment_ids[0])
        state = lax.cond(reached, compute, lambda current: current, state)
        return (state, None)

    block_ids = jnp.arange(block_count, dtype=jnp.int32)
    result, unused = lax.scan(advance, start_sums, (key_blocks, value_blocks, block_ids))
    acc_sum, key_total = result
    attended = acc_sum / jnp.sqrt(key_total)[:, None]
    hand_state = (resid.astype(jnp.float32) + attended).astype(jnp.bfloat16)
    hand_f32 = hand_state.astype(jnp.float32)
    square_sums = lax.psum(jnp.sum(hand_f32 * hand_f32, axis=1), ("tp", "sub"))
    normed = (
        hand_f32 * lax.rsqrt(square_sums / D + EPS)[:, None] * norm_gain.astype(jnp.float32)
    ).astype(jnp.bfloat16)
    ctx_count = lax.axis_size("ctx")
    expert_count = ctx_count // 2
    capacity = block_slots(ctx_count, tok_count)
    slot_total = expert_count * capacity
    recv_total = ctx_count * capacity
    flat_routes = routes.reshape(-1)
    onehot = (flat_routes[:, None] == jnp.arange(expert_count, dtype=jnp.int32)[None, :]).astype(
        jnp.int32
    )
    slot_rank = jnp.sum((jnp.cumsum(onehot, axis=0) - 1) * onehot, axis=1)
    slot_index = flat_routes * capacity + slot_rank
    position = jnp.arange(tok_count * TOPK, dtype=jnp.int32) // TOPK
    slot_source = jnp.full((slot_total,), tok_count, jnp.int32).at[slot_index].set(position)
    gate_local = w_gate[0]
    up_local = w_up[0]
    down_local = w_down[0]
    gathered = lax.all_gather(normed, ("tp", "sub"), axis=1, tiled=True)
    padded = jnp.concatenate([gathered, jnp.zeros((1, gathered.shape[1]), gathered.dtype)], axis=0)
    filled = padded[slot_source].reshape(expert_count, capacity, gathered.shape[1])
    arrived = lax.all_to_all(
        jnp.repeat(filled, 2, axis=0), "ctx", split_axis=0, concat_axis=0, tiled=True
    ).reshape(recv_total, gathered.shape[1])
    gate_sum = jnp.dot(arrived, gate_local, preferred_element_type=jnp.float32)
    up_sum = jnp.dot(arrived, up_local, preferred_element_type=jnp.float32)
    hidden = (jax.nn.silu(gate_sum) * up_sum).astype(jnp.bfloat16)
    down_rows_out = jnp.dot(
        lax.all_gather(hidden, ("tp", "sub"), axis=1, tiled=True),
        down_local,
        preferred_element_type=jnp.float32,
    ).astype(jnp.bfloat16)
    returned = lax.all_to_all(
        down_rows_out.reshape(ctx_count, capacity, feat_width),
        "ctx",
        split_axis=0,
        concat_axis=0,
        tiled=True,
    )
    combined = jnp.sum(
        returned.reshape(expert_count, 2, capacity, feat_width).astype(jnp.float32), axis=1
    ).reshape(slot_total, feat_width)
    picked = combined[slot_index].reshape(tok_count, TOPK, feat_width)
    mixed = hand_f32 + jnp.sum(route_gates[:, :, None] * picked, axis=1)
    return mixed.astype(jnp.bfloat16)


def block_slots(ctx, tok):
    return min(tok, max(2, tok * 10 // ctx))


def fits(mesh, resid):
    ctx, tp = mesh.shape["ctx"], mesh.shape["tp"]
    heads = resid.shape[1] // tp // HD
    tok = resid.shape[0] // mesh.shape["groups"] // ctx
    slots = ctx // 4 * block_slots(ctx, tok)
    whole = heads == ctx and 2 * tok == LANES and slots % 16 == 0
    return tp == 2 and mesh.shape["sub"] == 1 and whole and ctx >= 8 and ctx & (ctx - 1) == 0


def solution(mesh):
    placed = (
        P(("groups", "ctx"), ("tp", "sub")),
        P(("groups", "ctx"), ("tp", "sub")),
        P(("groups", "ctx"), ("tp", "sub")),
        P(("groups", "ctx"), ("tp", "sub")),
        P(("tp", "sub")),
        P(("groups", "ctx"), None),
        P(("groups", "ctx"), None),
        P(("groups", "ctx")),
        P("ctx", None, ("tp", "sub")),
        P("ctx", None, ("tp", "sub")),
        P("ctx", None, ("tp", "sub")),
    )

    def step(resid, *rest):
        per_device = heads_over_ctx if fits(mesh, resid) else general
        return jax.shard_map(
            per_device,
            mesh=mesh,
            in_specs=placed,
            out_specs=P(("groups", "ctx"), ("tp", "sub")),
            check_vma=False,
        )(resid, *rest)

    return step
```

```python
import functools
import math

import jax
import jax.numpy as jnp
from jax import lax
from jax.experimental import pallas as pl
from jax.experimental.pallas import tpu as pltpu
from jax.sharding import PartitionSpec as P

D = 4096
HD = 128
TOPK = 4
EPS = 1e-06
META = 16
LANES = 128
MIB = 1 << 20
PARTS = 4
GROUPS = (((0, 1, 2, 3, 4, 5, 6),), ((0, 2, 4), (1, 3, 5, 6)))


def silu(v):
    return v * (0.5 * jnp.tanh(0.5 * v) + 0.5)


def call(kernel, out_shape, args, smem=0, hbm=(), scratch=(), vmem=8, flops=0, moved=0):
    spaces = [pltpu.SMEM if n < smem else pltpu.HBM if n in hbm else pltpu.VMEM for n in range(len(args))]
    several = isinstance(out_shape, (tuple, list))
    out = pl.BlockSpec(memory_space=pltpu.VMEM)
    return pl.pallas_call(
        kernel,
        out_shape=out_shape,
        in_specs=[pl.BlockSpec(memory_space=space) for space in spaces],
        out_specs=tuple(out for _ in out_shape) if several else out,
        scratch_shapes=list(scratch),
        compiler_params=pltpu.CompilerParams(vmem_limit_bytes=vmem * MIB),
    )(*args)


def pack_kernel(seg_ref, route_ref, gate_ref, q_ref, k_ref, v_ref, r_ref, out_ref, held_ref, sems):
    heads, tok = out_ref.shape[0], q_ref.shape[0]
    copies = [pltpu.make_async_copy(ref, held_ref.at[n], sems.at[n]) for n, ref in enumerate((q_ref, k_ref, v_ref, r_ref))]
    for copy in copies:
        copy.start()
    row = lax.broadcasted_iota(jnp.int32, (META, tok), 0)
    seg = jnp.broadcast_to(seg_ref[...].astype(jnp.float32), (META, tok))
    parts = []
    for e in range(heads // 2):
        gate = jnp.sum(jnp.where(route_ref[...] == e, gate_ref[...], 0.0), axis=0, keepdims=True)
        gate = jnp.broadcast_to(gate, (META, tok))
        high = gate.astype(jnp.bfloat16).astype(jnp.float32)
        middle = (gate - high).astype(jnp.bfloat16).astype(jnp.float32)
        parts.append((high, middle, gate - high - middle))
    out_ref[:, 4 * tok :, :] = jnp.zeros((heads, META, HD), jnp.bfloat16)
    for h in range(heads):
        meta = jnp.where(row == 0, seg, 0.0)
        for n, piece in enumerate(parts[h // 2] + parts[h // 2 ^ 1], 1):
            meta = jnp.where(row == n, piece, meta)
        out_ref[h, 4 * tok :, 0:tok] = meta.astype(jnp.bfloat16)
    for n, copy in enumerate(copies):
        copy.wait()
        for h in range(heads):
            out_ref[h, n * tok : (n + 1) * tok, :] = held_ref[n, :, h * HD : (h + 1) * HD]


def attend_kernel(capacity, x_ref, even_ref, odd_ref, pick_even_ref, pick_odd_ref, gate_even_ref, gate_odd_ref):
    blocks = x_ref.shape[0]
    tok = LANES // 2
    levels = blocks // 4
    scale = 1.0 / math.sqrt(HD)
    lane = lax.broadcasted_iota(jnp.int32, (META, LANES), 1)
    row_at = lax.broadcasted_iota(jnp.int32, (LANES, LANES), 0)
    lane_at = lax.broadcasted_iota(jnp.int32, (LANES, LANES), 1)
    causal = lane_at <= row_at
    span = levels * tok
    slots = levels * capacity
    earlier_at = lax.broadcasted_iota(jnp.int32, (span, span), 0)
    later_at = lax.broadcasted_iota(jnp.int32, (span, span), 1)
    earlier = jnp.logical_and(earlier_at < later_at, earlier_at // tok == later_at // tok)
    earlier = earlier.astype(jnp.float32).astype(jnp.bfloat16)
    slot_at = lax.broadcasted_iota(jnp.int32, (slots, span), 0).astype(jnp.float32)
    base = (lax.broadcasted_iota(jnp.int32, (1, span), 1) // tok * capacity).astype(jnp.float32)

    def part(n, first, last):
        return x_ref[first:last, n * tok : (n + 1) * tok, :].reshape((last - first) * tok, HD)

    def scalars(first, second):
        left = x_ref[first, 4 * tok :, :].astype(jnp.float32)
        right = pltpu.roll(x_ref[second, 4 * tok :, :].astype(jnp.float32), tok, 1)
        return jnp.where(lane < tok, left, right)

    def gate_of(meta, which):
        first = 1 + 3 * which
        return meta[first : first + 1, :] + (meta[first + 1 : first + 2, :] + meta[first + 2 : first + 3, :])

    def down_rows(row):
        return jnp.transpose(jnp.broadcast_to(row, (LANES, LANES)))

    for y in range(2):
        for odd, (pick_ref, gate_ref) in enumerate(((pick_even_ref, gate_even_ref), (pick_odd_ref, gate_odd_ref))):
            metas = [scalars(4 * z + 2 * y + odd, 4 * z + 4 + 2 * y + odd) for z in range(0, levels, 2)]
            for which in range(2):
                rows = [gate_of(meta, which) for meta in metas]
                for n, row in enumerate(rows):
                    gate_ref[which, y * span + n * LANES : y * span + (n + 1) * LANES, :] = down_rows(row)
                named = (jnp.concatenate(rows, axis=1) > 0.0).astype(jnp.float32)
                rank = jnp.dot(
                    jnp.broadcast_to(named, (META, span)).astype(jnp.bfloat16),
                    earlier,
                    preferred_element_type=jnp.float32,
                )[0:1, :]
                target = jnp.broadcast_to(jnp.where(named > 0.0, base + rank, -1.0), (slots, span))
                pick = (slot_at == target).astype(jnp.float32).astype(jnp.bfloat16)
                pick_ref[which, y * slots : (y + 1) * slots, :] = pick

    seg_rows = []
    for i in range(blocks // 2):
        seg_rows.append(scalars(2 * i, 2 * i + 1)[0:1, :])
        seg_col = down_rows(seg_rows[i])
        masks = []
        for j in range(i + 1):
            same = seg_col == jnp.broadcast_to(seg_rows[j], (LANES, LANES))
            if j == i:
                same = jnp.logical_and(same, causal)
            masks.append(same.astype(jnp.float32))
        visible = jnp.concatenate(masks, axis=1)
        query = part(0, 2 * i, 2 * i + 2)
        keys = part(1, 0, 2 * i + 2)
        values = part(2, 0, 2 * i + 2)
        scores = (
            lax.dot_general(query, keys, (((1,), (1,)), ((), ())), preferred_element_type=jnp.float32) * scale
        )
        weights = (silu(scores) * visible).astype(jnp.bfloat16)
        summed = jnp.dot(weights, values, preferred_element_type=jnp.float32)
        counted = jnp.sum(visible, axis=1, keepdims=True)
        hand = (part(3, 2 * i, 2 * i + 2).astype(jnp.float32) + summed / jnp.sqrt(counted)).astype(jnp.bfloat16)
        at = (i % 2 * levels + i // 2) * tok
        even_ref[at : at + tok, :] = hand[:tok, :]
        odd_ref[at : at + tok, :] = hand[tok:, :]


def near_kernel(pick_even_ref, pick_odd_ref, even_ref, odd_ref, mine_ref, theirs_ref):
    slots, span = pick_even_ref.shape[1] // 2, pick_even_ref.shape[2]
    for n, (pick_ref, ref) in enumerate(((pick_even_ref, even_ref), (pick_odd_ref, odd_ref))):
        for group in range(2):
            here = slice(group * slots, (group + 1) * slots)
            block = ref[group * span : (group + 1) * span, :]
            for which, out_ref in enumerate((mine_ref, theirs_ref)):
                rows = jnp.dot(pick_ref[which, here, :], block, preferred_element_type=jnp.float32)
                out_ref[n, here, :] = rows.astype(jnp.bfloat16)


def compact_kernel(idx_ref, pick_ref, *refs):
    *out_refs, mine_own_ref, theirs_own_ref = refs[-4:]
    me = idx_ref[0]
    levels, tok = mine_own_ref.shape[:2]
    pieces = refs[:levels]
    slots, span = pick_ref.shape[1] // 2, pick_ref.shape[2]
    z, y = lax.div(me, 4), lax.rem(lax.div(me, 2), 2)
    for group in range(2):
        block = jnp.concatenate([p[group * span : (group + 1) * span, :] for p in pieces], axis=1)
        for which, out_ref in enumerate(out_refs):
            here = slice(group * slots, (group + 1) * slots)
            rows = jnp.dot(pick_ref[which, here, :], block, preferred_element_type=jnp.float32).astype(jnp.bfloat16)
            for k in range(levels):
                out_ref[k, here, :] = rows[:, k * HD : (k + 1) * HD]
    for which, out_ref in enumerate((mine_own_ref, theirs_own_ref)):
        own = pl.ds(pl.multiple_of(((y ^ which) * levels + z) * tok, tok), tok)
        for k in range(levels):
            out_ref[k, :, :] = pieces[k][own, :]


def gather_kernel(*refs):
    out_ref = refs[-1]
    for n in range(out_ref.shape[0]):
        out_ref[n] = refs[n][...]


def own_rows_kernel(idx_ref, even_ref, odd_ref, by_y_ref, keep_ref, send_ref):
    core = lax.rem(idx_ref[0], 2)
    levels = even_ref.shape[0]
    for n, ref in enumerate((even_ref, odd_ref)):
        for same, out_ref in ((True, keep_ref), (False, send_ref)):
            @pl.when((core == n) == same)
            def _(ref=ref, out_ref=out_ref, n=n):
                out_ref[:levels] = ref[...]
                out_ref[levels:] = by_y_ref[n]


def thirds(value):
    high = value.astype(jnp.bfloat16)
    rest = value - high.astype(jnp.float32)
    middle = rest.astype(jnp.bfloat16)
    return high, middle, (rest - middle.astype(jnp.float32)).astype(jnp.bfloat16)


def scale_kernel(places, idx_ref, gain_ref, *refs):
    pieces, out_ref = refs[: len(places)], refs[-1]
    me = idx_ref[0]
    heads = gain_ref.shape[1] // HD
    rows = out_ref.shape[0]
    width = sum(map(len, places)) * HD
    tile = rows // 2
    for r in range(rows // tile):
        here = slice(r * tile, (r + 1) * tile)
        squares = jnp.zeros((tile, HD), jnp.float32)
        n = 0
        for ref, entries in zip(pieces, places):
            for k, other, low, back in entries:
                head = lax.rem((me ^ low) + heads - 4 * back, heads)
                gain = gain_ref[other : other + 1, pl.ds(pl.multiple_of(head * HD, HD), HD)]
                v = ref[k, here, :].astype(jnp.float32)
                squares = squares + v * v
                out_ref[here, n : n + HD] = (v * gain).astype(jnp.bfloat16)
                n += HD
        lane = lax.broadcasted_iota(jnp.int32, (tile, HD), 1)
        high, middle, low = thirds(jnp.broadcast_to(jnp.sum(squares, axis=1, keepdims=True), (tile, HD)))
        parts = jnp.where(lane == 0, high, jnp.where(lane == 1, middle, jnp.where(lane == 2, low, 0)))
        out_ref[here, width:] = parts.astype(jnp.bfloat16)


def row_offsets(places, heads, me, plane, flip):
    found = []
    for _, other, low, back in (entry for entries in places for entry in entries):
        head = lax.rem((me ^ low ^ flip) + heads - 4 * back, heads)
        found.append(pl.multiple_of(((plane ^ other) * heads + head) * HD, HD))
    return found


def half_projection(lhs, offsets, weight_ref, cols):
    weights = jnp.concatenate([weight_ref[pl.ds(at, HD), cols] for at in offsets], axis=0)
    return jnp.dot(lhs, weights, preferred_element_type=jnp.float32)


def project_kernel(places, heads, flip, idx_ref, wg_ref, wu_ref, lhs_ref, *refs):
    *before, gate_ref, up_ref = refs
    rows = gate_ref.shape[0]
    offsets = row_offsets(places, heads, idx_ref[0], idx_ref[1], flip)
    width = min(256, wg_ref.shape[1])
    for n in range(wg_ref.shape[1] // width):
        cols = slice(n * width, (n + 1) * width)
        lhs = lhs_ref[0:rows, 0 : len(offsets) * HD]
        for m, (weight_ref, out_ref) in enumerate(((wg_ref, gate_ref), (wu_ref, up_ref))):
            total = half_projection(lhs, offsets, weight_ref, cols)
            out_ref[:, cols] = before[m][:, cols] + total if before else total


def hidden_kernel(places, heads, idx_ref, wg_ref, wu_ref, gate_ref, up_ref, lhs_ref, *refs):
    hidden_ref = refs[-1]
    rows = gate_ref.shape[0]
    offsets = row_offsets(places, heads, idx_ref[0], idx_ref[1], 1)
    squares = jnp.zeros((rows, HD), jnp.float32)
    for ref in (lhs_ref, *refs[:-1]):
        squares = squares + ref[:, ref.shape[1] - HD :].astype(jnp.float32)
    scale = lax.rsqrt(jnp.sum(squares, axis=1, keepdims=True) / D + EPS)
    width = min(256, wg_ref.shape[1])
    for n in range(wg_ref.shape[1] // width):
        cols = slice(n * width, (n + 1) * width)
        lhs = lhs_ref[0:rows, 0 : len(offsets) * HD]
        gate = (gate_ref[:, cols] + half_projection(lhs, offsets, wg_ref, cols)) * scale
        up = (up_ref[:, cols] + half_projection(lhs, offsets, wu_ref, cols)) * scale
        hidden_ref[:, cols] = (silu(gate) * up).astype(jnp.bfloat16)


def down_kernel(flip, parts, idx_ref, wd_ref, own_ref, peer_ref, *refs):
    out_refs = refs[-parts:]
    core, plane = lax.rem(idx_ref[0], 2), idx_ref[1]
    depth, width = own_ref.shape[1], out_refs[0].shape[1]
    total_width = parts * width
    first = (core ^ flip) * total_width
    own_rows = pl.ds(pl.multiple_of(plane * depth, depth), depth)
    peer_rows = pl.ds(pl.multiple_of((1 - plane) * depth, depth), depth)
    for n, out_ref in enumerate(out_refs):
        cols = pl.ds(pl.multiple_of(first + n * width, width), width)
        total = jnp.dot(own_ref[...], wd_ref[own_rows, cols], preferred_element_type=jnp.float32)
        total = total + jnp.dot(peer_ref[...], wd_ref[peer_rows, cols], preferred_element_type=jnp.float32)
        out_ref[...] = total.astype(jnp.bfloat16)


def pair_kernel(parts, idx_ref, *refs):
    send_ref = refs[-1]
    slots = send_ref.shape[0]
    y = lax.rem(lax.div(idx_ref[0], 2), 2)
    theirs = pl.ds(pl.multiple_of((1 - y) * slots, slots), slots)
    width = refs[0].shape[1]
    for n in range(parts):
        both = refs[n][theirs, :].astype(jnp.float32) + refs[parts + n][theirs, :].astype(jnp.float32)
        send_ref[:, n * width : (n + 1) * width] = both.astype(jnp.bfloat16)


def spread(pick, rows):
    return lax.dot_general(pick, rows, (((0,), (0,)), ((), ())), preferred_element_type=jnp.float32)


def weigh_kernel(parts, idx_ref, pick_ref, gate_ref, *refs):
    slots, span = pick_ref.shape[1] // 2, pick_ref.shape[2]
    y = lax.rem(lax.div(idx_ref[0], 2), 2)
    mine = pl.ds(pl.multiple_of(y * slots, slots), slots)
    gate = gate_ref[0, pl.ds(pl.multiple_of(y * span, span), span), :]
    pick = pick_ref[0, mine, :]
    width = refs[0].shape[1]
    for n in range(parts):
        cols = slice(n * width, (n + 1) * width)
        total = spread(pick, refs[n][mine, :]) + spread(pick, refs[parts + n][mine, :])
        refs[-1][:, cols] = total * jnp.concatenate([gate] * (width // LANES), axis=1)


def add_kernel(idx_ref, pick_ref, gate_ref, keep_ref, got_ref, own_ref, *refs):
    send_refs, total_ref = refs[:-1], refs[-1]
    slots, span = pick_ref.shape[1] // 2, pick_ref.shape[2]
    tok = own_ref.shape[0]
    z, y = lax.div(idx_ref[0], 4), lax.rem(lax.div(idx_ref[0], 2), 2)
    gate = gate_ref[1, pl.ds(pl.multiple_of(y * span, span), span), :]
    pick = pick_ref[1, pl.ds(pl.multiple_of(y * slots, slots), slots), :]
    width = 4 * LANES
    for n in range(got_ref.shape[1] // width):
        cols = slice(n * width, (n + 1) * width)
        more = spread(pick, got_ref[:, cols]) * jnp.concatenate([gate] * (width // LANES), axis=1)
        total_ref[:, cols] = keep_ref[:, cols] + more
    own_ref[...] = total_ref[pl.ds(pl.multiple_of(z * tok, tok), tok), :]
    for k, ref in enumerate(send_refs, 1):
        there = lax.rem(z + k, len(send_refs) + 1)
        ref[...] = total_ref[pl.ds(pl.multiple_of(there * tok, tok), tok), :].astype(jnp.bfloat16)


def sum_kernel(own_ref, *refs):
    total = own_ref[...]
    for ref in refs[:-1]:
        total = total + ref[...].astype(jnp.float32)
    refs[-1][...] = total.astype(refs[-1].dtype)


def final_kernel(idx_ref, *refs):
    hand_refs, sum_refs, out_ref = refs[:2], refs[2:-1], refs[-1]
    me = idx_ref[0]
    core = lax.rem(me, 2)
    levels = hand_refs[0].shape[0] // 2
    heads = out_ref.shape[1] // HD
    for n in range(2):
        own_ref, other_ref = sum_refs[2 * n : 2 * n + 2]
        half = own_ref.shape[1]

        @pl.when(core == n)
        def _(halves=(own_ref, other_ref) if n == 0 else (other_ref, own_ref)):
            for flip, hand_ref in enumerate(hand_refs):
                for low in range(2):
                    for back in range(levels):
                        head = lax.rem((me ^ (2 * low) ^ flip) + heads - 4 * back, heads)
                        hand = hand_ref[low * levels + back].astype(jnp.float32)
                        at = pl.multiple_of(head * HD, HD)
                        inside = pl.multiple_of(lax.rem(head, heads // 2) * HD, HD)
                        first = halves[0][:, pl.ds(inside, HD)].astype(jnp.float32)
                        second = halves[1][:, pl.ds(inside, HD)].astype(jnp.float32)
                        total = hand + jnp.where(head < heads // 2, first, second)
                        out_ref[:, pl.ds(at, HD)] = total.astype(jnp.bfloat16)


def heads_over_ctx(
    resid, query, key, value, norm_gain, routes, route_gates, segment_ids, w_gate, w_up, w_down
):
    ctx = lax.axis_size("ctx")
    heads, tok, width = ctx, resid.shape[0], resid.shape[1]
    levels = ctx // 4
    bf16, f32 = jnp.bfloat16, jnp.float32
    rows = ctx // 2 * tok
    span, slots = levels * tok, levels * block_slots(ctx, tok)
    me, plane = lax.axis_index("ctx"), lax.axis_index("tp")
    idx = jnp.stack([me, plane]).astype(jnp.int32)

    def shape(*dims, dtype=bf16):
        return jax.ShapeDtypeStruct(dims, dtype)

    def over_ctx(x, mask, core=None):
        return lax.ppermute(x, "ctx", [(c, c ^ mask) for c in range(ctx) if core is None or c % 2 == core])

    def along_z(x, steps):
        return lax.ppermute(x, "ctx", [(c, (c + 4 * steps) % ctx) for c in range(ctx)])

    def over_tp(x):
        return lax.ppermute(x, "tp", [(0, 1), (1, 0)])

    def across(x):
        pairs = [(2 * c + t, 2 * (c ^ 2) + (t ^ 1)) for c in range(ctx) for t in range(2)]
        return lax.ppermute(x, ("ctx", "tp"), pairs)

    def to_core(x, core):
        return lax.ppermute(x, "ctx", [(c, c ^ 1) for c in range(ctx) if c % 2 != core])

    packed = call(
        pack_kernel,
        shape(ctx, 4 * tok + META, HD),
        (segment_ids[None, :], routes.T, route_gates.T, query, key, value, resid),
        hbm=(3, 4, 5, 6),
        scratch=[pltpu.VMEM((4, tok, width), bf16), pltpu.SemaphoreType.DMA((4,))],
        vmem=60,
    )
    gain = over_tp(norm_gain)
    arrived = lax.all_to_all(packed, "ctx", split_axis=0, concat_axis=0, tiled=True)
    wg, wu, wd = w_gate[0], w_up[0], w_down[0]
    hidden_width = wg.shape[1]
    arrived, gain = lax.optimization_barrier((arrived, gain))
    gain = jnp.stack([norm_gain, gain]).astype(f32)
    hands = call(
        functools.partial(attend_kernel, block_slots(ctx, tok)),
        [shape(rows, HD)] * 2 + [shape(2, 2 * slots, span)] * 2 + [shape(2, 2 * span, LANES, dtype=f32)] * 2,
        (arrived,),
    )
    half = width // 2
    columns = []
    for hand in hands[:2]:
        if columns:
            hand, columns[0][1] = lax.optimization_barrier((hand, columns[0][1]))
        columns.append([hand] + [along_z(hand, k) for k in range(1, levels)])
    near = call(near_kernel, [shape(2, 2 * slots, HD)] * 2, (*hands[2:4], *hands[:2]))
    near = [over_tp(near[0]), across(near[1]), over_ctx(near[1], 2)]
    pieces, places, blocks, compacted = [], [], [], near
    for core, (pick, column) in enumerate(zip(hands[2:4], columns)):
        mine, theirs, *own_rows = call(
            compact_kernel,
            [shape(levels, 2 * slots, HD)] * 2 + [shape(levels, tok, HD)] * 2,
            (idx, pick, *column, *compacted),
            smem=1,
        )
        blocks.append(own_rows)
        far = [over_tp(mine[1:]), across(theirs[1:])]
        pieces.append([mine, over_ctx(theirs[1:], 2), *far, *near])
        compacted = pieces[0][1:4]
        places.append(
            [[(k, 0, 0, k) for k in range(levels)]]
            + [[(k - 1, t, f, k) for k in range(1, levels)] for t, f in ((0, 2), (1, 0), (1, 2))]
            + [[(core, t, f, 0)] for t, f in ((1, 0), (1, 2), (0, 2))]
        )
    fronts, after = [], pieces[1][0]
    for groups, got, where in zip(GROUPS, pieces, places):
        sums, swapped = [], []
        for group in groups:
            chosen = [where[n] for n in group]
            mixed = call(
                functools.partial(scale_kernel, chosen),
                shape(2 * slots, (sum(map(len, chosen)) + 1) * HD),
                (idx, gain, *[got[n] for n in group], after),
                smem=1,
            )
            sums = call(
                functools.partial(project_kernel, chosen, heads, 0),
                [shape(2 * slots, hidden_width, dtype=f32)] * 2,
                (idx, wg, wu, mixed, *sums),
                smem=1,
            )
            other = over_ctx(mixed, 1)
            swapped += [mixed, other]
            if group is not groups[-1]:
                sums = call(
                    functools.partial(project_kernel, chosen, heads, 1),
                    [shape(2 * slots, hidden_width, dtype=f32)] * 2,
                    (idx, wg, wu, other, *sums),
                    smem=1,
                )
        hidden = call(
            functools.partial(hidden_kernel, chosen, heads),
            shape(2 * slots, hidden_width),
            (idx, wg, wu, *sums, swapped[-1], *swapped[:-1]),
            smem=1,
        )
        fronts.append((hidden, over_tp(hidden)))
        after = hidden
    half = width // 2
    results, after, added = [], [fronts[1][0]], [fronts[1][1]]

    def down(flip, *args):
        return call(
            functools.partial(down_kernel, flip, PARTS),
            [shape(2 * slots, half // PARTS)] * PARTS,
            (idx, wd, *args),
            smem=1,
        )

    by_y = call(gather_kernel, shape(2, levels, tok, HD), (blocks[0][1], blocks[1][1], fronts[1][0]))
    keep_rows, send_rows = call(
        own_rows_kernel,
        [shape(2 * levels, tok, HD)] * 2,
        (idx, blocks[0][0], blocks[1][0], over_ctx(by_y, 2)),
        smem=1,
    )
    for core, (hidden, peer) in enumerate(fronts):
        pick, gates = hands[2 + core], hands[4 + core]
        other = [over_ctx(part, 1) for part in down(1, hidden, peer, *after)]
        half_out = down(0, hidden, peer)
        send = call(
            functools.partial(pair_kernel, PARTS), shape(slots, half), (idx, *half_out, *other, *added), smem=1
        )
        after = [send]
        got = over_ctx(send, 2)
        keep = call(
            functools.partial(weigh_kernel, PARTS),
            shape(span, half, dtype=f32),
            (idx, pick, gates, *half_out, *other),
            smem=1,
        )
        own, *sends = call(
            add_kernel,
            [shape(tok, half, dtype=f32)] + [shape(tok, half)] * (levels - 1),
            (idx, pick, gates, keep, got),
            smem=1,
            scratch=[pltpu.VMEM((span, half), f32)],
        )
        added = [own]
        summed = call(sum_kernel, shape(tok, half, dtype=f32), (own, *[along_z(s, k) for k, s in enumerate(sends, 1)]))
        results += [summed, to_core(summed, core)]
    return call(final_kernel, shape(tok, width), (idx, keep_rows, over_ctx(send_rows, 1), *results), smem=1)


def general(
    resid, query, key, value, norm_gain, routes, route_gates, segment_ids, w_gate, w_up, w_down
):
    tok_count = resid.shape[0]
    feat_width = resid.shape[1]
    head_count = feat_width // HD
    score_scale = 1.0 / math.sqrt(HD)
    query_pos = lax.axis_index("ctx") * tok_count + jnp.arange(tok_count, dtype=jnp.int32)
    key_segments = lax.all_gather(segment_ids, "ctx", axis=0, tiled=True)
    query_heads = query.reshape(tok_count, head_count, HD)
    start_sums = (
        jnp.zeros((tok_count, feat_width), jnp.float32),
        jnp.zeros((tok_count,), jnp.float32),
    )
    key_piece = lax.all_gather(key, "ctx", axis=0, tiled=True)
    value_piece = lax.all_gather(value, "ctx", axis=0, tiled=True)
    piece_len = key_piece.shape[0]
    block_len = math.gcd(piece_len, 512)
    block_count = piece_len // block_len
    key_blocks = key_piece.reshape(block_count, block_len, head_count, HD)
    value_blocks = value_piece.reshape(block_count, block_len, head_count, HD)

    def advance(state, inputs):
        key_block, value_block, block_id = inputs
        key_first = block_id * block_len

        def compute(current):
            acc_sum, key_total = current
            key_pos = key_first + jnp.arange(block_len, dtype=jnp.int32)
            key_segs = lax.dynamic_slice_in_dim(key_segments, key_first, block_len, 0)
            visible = jnp.logical_and(
                key_segs[None, :] == segment_ids[:, None], key_pos[None, :] <= query_pos[:, None]
            ).astype(jnp.float32)
            scores = (
                jnp.einsum(
                    "thd,shd->hts", query_heads, key_block, preferred_element_type=jnp.float32
                )
                * score_scale
            )
            weights = (jax.nn.silu(scores) * visible[None]).astype(jnp.bfloat16)
            summed = jnp.einsum(
                "hts,shd->thd", weights, value_block, preferred_element_type=jnp.float32
            )
            return (
                acc_sum + summed.reshape(tok_count, feat_width),
                key_total + jnp.sum(visible, axis=1),
            )

        last_key_seg = lax.dynamic_slice_in_dim(key_segments, key_first + block_len - 1, 1, 0)[0]
        reached = jnp.logical_and(key_first <= query_pos[-1], last_key_seg >= segment_ids[0])
        state = lax.cond(reached, compute, lambda current: current, state)
        return (state, None)

    block_ids = jnp.arange(block_count, dtype=jnp.int32)
    result, unused = lax.scan(advance, start_sums, (key_blocks, value_blocks, block_ids))
    acc_sum, key_total = result
    attended = acc_sum / jnp.sqrt(key_total)[:, None]
    hand_state = (resid.astype(jnp.float32) + attended).astype(jnp.bfloat16)
    hand_f32 = hand_state.astype(jnp.float32)
    square_sums = lax.psum(jnp.sum(hand_f32 * hand_f32, axis=1), ("tp", "sub"))
    normed = (
        hand_f32 * lax.rsqrt(square_sums / D + EPS)[:, None] * norm_gain.astype(jnp.float32)
    ).astype(jnp.bfloat16)
    ctx_count = lax.axis_size("ctx")
    expert_count = ctx_count // 2
    capacity = block_slots(ctx_count, tok_count)
    slot_total = expert_count * capacity
    recv_total = ctx_count * capacity
    flat_routes = routes.reshape(-1)
    onehot = (flat_routes[:, None] == jnp.arange(expert_count, dtype=jnp.int32)[None, :]).astype(
        jnp.int32
    )
    slot_rank = jnp.sum((jnp.cumsum(onehot, axis=0) - 1) * onehot, axis=1)
    slot_index = flat_routes * capacity + slot_rank
    position = jnp.arange(tok_count * TOPK, dtype=jnp.int32) // TOPK
    slot_source = jnp.full((slot_total,), tok_count, jnp.int32).at[slot_index].set(position)
    gate_local = w_gate[0]
    up_local = w_up[0]
    down_local = w_down[0]
    gathered = lax.all_gather(normed, ("tp", "sub"), axis=1, tiled=True)
    padded = jnp.concatenate([gathered, jnp.zeros((1, gathered.shape[1]), gathered.dtype)], axis=0)
    filled = padded[slot_source].reshape(expert_count, capacity, gathered.shape[1])
    arrived = lax.all_to_all(
        jnp.repeat(filled, 2, axis=0), "ctx", split_axis=0, concat_axis=0, tiled=True
    ).reshape(recv_total, gathered.shape[1])
    gate_sum = jnp.dot(arrived, gate_local, preferred_element_type=jnp.float32)
    up_sum = jnp.dot(arrived, up_local, preferred_element_type=jnp.float32)
    hidden = (jax.nn.silu(gate_sum) * up_sum).astype(jnp.bfloat16)
    down_rows_out = jnp.dot(
        lax.all_gather(hidden, ("tp", "sub"), axis=1, tiled=True),
        down_local,
        preferred_element_type=jnp.float32,
    ).astype(jnp.bfloat16)
    returned = lax.all_to_all(
        down_rows_out.reshape(ctx_count, capacity, feat_width),
        "ctx",
        split_axis=0,
        concat_axis=0,
        tiled=True,
    )
    combined = jnp.sum(
        returned.reshape(expert_count, 2, capacity, feat_width).astype(jnp.float32), axis=1
    ).reshape(slot_total, feat_width)
    picked = combined[slot_index].reshape(tok_count, TOPK, feat_width)
    mixed = hand_f32 + jnp.sum(route_gates[:, :, None] * picked, axis=1)
    return mixed.astype(jnp.bfloat16)


def block_slots(ctx, tok):
    return min(tok, max(2, tok * 10 // ctx))


def fits(mesh, resid):
    ctx, tp = mesh.shape["ctx"], mesh.shape["tp"]
    heads = resid.shape[1] // tp // HD
    tok = resid.shape[0] // mesh.shape["groups"] // ctx
    slots = ctx // 4 * block_slots(ctx, tok)
    whole = heads == ctx and 2 * tok == LANES and slots % 16 == 0
    return tp == 2 and mesh.shape["sub"] == 1 and whole and ctx >= 8 and ctx & (ctx - 1) == 0


def solution(mesh):
    placed = (
        P(("groups", "ctx"), ("tp", "sub")),
        P(("groups", "ctx"), ("tp", "sub")),
        P(("groups", "ctx"), ("tp", "sub")),
        P(("groups", "ctx"), ("tp", "sub")),
        P(("tp", "sub")),
        P(("groups", "ctx"), None),
        P(("groups", "ctx"), None),
        P(("groups", "ctx")),
        P("ctx", None, ("tp", "sub")),
        P("ctx", None, ("tp", "sub")),
        P("ctx", None, ("tp", "sub")),
    )

    def step(resid, *rest):
        per_device = heads_over_ctx if fits(mesh, resid) else general
        return jax.shard_map(
            per_device,
            mesh=mesh,
            in_specs=placed,
            out_specs=P(("groups", "ctx"), ("tp", "sub")),
            check_vma=False,
        )(resid, *rest)

    return step
```

```python
import functools
import math

import jax
import jax.numpy as jnp
from jax import lax
from jax.experimental import pallas as pl
from jax.experimental.pallas import tpu as pltpu
from jax.sharding import PartitionSpec as P

D = 4096
HD = 128
TOPK = 4
EPS = 1e-06
META = 16
LANES = 128
MIB = 1 << 20
PARTS = 4
GROUPS = (((0, 1, 2, 3, 4, 5, 6),), ((0, 1, 2, 3, 4, 5, 6),))


def silu(v):
    return v * (0.5 * jnp.tanh(0.5 * v) + 0.5)


def call(kernel, out_shape, args, smem=0, hbm=(), scratch=(), vmem=8, flops=0, moved=0):
    spaces = [pltpu.SMEM if n < smem else pltpu.HBM if n in hbm else pltpu.VMEM for n in range(len(args))]
    several = isinstance(out_shape, (tuple, list))
    out = pl.BlockSpec(memory_space=pltpu.VMEM)
    return pl.pallas_call(
        kernel,
        out_shape=out_shape,
        in_specs=[pl.BlockSpec(memory_space=space) for space in spaces],
        out_specs=tuple(out for _ in out_shape) if several else out,
        scratch_shapes=list(scratch),
        compiler_params=pltpu.CompilerParams(vmem_limit_bytes=vmem * MIB),
    )(*args)


def pack_kernel(seg_ref, route_ref, gate_ref, q_ref, k_ref, v_ref, r_ref, out_ref, held_ref, sems):
    heads, tok = out_ref.shape[0], q_ref.shape[0]
    copies = [pltpu.make_async_copy(ref, held_ref.at[n], sems.at[n]) for n, ref in enumerate((q_ref, k_ref, v_ref, r_ref))]
    for copy in copies:
        copy.start()
    row = lax.broadcasted_iota(jnp.int32, (META, tok), 0)
    seg = jnp.broadcast_to(seg_ref[...].astype(jnp.float32), (META, tok))
    parts = []
    for e in range(heads // 2):
        gate = jnp.sum(jnp.where(route_ref[...] == e, gate_ref[...], 0.0), axis=0, keepdims=True)
        gate = jnp.broadcast_to(gate, (META, tok))
        high = gate.astype(jnp.bfloat16).astype(jnp.float32)
        middle = (gate - high).astype(jnp.bfloat16).astype(jnp.float32)
        parts.append((high, middle, gate - high - middle))
    out_ref[:, 4 * tok :, :] = jnp.zeros((heads, META, HD), jnp.bfloat16)
    for h in range(heads):
        meta = jnp.where(row == 0, seg, 0.0)
        for n, piece in enumerate(parts[h // 2] + parts[h // 2 ^ 1], 1):
            meta = jnp.where(row == n, piece, meta)
        out_ref[h, 4 * tok :, 0:tok] = meta.astype(jnp.bfloat16)
    for n, copy in enumerate(copies):
        copy.wait()
        for h in range(heads):
            out_ref[h, n * tok : (n + 1) * tok, :] = held_ref[n, :, h * HD : (h + 1) * HD]


def attend_kernel(capacity, x_ref, even_ref, odd_ref, pick_even_ref, pick_odd_ref, gate_even_ref, gate_odd_ref):
    blocks = x_ref.shape[0]
    tok = LANES // 2
    levels = blocks // 4
    scale = 1.0 / math.sqrt(HD)
    lane = lax.broadcasted_iota(jnp.int32, (META, LANES), 1)
    row_at = lax.broadcasted_iota(jnp.int32, (LANES, LANES), 0)
    lane_at = lax.broadcasted_iota(jnp.int32, (LANES, LANES), 1)
    causal = lane_at <= row_at
    span = levels * tok
    slots = levels * capacity
    earlier_at = lax.broadcasted_iota(jnp.int32, (span, span), 0)
    later_at = lax.broadcasted_iota(jnp.int32, (span, span), 1)
    earlier = jnp.logical_and(earlier_at < later_at, earlier_at // tok == later_at // tok)
    earlier = earlier.astype(jnp.float32).astype(jnp.bfloat16)
    slot_at = lax.broadcasted_iota(jnp.int32, (slots, span), 0).astype(jnp.float32)
    base = (lax.broadcasted_iota(jnp.int32, (1, span), 1) // tok * capacity).astype(jnp.float32)

    def part(n, first, last):
        return x_ref[first:last, n * tok : (n + 1) * tok, :].reshape((last - first) * tok, HD)

    def scalars(first, second):
        left = x_ref[first, 4 * tok :, :].astype(jnp.float32)
        right = pltpu.roll(x_ref[second, 4 * tok :, :].astype(jnp.float32), tok, 1)
        return jnp.where(lane < tok, left, right)

    def gate_of(meta, which):
        first = 1 + 3 * which
        return meta[first : first + 1, :] + (meta[first + 1 : first + 2, :] + meta[first + 2 : first + 3, :])

    def down_rows(row):
        return jnp.transpose(jnp.broadcast_to(row, (LANES, LANES)))

    for y in range(2):
        for odd, (pick_ref, gate_ref) in enumerate(((pick_even_ref, gate_even_ref), (pick_odd_ref, gate_odd_ref))):
            metas = [scalars(4 * z + 2 * y + odd, 4 * z + 4 + 2 * y + odd) for z in range(0, levels, 2)]
            for which in range(2):
                rows = [gate_of(meta, which) for meta in metas]
                for n, row in enumerate(rows):
                    gate_ref[which, y * span + n * LANES : y * span + (n + 1) * LANES, :] = down_rows(row)
                named = (jnp.concatenate(rows, axis=1) > 0.0).astype(jnp.float32)
                rank = jnp.dot(
                    jnp.broadcast_to(named, (META, span)).astype(jnp.bfloat16),
                    earlier,
                    preferred_element_type=jnp.float32,
                )[0:1, :]
                target = jnp.broadcast_to(jnp.where(named > 0.0, base + rank, -1.0), (slots, span))
                pick = (slot_at == target).astype(jnp.float32).astype(jnp.bfloat16)
                pick_ref[which, y * slots : (y + 1) * slots, :] = pick

    seg_rows = []
    for i in range(blocks // 2):
        seg_rows.append(scalars(2 * i, 2 * i + 1)[0:1, :])
        seg_col = down_rows(seg_rows[i])
        masks = []
        for j in range(i + 1):
            same = seg_col == jnp.broadcast_to(seg_rows[j], (LANES, LANES))
            if j == i:
                same = jnp.logical_and(same, causal)
            masks.append(same.astype(jnp.float32))
        visible = jnp.concatenate(masks, axis=1)
        query = part(0, 2 * i, 2 * i + 2)
        keys = part(1, 0, 2 * i + 2)
        values = part(2, 0, 2 * i + 2)
        scores = (
            lax.dot_general(query, keys, (((1,), (1,)), ((), ())), preferred_element_type=jnp.float32) * scale
        )
        weights = (silu(scores) * visible).astype(jnp.bfloat16)
        summed = jnp.dot(weights, values, preferred_element_type=jnp.float32)
        counted = jnp.sum(visible, axis=1, keepdims=True)
        hand = (part(3, 2 * i, 2 * i + 2).astype(jnp.float32) + summed / jnp.sqrt(counted)).astype(jnp.bfloat16)
        at = (i % 2 * levels + i // 2) * tok
        even_ref[at : at + tok, :] = hand[:tok, :]
        odd_ref[at : at + tok, :] = hand[tok:, :]


def near_kernel(pick_even_ref, pick_odd_ref, even_ref, odd_ref, mine_ref, theirs_ref):
    slots, span = pick_even_ref.shape[1] // 2, pick_even_ref.shape[2]
    for n, (pick_ref, ref) in enumerate(((pick_even_ref, even_ref), (pick_odd_ref, odd_ref))):
        for group in range(2):
            here = slice(group * slots, (group + 1) * slots)
            block = ref[group * span : (group + 1) * span, :]
            for which, out_ref in enumerate((mine_ref, theirs_ref)):
                rows = jnp.dot(pick_ref[which, here, :], block, preferred_element_type=jnp.float32)
                out_ref[n, here, :] = rows.astype(jnp.bfloat16)


def compact_kernel(idx_ref, pick_ref, *refs):
    *out_refs, mine_own_ref, theirs_own_ref = refs[-4:]
    me = idx_ref[0]
    levels, tok = mine_own_ref.shape[:2]
    pieces = refs[:levels]
    slots, span = pick_ref.shape[1] // 2, pick_ref.shape[2]
    z, y = lax.div(me, 4), lax.rem(lax.div(me, 2), 2)
    for group in range(2):
        block = jnp.concatenate([p[group * span : (group + 1) * span, :] for p in pieces], axis=1)
        for which, out_ref in enumerate(out_refs):
            here = slice(group * slots, (group + 1) * slots)
            rows = jnp.dot(pick_ref[which, here, :], block, preferred_element_type=jnp.float32).astype(jnp.bfloat16)
            for k in range(levels):
                out_ref[k, here, :] = rows[:, k * HD : (k + 1) * HD]
    for which, out_ref in enumerate((mine_own_ref, theirs_own_ref)):
        own = pl.ds(pl.multiple_of(((y ^ which) * levels + z) * tok, tok), tok)
        for k in range(levels):
            out_ref[k, :, :] = pieces[k][own, :]


def gather_kernel(*refs):
    out_ref = refs[-1]
    for n in range(out_ref.shape[0]):
        out_ref[n] = refs[n][...]


def own_rows_kernel(idx_ref, even_ref, odd_ref, by_y_ref, keep_ref, send_ref):
    core = lax.rem(idx_ref[0], 2)
    levels = even_ref.shape[0]
    for n, ref in enumerate((even_ref, odd_ref)):
        for same, out_ref in ((True, keep_ref), (False, send_ref)):
            @pl.when((core == n) == same)
            def _(ref=ref, out_ref=out_ref, n=n):
                out_ref[:levels] = ref[...]
                out_ref[levels:] = by_y_ref[n]


def thirds(value):
    high = value.astype(jnp.bfloat16)
    rest = value - high.astype(jnp.float32)
    middle = rest.astype(jnp.bfloat16)
    return high, middle, (rest - middle.astype(jnp.float32)).astype(jnp.bfloat16)


def scale_kernel(places, idx_ref, gain_ref, *refs):
    pieces, out_ref = refs[: len(places)], refs[-1]
    me = idx_ref[0]
    heads = gain_ref.shape[1] // HD
    rows = out_ref.shape[0]
    width = sum(map(len, places)) * HD
    tile = rows // 2
    for r in range(rows // tile):
        here = slice(r * tile, (r + 1) * tile)
        squares = jnp.zeros((tile, HD), jnp.float32)
        n = 0
        for ref, entries in zip(pieces, places):
            for k, other, low, back in entries:
                head = lax.rem((me ^ low) + heads - 4 * back, heads)
                gain = gain_ref[other : other + 1, pl.ds(pl.multiple_of(head * HD, HD), HD)]
                v = ref[k, here, :].astype(jnp.float32)
                squares = squares + v * v
                out_ref[here, n : n + HD] = (v * gain).astype(jnp.bfloat16)
                n += HD
        lane = lax.broadcasted_iota(jnp.int32, (tile, HD), 1)
        high, middle, low = thirds(jnp.broadcast_to(jnp.sum(squares, axis=1, keepdims=True), (tile, HD)))
        parts = jnp.where(lane == 0, high, jnp.where(lane == 1, middle, jnp.where(lane == 2, low, 0)))
        out_ref[here, width:] = parts.astype(jnp.bfloat16)


def row_offsets(places, heads, me, plane, flip):
    found = []
    for _, other, low, back in (entry for entries in places for entry in entries):
        head = lax.rem((me ^ low ^ flip) + heads - 4 * back, heads)
        found.append(pl.multiple_of(((plane ^ other) * heads + head) * HD, HD))
    return found


def half_projection(lhs, offsets, weight_ref, cols):
    weights = jnp.concatenate([weight_ref[pl.ds(at, HD), cols] for at in offsets], axis=0)
    return jnp.dot(lhs, weights, preferred_element_type=jnp.float32)


def project_kernel(places, heads, flip, idx_ref, wg_ref, wu_ref, lhs_ref, *refs):
    *before, gate_ref, up_ref = refs
    rows = gate_ref.shape[0]
    offsets = row_offsets(places, heads, idx_ref[0], idx_ref[1], flip)
    width = min(256, wg_ref.shape[1])
    for n in range(wg_ref.shape[1] // width):
        cols = slice(n * width, (n + 1) * width)
        lhs = lhs_ref[0:rows, 0 : len(offsets) * HD]
        for m, (weight_ref, out_ref) in enumerate(((wg_ref, gate_ref), (wu_ref, up_ref))):
            total = half_projection(lhs, offsets, weight_ref, cols)
            out_ref[:, cols] = before[m][:, cols] + total if before else total


def hidden_kernel(places, heads, idx_ref, wg_ref, wu_ref, gate_ref, up_ref, lhs_ref, *refs):
    hidden_ref = refs[-1]
    rows = gate_ref.shape[0]
    offsets = row_offsets(places, heads, idx_ref[0], idx_ref[1], 1)
    squares = jnp.zeros((rows, HD), jnp.float32)
    for ref in (lhs_ref, *refs[:-1]):
        squares = squares + ref[:, ref.shape[1] - HD :].astype(jnp.float32)
    scale = lax.rsqrt(jnp.sum(squares, axis=1, keepdims=True) / D + EPS)
    width = min(256, wg_ref.shape[1])
    for n in range(wg_ref.shape[1] // width):
        cols = slice(n * width, (n + 1) * width)
        lhs = lhs_ref[0:rows, 0 : len(offsets) * HD]
        gate = (gate_ref[:, cols] + half_projection(lhs, offsets, wg_ref, cols)) * scale
        up = (up_ref[:, cols] + half_projection(lhs, offsets, wu_ref, cols)) * scale
        hidden_ref[:, cols] = (silu(gate) * up).astype(jnp.bfloat16)


def down_kernel(flip, parts, idx_ref, wd_ref, own_ref, peer_ref, *refs):
    out_refs = refs[-parts:]
    core, plane = lax.rem(idx_ref[0], 2), idx_ref[1]
    depth, width = own_ref.shape[1], out_refs[0].shape[1]
    total_width = parts * width
    first = (core ^ flip) * total_width
    own_rows = pl.ds(pl.multiple_of(plane * depth, depth), depth)
    peer_rows = pl.ds(pl.multiple_of((1 - plane) * depth, depth), depth)
    for n, out_ref in enumerate(out_refs):
        cols = pl.ds(pl.multiple_of(first + n * width, width), width)
        total = jnp.dot(own_ref[...], wd_ref[own_rows, cols], preferred_element_type=jnp.float32)
        total = total + jnp.dot(peer_ref[...], wd_ref[peer_rows, cols], preferred_element_type=jnp.float32)
        out_ref[...] = total.astype(jnp.bfloat16)


def pair_kernel(parts, idx_ref, *refs):
    send_ref = refs[-1]
    slots = send_ref.shape[0]
    y = lax.rem(lax.div(idx_ref[0], 2), 2)
    theirs = pl.ds(pl.multiple_of((1 - y) * slots, slots), slots)
    width = refs[0].shape[1]
    for n in range(parts):
        both = refs[n][theirs, :].astype(jnp.float32) + refs[parts + n][theirs, :].astype(jnp.float32)
        send_ref[:, n * width : (n + 1) * width] = both.astype(jnp.bfloat16)


def spread(pick, rows):
    return lax.dot_general(pick, rows, (((0,), (0,)), ((), ())), preferred_element_type=jnp.float32)


def weigh_kernel(parts, idx_ref, pick_ref, gate_ref, *refs):
    slots, span = pick_ref.shape[1] // 2, pick_ref.shape[2]
    y = lax.rem(lax.div(idx_ref[0], 2), 2)
    mine = pl.ds(pl.multiple_of(y * slots, slots), slots)
    gate = gate_ref[0, pl.ds(pl.multiple_of(y * span, span), span), :]
    pick = pick_ref[0, mine, :]
    width = refs[0].shape[1]
    for n in range(parts):
        cols = slice(n * width, (n + 1) * width)
        total = spread(pick, refs[n][mine, :]) + spread(pick, refs[parts + n][mine, :])
        refs[-1][:, cols] = total * jnp.concatenate([gate] * (width // LANES), axis=1)


def add_kernel(idx_ref, pick_ref, gate_ref, keep_ref, got_ref, own_ref, *refs):
    send_refs, total_ref = refs[:-1], refs[-1]
    slots, span = pick_ref.shape[1] // 2, pick_ref.shape[2]
    tok = own_ref.shape[0]
    z, y = lax.div(idx_ref[0], 4), lax.rem(lax.div(idx_ref[0], 2), 2)
    gate = gate_ref[1, pl.ds(pl.multiple_of(y * span, span), span), :]
    pick = pick_ref[1, pl.ds(pl.multiple_of(y * slots, slots), slots), :]
    width = 4 * LANES
    for n in range(got_ref.shape[1] // width):
        cols = slice(n * width, (n + 1) * width)
        more = spread(pick, got_ref[:, cols]) * jnp.concatenate([gate] * (width // LANES), axis=1)
        total_ref[:, cols] = keep_ref[:, cols] + more
    own_ref[...] = total_ref[pl.ds(pl.multiple_of(z * tok, tok), tok), :]
    for k, ref in enumerate(send_refs, 1):
        there = lax.rem(z + k, len(send_refs) + 1)
        ref[...] = total_ref[pl.ds(pl.multiple_of(there * tok, tok), tok), :].astype(jnp.bfloat16)


def sum_kernel(own_ref, *refs):
    total = own_ref[...]
    for ref in refs[:-1]:
        total = total + ref[...].astype(jnp.float32)
    refs[-1][...] = total.astype(refs[-1].dtype)


def final_kernel(idx_ref, *refs):
    hand_refs, sum_refs, out_ref = refs[:2], refs[2:-1], refs[-1]
    me = idx_ref[0]
    core = lax.rem(me, 2)
    levels = hand_refs[0].shape[0] // 2
    heads = out_ref.shape[1] // HD
    for n in range(2):
        own_ref, other_ref = sum_refs[2 * n : 2 * n + 2]
        half = own_ref.shape[1]

        @pl.when(core == n)
        def _(halves=(own_ref, other_ref) if n == 0 else (other_ref, own_ref)):
            for flip, hand_ref in enumerate(hand_refs):
                for low in range(2):
                    for back in range(levels):
                        head = lax.rem((me ^ (2 * low) ^ flip) + heads - 4 * back, heads)
                        hand = hand_ref[low * levels + back].astype(jnp.float32)
                        at = pl.multiple_of(head * HD, HD)
                        inside = pl.multiple_of(lax.rem(head, heads // 2) * HD, HD)
                        first = halves[0][:, pl.ds(inside, HD)].astype(jnp.float32)
                        second = halves[1][:, pl.ds(inside, HD)].astype(jnp.float32)
                        total = hand + jnp.where(head < heads // 2, first, second)
                        out_ref[:, pl.ds(at, HD)] = total.astype(jnp.bfloat16)


def heads_over_ctx(
    resid, query, key, value, norm_gain, routes, route_gates, segment_ids, w_gate, w_up, w_down
):
    ctx = lax.axis_size("ctx")
    heads, tok, width = ctx, resid.shape[0], resid.shape[1]
    levels = ctx // 4
    bf16, f32 = jnp.bfloat16, jnp.float32
    rows = ctx // 2 * tok
    span, slots = levels * tok, levels * block_slots(ctx, tok)
    me, plane = lax.axis_index("ctx"), lax.axis_index("tp")
    idx = jnp.stack([me, plane]).astype(jnp.int32)

    def shape(*dims, dtype=bf16):
        return jax.ShapeDtypeStruct(dims, dtype)

    def over_ctx(x, mask, core=None):
        return lax.ppermute(x, "ctx", [(c, c ^ mask) for c in range(ctx) if core is None or c % 2 == core])

    def along_z(x, steps):
        return lax.ppermute(x, "ctx", [(c, (c + 4 * steps) % ctx) for c in range(ctx)])

    def over_tp(x):
        return lax.ppermute(x, "tp", [(0, 1), (1, 0)])

    def across(x):
        pairs = [(2 * c + t, 2 * (c ^ 2) + (t ^ 1)) for c in range(ctx) for t in range(2)]
        return lax.ppermute(x, ("ctx", "tp"), pairs)

    def to_core(x, core):
        return lax.ppermute(x, "ctx", [(c, c ^ 1) for c in range(ctx) if c % 2 != core])

    packed = call(
        pack_kernel,
        shape(ctx, 4 * tok + META, HD),
        (segment_ids[None, :], routes.T, route_gates.T, query, key, value, resid),
        hbm=(3, 4, 5, 6),
        scratch=[pltpu.VMEM((4, tok, width), bf16), pltpu.SemaphoreType.DMA((4,))],
        vmem=60,
    )
    gain = over_tp(norm_gain)
    arrived = lax.all_to_all(packed, "ctx", split_axis=0, concat_axis=0, tiled=True)
    wg, wu, wd = w_gate[0], w_up[0], w_down[0]
    hidden_width = wg.shape[1]
    arrived, gain = lax.optimization_barrier((arrived, gain))
    gain = jnp.stack([norm_gain, gain]).astype(f32)
    hands = call(
        functools.partial(attend_kernel, block_slots(ctx, tok)),
        [shape(rows, HD)] * 2 + [shape(2, 2 * slots, span)] * 2 + [shape(2, 2 * span, LANES, dtype=f32)] * 2,
        (arrived,),
    )
    half = width // 2
    columns = []
    for hand in hands[:2]:
        if columns:
            hand, columns[0][1] = lax.optimization_barrier((hand, columns[0][1]))
        columns.append([hand] + [along_z(hand, k) for k in range(1, levels)])
    near = call(near_kernel, [shape(2, 2 * slots, HD)] * 2, (*hands[2:4], *hands[:2]))
    near = [over_tp(near[0]), across(near[1]), over_ctx(near[1], 2)]
    pieces, places, blocks, compacted = [], [], [], near
    for core, (pick, column) in enumerate(zip(hands[2:4], columns)):
        mine, theirs, *own_rows = call(
            compact_kernel,
            [shape(levels, 2 * slots, HD)] * 2 + [shape(levels, tok, HD)] * 2,
            (idx, pick, *column, *compacted),
            smem=1,
        )
        blocks.append(own_rows)
        far = [over_tp(mine[1:]), across(theirs[1:])]
        pieces.append([mine, over_ctx(theirs[1:], 2), *far, *near])
        compacted = [theirs]
        places.append(
            [[(k, 0, 0, k) for k in range(levels)]]
            + [[(k - 1, t, f, k) for k in range(1, levels)] for t, f in ((0, 2), (1, 0), (1, 2))]
            + [[(core, t, f, 0)] for t, f in ((1, 0), (1, 2), (0, 2))]
        )
    fronts, after = [], pieces[1][0]
    for groups, got, where in zip(GROUPS, pieces, places):
        sums, swapped = [], []
        for group in groups:
            chosen = [where[n] for n in group]
            mixed = call(
                functools.partial(scale_kernel, chosen),
                shape(2 * slots, (sum(map(len, chosen)) + 1) * HD),
                (idx, gain, *[got[n] for n in group], after),
                smem=1,
            )
            sums = call(
                functools.partial(project_kernel, chosen, heads, 0),
                [shape(2 * slots, hidden_width, dtype=f32)] * 2,
                (idx, wg, wu, mixed, *sums),
                smem=1,
            )
            other = over_ctx(mixed, 1)
            swapped += [mixed, other]
            if group is not groups[-1]:
                sums = call(
                    functools.partial(project_kernel, chosen, heads, 1),
                    [shape(2 * slots, hidden_width, dtype=f32)] * 2,
                    (idx, wg, wu, other, *sums),
                    smem=1,
                )
        hidden = call(
            functools.partial(hidden_kernel, chosen, heads),
            shape(2 * slots, hidden_width),
            (idx, wg, wu, *sums, swapped[-1], *swapped[:-1]),
            smem=1,
        )
        fronts.append((hidden, over_tp(hidden)))
        after = hidden
    half = width // 2
    results, after, added = [], [fronts[1][0]], [fronts[1][1]]

    def down(flip, *args):
        return call(
            functools.partial(down_kernel, flip, PARTS),
            [shape(2 * slots, half // PARTS)] * PARTS,
            (idx, wd, *args),
            smem=1,
        )

    by_y = call(gather_kernel, shape(2, levels, tok, HD), (blocks[0][1], blocks[1][1], fronts[1][0]))
    keep_rows, send_rows = call(
        own_rows_kernel,
        [shape(2 * levels, tok, HD)] * 2,
        (idx, blocks[0][0], blocks[1][0], over_ctx(by_y, 2)),
        smem=1,
    )
    for core, (hidden, peer) in enumerate(fronts):
        pick, gates = hands[2 + core], hands[4 + core]
        other = [over_ctx(part, 1) for part in down(1, hidden, peer, *after)]
        half_out = down(0, hidden, peer)
        send = call(
            functools.partial(pair_kernel, PARTS), shape(slots, half), (idx, *half_out, *other, *added), smem=1
        )
        after = [send]
        got = over_ctx(send, 2)
        keep = call(
            functools.partial(weigh_kernel, PARTS),
            shape(span, half, dtype=f32),
            (idx, pick, gates, *half_out, *other),
            smem=1,
        )
        own, *sends = call(
            add_kernel,
            [shape(tok, half, dtype=f32)] + [shape(tok, half)] * (levels - 1),
            (idx, pick, gates, keep, got),
            smem=1,
            scratch=[pltpu.VMEM((span, half), f32)],
        )
        added = [own]
        summed = call(sum_kernel, shape(tok, half, dtype=f32), (own, *[along_z(s, k) for k, s in enumerate(sends, 1)]))
        results += [summed, to_core(summed, core)]
    return call(final_kernel, shape(tok, width), (idx, keep_rows, over_ctx(send_rows, 1), *results), smem=1)


def general(
    resid, query, key, value, norm_gain, routes, route_gates, segment_ids, w_gate, w_up, w_down
):
    tok_count = resid.shape[0]
    feat_width = resid.shape[1]
    head_count = feat_width // HD
    score_scale = 1.0 / math.sqrt(HD)
    query_pos = lax.axis_index("ctx") * tok_count + jnp.arange(tok_count, dtype=jnp.int32)
    key_segments = lax.all_gather(segment_ids, "ctx", axis=0, tiled=True)
    query_heads = query.reshape(tok_count, head_count, HD)
    start_sums = (
        jnp.zeros((tok_count, feat_width), jnp.float32),
        jnp.zeros((tok_count,), jnp.float32),
    )
    key_piece = lax.all_gather(key, "ctx", axis=0, tiled=True)
    value_piece = lax.all_gather(value, "ctx", axis=0, tiled=True)
    piece_len = key_piece.shape[0]
    block_len = math.gcd(piece_len, 512)
    block_count = piece_len // block_len
    key_blocks = key_piece.reshape(block_count, block_len, head_count, HD)
    value_blocks = value_piece.reshape(block_count, block_len, head_count, HD)

    def advance(state, inputs):
        key_block, value_block, block_id = inputs
        key_first = block_id * block_len

        def compute(current):
            acc_sum, key_total = current
            key_pos = key_first + jnp.arange(block_len, dtype=jnp.int32)
            key_segs = lax.dynamic_slice_in_dim(key_segments, key_first, block_len, 0)
            visible = jnp.logical_and(
                key_segs[None, :] == segment_ids[:, None], key_pos[None, :] <= query_pos[:, None]
            ).astype(jnp.float32)
            scores = (
                jnp.einsum(
                    "thd,shd->hts", query_heads, key_block, preferred_element_type=jnp.float32
                )
                * score_scale
            )
            weights = (jax.nn.silu(scores) * visible[None]).astype(jnp.bfloat16)
            summed = jnp.einsum(
                "hts,shd->thd", weights, value_block, preferred_element_type=jnp.float32
            )
            return (
                acc_sum + summed.reshape(tok_count, feat_width),
                key_total + jnp.sum(visible, axis=1),
            )

        last_key_seg = lax.dynamic_slice_in_dim(key_segments, key_first + block_len - 1, 1, 0)[0]
        reached = jnp.logical_and(key_first <= query_pos[-1], last_key_seg >= segment_ids[0])
        state = lax.cond(reached, compute, lambda current: current, state)
        return (state, None)

    block_ids = jnp.arange(block_count, dtype=jnp.int32)
    result, unused = lax.scan(advance, start_sums, (key_blocks, value_blocks, block_ids))
    acc_sum, key_total = result
    attended = acc_sum / jnp.sqrt(key_total)[:, None]
    hand_state = (resid.astype(jnp.float32) + attended).astype(jnp.bfloat16)
    hand_f32 = hand_state.astype(jnp.float32)
    square_sums = lax.psum(jnp.sum(hand_f32 * hand_f32, axis=1), ("tp", "sub"))
    normed = (
        hand_f32 * lax.rsqrt(square_sums / D + EPS)[:, None] * norm_gain.astype(jnp.float32)
    ).astype(jnp.bfloat16)
    ctx_count = lax.axis_size("ctx")
    expert_count = ctx_count // 2
    capacity = block_slots(ctx_count, tok_count)
    slot_total = expert_count * capacity
    recv_total = ctx_count * capacity
    flat_routes = routes.reshape(-1)
    onehot = (flat_routes[:, None] == jnp.arange(expert_count, dtype=jnp.int32)[None, :]).astype(
        jnp.int32
    )
    slot_rank = jnp.sum((jnp.cumsum(onehot, axis=0) - 1) * onehot, axis=1)
    slot_index = flat_routes * capacity + slot_rank
    position = jnp.arange(tok_count * TOPK, dtype=jnp.int32) // TOPK
    slot_source = jnp.full((slot_total,), tok_count, jnp.int32).at[slot_index].set(position)
    gate_local = w_gate[0]
    up_local = w_up[0]
    down_local = w_down[0]
    gathered = lax.all_gather(normed, ("tp", "sub"), axis=1, tiled=True)
    padded = jnp.concatenate([gathered, jnp.zeros((1, gathered.shape[1]), gathered.dtype)], axis=0)
    filled = padded[slot_source].reshape(expert_count, capacity, gathered.shape[1])
    arrived = lax.all_to_all(
        jnp.repeat(filled, 2, axis=0), "ctx", split_axis=0, concat_axis=0, tiled=True
    ).reshape(recv_total, gathered.shape[1])
    gate_sum = jnp.dot(arrived, gate_local, preferred_element_type=jnp.float32)
    up_sum = jnp.dot(arrived, up_local, preferred_element_type=jnp.float32)
    hidden = (jax.nn.silu(gate_sum) * up_sum).astype(jnp.bfloat16)
    down_rows_out = jnp.dot(
        lax.all_gather(hidden, ("tp", "sub"), axis=1, tiled=True),
        down_local,
        preferred_element_type=jnp.float32,
    ).astype(jnp.bfloat16)
    returned = lax.all_to_all(
        down_rows_out.reshape(ctx_count, capacity, feat_width),
        "ctx",
        split_axis=0,
        concat_axis=0,
        tiled=True,
    )
    combined = jnp.sum(
        returned.reshape(expert_count, 2, capacity, feat_width).astype(jnp.float32), axis=1
    ).reshape(slot_total, feat_width)
    picked = combined[slot_index].reshape(tok_count, TOPK, feat_width)
    mixed = hand_f32 + jnp.sum(route_gates[:, :, None] * picked, axis=1)
    return mixed.astype(jnp.bfloat16)


def block_slots(ctx, tok):
    return min(tok, max(2, tok * 10 // ctx))


def fits(mesh, resid):
    ctx, tp = mesh.shape["ctx"], mesh.shape["tp"]
    heads = resid.shape[1] // tp // HD
    tok = resid.shape[0] // mesh.shape["groups"] // ctx
    slots = ctx // 4 * block_slots(ctx, tok)
    whole = heads == ctx and 2 * tok == LANES and slots % 16 == 0
    return tp == 2 and mesh.shape["sub"] == 1 and whole and ctx >= 8 and ctx & (ctx - 1) == 0


def solution(mesh):
    placed = (
        P(("groups", "ctx"), ("tp", "sub")),
        P(("groups", "ctx"), ("tp", "sub")),
        P(("groups", "ctx"), ("tp", "sub")),
        P(("groups", "ctx"), ("tp", "sub")),
        P(("tp", "sub")),
        P(("groups", "ctx"), None),
        P(("groups", "ctx"), None),
        P(("groups", "ctx")),
        P("ctx", None, ("tp", "sub")),
        P("ctx", None, ("tp", "sub")),
        P("ctx", None, ("tp", "sub")),
    )

    def step(resid, *rest):
        per_device = heads_over_ctx if fits(mesh, resid) else general
        return jax.shard_map(
            per_device,
            mesh=mesh,
            in_specs=placed,
            out_specs=P(("groups", "ctx"), ("tp", "sub")),
            check_vma=False,
        )(resid, *rest)

    return step
```

```python
import functools
import math

import jax
import jax.numpy as jnp
from jax import lax
from jax.experimental import pallas as pl
from jax.experimental.pallas import tpu as pltpu
from jax.sharding import PartitionSpec as P

D = 4096
HD = 128
TOPK = 4
EPS = 1e-06
META = 16
LANES = 128
MIB = 1 << 20
PARTS = 4
GROUPS = (((0, 1, 2, 3, 4, 5, 6),), ((0, 1, 2, 3, 4, 5, 6),))


def silu(v):
    return v * (0.5 * jnp.tanh(0.5 * v) + 0.5)


def call(kernel, out_shape, args, smem=0, hbm=(), scratch=(), vmem=8, out_space=pltpu.VMEM):
    spaces = [pltpu.SMEM if n < smem else pltpu.HBM if n in hbm else pltpu.VMEM for n in range(len(args))]
    several = isinstance(out_shape, (tuple, list))
    out = pl.BlockSpec(memory_space=out_space)
    return pl.pallas_call(
        kernel,
        out_shape=out_shape,
        in_specs=[pl.BlockSpec(memory_space=space) for space in spaces],
        out_specs=tuple(out for _ in out_shape) if several else out,
        scratch_shapes=list(scratch),
        compiler_params=pltpu.CompilerParams(vmem_limit_bytes=vmem * MIB),
    )(*args)


def pack_kernel(seg_ref, route_ref, gate_ref, q_ref, k_ref, v_ref, r_ref, out_ref, held_ref, meta_ref, staged_ref, sems):
    heads, tok = out_ref.shape[0], q_ref.shape[0]
    arrays = (q_ref, k_ref, v_ref, r_ref)
    copies = [pltpu.make_async_copy(ref, held_ref.at[n], sems.at[0, n]) for n, ref in enumerate(arrays)]
    for copy in copies:
        copy.start()
    row = lax.broadcasted_iota(jnp.int32, (META, tok), 0)
    seg = jnp.broadcast_to(seg_ref[...].astype(jnp.float32), (META, tok))
    parts = []
    for e in range(heads // 2):
        gate = jnp.sum(jnp.where(route_ref[...] == e, gate_ref[...], 0.0), axis=0, keepdims=True)
        gate = jnp.broadcast_to(gate, (META, tok))
        high = gate.astype(jnp.bfloat16).astype(jnp.float32)
        middle = (gate - high).astype(jnp.bfloat16).astype(jnp.float32)
        parts.append((high, middle, gate - high - middle))
    meta_ref[...] = jnp.zeros(meta_ref.shape, jnp.bfloat16)
    for h in range(heads):
        meta = jnp.where(row == 0, seg, 0.0)
        for n, piece in enumerate(parts[h // 2] + parts[h // 2 ^ 1], 1):
            meta = jnp.where(row == n, piece, meta)
        meta_ref[h, :, 0:tok] = meta.astype(jnp.bfloat16)
    sent = [pltpu.make_async_copy(meta_ref, out_ref.at[:, 4 * tok :, :], sems.at[1, 4])]
    sent[0].start()
    for n, copy in enumerate(copies):
        copy.wait()
        for h in range(heads):
            staged_ref[n, h, :, :] = held_ref[n, :, h * HD : (h + 1) * HD]
        sent.append(pltpu.make_async_copy(staged_ref.at[n], out_ref.at[:, n * tok : (n + 1) * tok, :], sems.at[1, n]))
        sent[-1].start()
    for copy in sent:
        copy.wait()


def attend_kernel(capacity, x_ref, even_ref, odd_ref, pick_even_ref, pick_odd_ref, gate_even_ref, gate_odd_ref):
    blocks = x_ref.shape[0]
    tok = LANES // 2
    levels = blocks // 4
    scale = 1.0 / math.sqrt(HD)
    lane = lax.broadcasted_iota(jnp.int32, (META, LANES), 1)
    row_at = lax.broadcasted_iota(jnp.int32, (LANES, LANES), 0)
    lane_at = lax.broadcasted_iota(jnp.int32, (LANES, LANES), 1)
    causal = lane_at <= row_at
    span = levels * tok
    slots = levels * capacity
    earlier_at = lax.broadcasted_iota(jnp.int32, (span, span), 0)
    later_at = lax.broadcasted_iota(jnp.int32, (span, span), 1)
    earlier = jnp.logical_and(earlier_at < later_at, earlier_at // tok == later_at // tok)
    earlier = earlier.astype(jnp.float32).astype(jnp.bfloat16)
    slot_at = lax.broadcasted_iota(jnp.int32, (slots, span), 0).astype(jnp.float32)
    base = (lax.broadcasted_iota(jnp.int32, (1, span), 1) // tok * capacity).astype(jnp.float32)

    def part(n, first, last):
        return x_ref[first:last, n * tok : (n + 1) * tok, :].reshape((last - first) * tok, HD)

    def scalars(first, second):
        left = x_ref[first, 4 * tok :, :].astype(jnp.float32)
        right = pltpu.roll(x_ref[second, 4 * tok :, :].astype(jnp.float32), tok, 1)
        return jnp.where(lane < tok, left, right)

    def gate_of(meta, which):
        first = 1 + 3 * which
        return meta[first : first + 1, :] + (meta[first + 1 : first + 2, :] + meta[first + 2 : first + 3, :])

    def down_rows(row):
        return jnp.transpose(jnp.broadcast_to(row, (LANES, LANES)))

    for y in range(2):
        for odd, (pick_ref, gate_ref) in enumerate(((pick_even_ref, gate_even_ref), (pick_odd_ref, gate_odd_ref))):
            metas = [scalars(4 * z + 2 * y + odd, 4 * z + 4 + 2 * y + odd) for z in range(0, levels, 2)]
            for which in range(2):
                rows = [gate_of(meta, which) for meta in metas]
                for n, row in enumerate(rows):
                    gate_ref[which, y * span + n * LANES : y * span + (n + 1) * LANES, :] = down_rows(row)
                named = (jnp.concatenate(rows, axis=1) > 0.0).astype(jnp.float32)
                rank = jnp.dot(
                    jnp.broadcast_to(named, (META, span)).astype(jnp.bfloat16),
                    earlier,
                    preferred_element_type=jnp.float32,
                )[0:1, :]
                target = jnp.broadcast_to(jnp.where(named > 0.0, base + rank, -1.0), (slots, span))
                pick = (slot_at == target).astype(jnp.float32).astype(jnp.bfloat16)
                pick_ref[which, y * slots : (y + 1) * slots, :] = pick

    seg_rows = []
    for i in range(blocks // 2):
        seg_rows.append(scalars(2 * i, 2 * i + 1)[0:1, :])
        seg_col = down_rows(seg_rows[i])
        masks = []
        for j in range(i + 1):
            same = seg_col == jnp.broadcast_to(seg_rows[j], (LANES, LANES))
            if j == i:
                same = jnp.logical_and(same, causal)
            masks.append(same.astype(jnp.float32))
        visible = jnp.concatenate(masks, axis=1)
        query = part(0, 2 * i, 2 * i + 2)
        keys = part(1, 0, 2 * i + 2)
        values = part(2, 0, 2 * i + 2)
        scores = (
            lax.dot_general(query, keys, (((1,), (1,)), ((), ())), preferred_element_type=jnp.float32) * scale
        )
        weights = (silu(scores) * visible).astype(jnp.bfloat16)
        summed = jnp.dot(weights, values, preferred_element_type=jnp.float32)
        counted = jnp.sum(visible, axis=1, keepdims=True)
        hand = (part(3, 2 * i, 2 * i + 2).astype(jnp.float32) + summed / jnp.sqrt(counted)).astype(jnp.bfloat16)
        at = (i % 2 * levels + i // 2) * tok
        even_ref[at : at + tok, :] = hand[:tok, :]
        odd_ref[at : at + tok, :] = hand[tok:, :]


def near_kernel(pick_even_ref, pick_odd_ref, even_ref, odd_ref, mine_ref, theirs_ref):
    slots, span = pick_even_ref.shape[1] // 2, pick_even_ref.shape[2]
    for n, (pick_ref, ref) in enumerate(((pick_even_ref, even_ref), (pick_odd_ref, odd_ref))):
        for group in range(2):
            here = slice(group * slots, (group + 1) * slots)
            block = ref[group * span : (group + 1) * span, :]
            for which, out_ref in enumerate((mine_ref, theirs_ref)):
                rows = jnp.dot(pick_ref[which, here, :], block, preferred_element_type=jnp.float32)
                out_ref[n, here, :] = rows.astype(jnp.bfloat16)


def compact_kernel(idx_ref, pick_ref, *refs):
    *out_refs, mine_own_ref, theirs_own_ref = refs[-4:]
    me = idx_ref[0]
    levels, tok = mine_own_ref.shape[:2]
    pieces = refs[:levels]
    slots, span = pick_ref.shape[1] // 2, pick_ref.shape[2]
    z, y = lax.div(me, 4), lax.rem(lax.div(me, 2), 2)
    for group in range(2):
        block = jnp.concatenate([p[group * span : (group + 1) * span, :] for p in pieces], axis=1)
        for which, out_ref in enumerate(out_refs):
            here = slice(group * slots, (group + 1) * slots)
            rows = jnp.dot(pick_ref[which, here, :], block, preferred_element_type=jnp.float32).astype(jnp.bfloat16)
            for k in range(levels):
                out_ref[k, here, :] = rows[:, k * HD : (k + 1) * HD]
    for which, out_ref in enumerate((mine_own_ref, theirs_own_ref)):
        own = pl.ds(pl.multiple_of(((y ^ which) * levels + z) * tok, tok), tok)
        for k in range(levels):
            out_ref[k, :, :] = pieces[k][own, :]


def gather_kernel(*refs):
    out_ref = refs[-1]
    for n in range(out_ref.shape[0]):
        out_ref[n] = refs[n][...]


def own_rows_kernel(idx_ref, even_ref, odd_ref, by_y_ref, keep_ref, send_ref):
    core = lax.rem(idx_ref[0], 2)
    levels = even_ref.shape[0]
    for n, ref in enumerate((even_ref, odd_ref)):
        for same, out_ref in ((True, keep_ref), (False, send_ref)):
            @pl.when((core == n) == same)
            def _(ref=ref, out_ref=out_ref, n=n):
                out_ref[:levels] = ref[...]
                out_ref[levels:] = by_y_ref[n]


def thirds(value):
    high = value.astype(jnp.bfloat16)
    rest = value - high.astype(jnp.float32)
    middle = rest.astype(jnp.bfloat16)
    return high, middle, (rest - middle.astype(jnp.float32)).astype(jnp.bfloat16)


def scale_kernel(places, idx_ref, gain_ref, *refs):
    pieces, out_ref = refs[: len(places)], refs[-1]
    me = idx_ref[0]
    heads = gain_ref.shape[1] // HD
    rows = out_ref.shape[0]
    width = sum(map(len, places)) * HD
    tile = rows // 2
    for r in range(rows // tile):
        here = slice(r * tile, (r + 1) * tile)
        squares = jnp.zeros((tile, HD), jnp.float32)
        n = 0
        for ref, entries in zip(pieces, places):
            for k, other, low, back in entries:
                head = lax.rem((me ^ low) + heads - 4 * back, heads)
                gain = gain_ref[other : other + 1, pl.ds(pl.multiple_of(head * HD, HD), HD)]
                v = ref[k, here, :].astype(jnp.float32)
                squares = squares + v * v
                out_ref[here, n : n + HD] = (v * gain).astype(jnp.bfloat16)
                n += HD
        lane = lax.broadcasted_iota(jnp.int32, (tile, HD), 1)
        high, middle, low = thirds(jnp.broadcast_to(jnp.sum(squares, axis=1, keepdims=True), (tile, HD)))
        parts = jnp.where(lane == 0, high, jnp.where(lane == 1, middle, jnp.where(lane == 2, low, 0)))
        out_ref[here, width:] = parts.astype(jnp.bfloat16)


def row_offsets(places, heads, me, plane, flip):
    found = []
    for _, other, low, back in (entry for entries in places for entry in entries):
        head = lax.rem((me ^ low ^ flip) + heads - 4 * back, heads)
        found.append(pl.multiple_of(((plane ^ other) * heads + head) * HD, HD))
    return found


def half_projection(lhs, offsets, weight_ref, cols):
    weights = jnp.concatenate([weight_ref[pl.ds(at, HD), cols] for at in offsets], axis=0)
    return jnp.dot(lhs, weights, preferred_element_type=jnp.float32)


def project_kernel(places, heads, flip, idx_ref, wg_ref, wu_ref, lhs_ref, *refs):
    *before, gate_ref, up_ref = refs
    rows = gate_ref.shape[0]
    offsets = row_offsets(places, heads, idx_ref[0], idx_ref[1], flip)
    width = min(256, wg_ref.shape[1])
    for n in range(wg_ref.shape[1] // width):
        cols = slice(n * width, (n + 1) * width)
        lhs = lhs_ref[0:rows, 0 : len(offsets) * HD]
        for m, (weight_ref, out_ref) in enumerate(((wg_ref, gate_ref), (wu_ref, up_ref))):
            total = half_projection(lhs, offsets, weight_ref, cols)
            out_ref[:, cols] = before[m][:, cols] + total if before else total


def hidden_kernel(places, heads, idx_ref, wg_ref, wu_ref, gate_ref, up_ref, lhs_ref, *refs):
    hidden_ref = refs[-1]
    rows = gate_ref.shape[0]
    offsets = row_offsets(places, heads, idx_ref[0], idx_ref[1], 1)
    squares = jnp.zeros((rows, HD), jnp.float32)
    for ref in (lhs_ref, *refs[:-1]):
        squares = squares + ref[:, ref.shape[1] - HD :].astype(jnp.float32)
    scale = lax.rsqrt(jnp.sum(squares, axis=1, keepdims=True) / D + EPS)
    width = min(256, wg_ref.shape[1])
    for n in range(wg_ref.shape[1] // width):
        cols = slice(n * width, (n + 1) * width)
        lhs = lhs_ref[0:rows, 0 : len(offsets) * HD]
        gate = (gate_ref[:, cols] + half_projection(lhs, offsets, wg_ref, cols)) * scale
        up = (up_ref[:, cols] + half_projection(lhs, offsets, wu_ref, cols)) * scale
        hidden_ref[:, cols] = (silu(gate) * up).astype(jnp.bfloat16)


def down_kernel(flip, parts, idx_ref, wd_ref, own_ref, peer_ref, *refs):
    out_refs = refs[-parts:]
    core, plane = lax.rem(idx_ref[0], 2), idx_ref[1]
    depth, width = own_ref.shape[1], out_refs[0].shape[1]
    total_width = parts * width
    first = (core ^ flip) * total_width
    own_rows = pl.ds(pl.multiple_of(plane * depth, depth), depth)
    peer_rows = pl.ds(pl.multiple_of((1 - plane) * depth, depth), depth)
    for n, out_ref in enumerate(out_refs):
        cols = pl.ds(pl.multiple_of(first + n * width, width), width)
        total = jnp.dot(own_ref[...], wd_ref[own_rows, cols], preferred_element_type=jnp.float32)
        total = total + jnp.dot(peer_ref[...], wd_ref[peer_rows, cols], preferred_element_type=jnp.float32)
        out_ref[...] = total.astype(jnp.bfloat16)


def pair_kernel(parts, idx_ref, *refs):
    send_ref = refs[-1]
    slots = send_ref.shape[0]
    y = lax.rem(lax.div(idx_ref[0], 2), 2)
    theirs = pl.ds(pl.multiple_of((1 - y) * slots, slots), slots)
    width = refs[0].shape[1]
    for n in range(parts):
        both = refs[n][theirs, :].astype(jnp.float32) + refs[parts + n][theirs, :].astype(jnp.float32)
        send_ref[:, n * width : (n + 1) * width] = both.astype(jnp.bfloat16)


def spread(pick, rows):
    return lax.dot_general(pick, rows, (((0,), (0,)), ((), ())), preferred_element_type=jnp.float32)


def weigh_kernel(parts, idx_ref, pick_ref, gate_ref, *refs):
    slots, span = pick_ref.shape[1] // 2, pick_ref.shape[2]
    y = lax.rem(lax.div(idx_ref[0], 2), 2)
    mine = pl.ds(pl.multiple_of(y * slots, slots), slots)
    gate = gate_ref[0, pl.ds(pl.multiple_of(y * span, span), span), :]
    pick = pick_ref[0, mine, :]
    width = refs[0].shape[1]
    for n in range(parts):
        cols = slice(n * width, (n + 1) * width)
        total = spread(pick, refs[n][mine, :]) + spread(pick, refs[parts + n][mine, :])
        refs[-1][:, cols] = total * jnp.concatenate([gate] * (width // LANES), axis=1)


def add_kernel(idx_ref, pick_ref, gate_ref, keep_ref, got_ref, own_ref, *refs):
    send_refs, total_ref = refs[:-1], refs[-1]
    slots, span = pick_ref.shape[1] // 2, pick_ref.shape[2]
    tok = own_ref.shape[0]
    z, y = lax.div(idx_ref[0], 4), lax.rem(lax.div(idx_ref[0], 2), 2)
    gate = gate_ref[1, pl.ds(pl.multiple_of(y * span, span), span), :]
    pick = pick_ref[1, pl.ds(pl.multiple_of(y * slots, slots), slots), :]
    width = 4 * LANES
    for n in range(got_ref.shape[1] // width):
        cols = slice(n * width, (n + 1) * width)
        more = spread(pick, got_ref[:, cols]) * jnp.concatenate([gate] * (width // LANES), axis=1)
        total_ref[:, cols] = keep_ref[:, cols] + more
    own_ref[...] = total_ref[pl.ds(pl.multiple_of(z * tok, tok), tok), :]
    for k, ref in enumerate(send_refs, 1):
        there = lax.rem(z + k, len(send_refs) + 1)
        ref[...] = total_ref[pl.ds(pl.multiple_of(there * tok, tok), tok), :].astype(jnp.bfloat16)


def sum_kernel(own_ref, *refs):
    total = own_ref[...]
    for ref in refs[:-1]:
        total = total + ref[...].astype(jnp.float32)
    refs[-1][...] = total.astype(refs[-1].dtype)


def final_kernel(idx_ref, *refs):
    hand_refs, sum_refs, out_ref = refs[:2], refs[2:-1], refs[-1]
    me = idx_ref[0]
    core = lax.rem(me, 2)
    levels = hand_refs[0].shape[0] // 2
    heads = out_ref.shape[1] // HD
    for n in range(2):
        own_ref, other_ref = sum_refs[2 * n : 2 * n + 2]

        @pl.when(core == n)
        def _(halves=(own_ref, other_ref) if n == 0 else (other_ref, own_ref), n=n):
            for head in range(heads):
                low = lax.rem(lax.div(me ^ head, 2), 2)
                back = lax.rem(lax.div(me, 4) + levels - head // 4, levels)
                hand = hand_refs[(head % 2) ^ n][low * levels + back].astype(jnp.float32)
                first = head % (heads // 2) * HD
                total = halves[head // (heads // 2)][:, first : first + HD].astype(jnp.float32)
                out_ref[:, head * HD : (head + 1) * HD] = (hand + total).astype(jnp.bfloat16)


def heads_over_ctx(
    resid, query, key, value, norm_gain, routes, route_gates, segment_ids, w_gate, w_up, w_down
):
    ctx = lax.axis_size("ctx")
    heads, tok, width = ctx, resid.shape[0], resid.shape[1]
    levels = ctx // 4
    bf16, f32 = jnp.bfloat16, jnp.float32
    rows = ctx // 2 * tok
    span, slots = levels * tok, levels * block_slots(ctx, tok)
    me, plane = lax.axis_index("ctx"), lax.axis_index("tp")
    idx = jnp.stack([me, plane]).astype(jnp.int32)

    def shape(*dims, dtype=bf16):
        return jax.ShapeDtypeStruct(dims, dtype)

    def over_ctx(x, mask, core=None):
        return lax.ppermute(x, "ctx", [(c, c ^ mask) for c in range(ctx) if core is None or c % 2 == core])

    def along_z(x, steps):
        return lax.ppermute(x, "ctx", [(c, (c + 4 * steps) % ctx) for c in range(ctx)])

    def over_tp(x):
        return lax.ppermute(x, "tp", [(0, 1), (1, 0)])

    def across(x):
        pairs = [(2 * c + t, 2 * (c ^ 2) + (t ^ 1)) for c in range(ctx) for t in range(2)]
        return lax.ppermute(x, ("ctx", "tp"), pairs)

    def to_core(x, core):
        return lax.ppermute(x, "ctx", [(c, c ^ 1) for c in range(ctx) if c % 2 != core])

    packed = call(
        pack_kernel,
        shape(ctx, 4 * tok + META, HD),
        (segment_ids[None, :], routes.T, route_gates.T, query, key, value, resid),
        hbm=(3, 4, 5, 6),
        scratch=[pltpu.VMEM((4, tok, width), bf16), pltpu.VMEM((ctx, META, HD), bf16)]
        + [pltpu.VMEM((4, ctx, tok, HD), bf16), pltpu.SemaphoreType.DMA((2, 5))],
        vmem=60,
        out_space=pltpu.HBM,
    )
    gain = over_tp(norm_gain)
    arrived = lax.all_to_all(packed, "ctx", split_axis=0, concat_axis=0, tiled=True)
    wg, wu, wd = w_gate[0], w_up[0], w_down[0]
    hidden_width = wg.shape[1]
    arrived, gain = lax.optimization_barrier((arrived, gain))
    gain = jnp.stack([norm_gain, gain]).astype(f32)
    hands = call(
        functools.partial(attend_kernel, block_slots(ctx, tok)),
        [shape(rows, HD)] * 2 + [shape(2, 2 * slots, span)] * 2 + [shape(2, 2 * span, LANES, dtype=f32)] * 2,
        (arrived,),
    )
    half = width // 2
    columns = []
    for hand in hands[:2]:
        if columns:
            hand, columns[0][1] = lax.optimization_barrier((hand, columns[0][1]))
        columns.append([hand] + [along_z(hand, k) for k in range(1, levels)])
    near = call(near_kernel, [shape(2, 2 * slots, HD)] * 2, (*hands[2:4], *hands[:2]))
    near = [over_tp(near[0]), across(near[1]), over_ctx(near[1], 2)]
    pieces, places, blocks, compacted = [], [], [], near
    for core, (pick, column) in enumerate(zip(hands[2:4], columns)):
        mine, theirs, *own_rows = call(
            compact_kernel,
            [shape(levels, 2 * slots, HD)] * 2 + [shape(levels, tok, HD)] * 2,
            (idx, pick, *column, *compacted),
            smem=1,
        )
        blocks.append(own_rows)
        far = [over_tp(mine[1:]), across(theirs[1:])]
        pieces.append([mine, over_ctx(theirs[1:], 2), *far, *near])
        compacted = [theirs]
        places.append(
            [[(k, 0, 0, k) for k in range(levels)]]
            + [[(k - 1, t, f, k) for k in range(1, levels)] for t, f in ((0, 2), (1, 0), (1, 2))]
            + [[(core, t, f, 0)] for t, f in ((1, 0), (1, 2), (0, 2))]
        )
    fronts, after = [], pieces[1][0]
    for groups, got, where in zip(GROUPS, pieces, places):
        sums, swapped = [], []
        for group in groups:
            chosen = [where[n] for n in group]
            mixed = call(
                functools.partial(scale_kernel, chosen),
                shape(2 * slots, (sum(map(len, chosen)) + 1) * HD),
                (idx, gain, *[got[n] for n in group], after),
                smem=1,
            )
            sums = call(
                functools.partial(project_kernel, chosen, heads, 0),
                [shape(2 * slots, hidden_width, dtype=f32)] * 2,
                (idx, wg, wu, mixed, *sums),
                smem=1,
            )
            other = over_ctx(mixed, 1)
            swapped += [mixed, other]
            if group is not groups[-1]:
                sums = call(
                    functools.partial(project_kernel, chosen, heads, 1),
                    [shape(2 * slots, hidden_width, dtype=f32)] * 2,
                    (idx, wg, wu, other, *sums),
                    smem=1,
                )
        hidden = call(
            functools.partial(hidden_kernel, chosen, heads),
            shape(2 * slots, hidden_width),
            (idx, wg, wu, *sums, swapped[-1], *swapped[:-1]),
            smem=1,
        )
        fronts.append((hidden, over_tp(hidden)))
        after = hidden
    half = width // 2
    results, after, added = [], [fronts[1][0]], [fronts[1][1]]

    def down(flip, *args):
        return call(
            functools.partial(down_kernel, flip, PARTS),
            [shape(2 * slots, half // PARTS)] * PARTS,
            (idx, wd, *args),
            smem=1,
        )

    by_y = call(gather_kernel, shape(2, levels, tok, HD), (blocks[0][1], blocks[1][1], fronts[1][0]))
    keep_rows, send_rows = call(
        own_rows_kernel,
        [shape(2 * levels, tok, HD)] * 2,
        (idx, blocks[0][0], blocks[1][0], over_ctx(by_y, 2)),
        smem=1,
    )
    for core, (hidden, peer) in enumerate(fronts):
        pick, gates = hands[2 + core], hands[4 + core]
        other = [over_ctx(part, 1) for part in down(1, hidden, peer, *after)]
        half_out = down(0, hidden, peer)
        send = call(
            functools.partial(pair_kernel, PARTS), shape(slots, half), (idx, *half_out, *other, *added), smem=1
        )
        after = [send]
        got = over_ctx(send, 2)
        keep = call(
            functools.partial(weigh_kernel, PARTS),
            shape(span, half, dtype=f32),
            (idx, pick, gates, *half_out, *other),
            smem=1,
        )
        own, *sends = call(
            add_kernel,
            [shape(tok, half, dtype=f32)] + [shape(tok, half)] * (levels - 1),
            (idx, pick, gates, keep, got),
            smem=1,
            scratch=[pltpu.VMEM((span, half), f32)],
        )
        added = [own]
        summed = call(sum_kernel, shape(tok, half, dtype=f32), (own, *[along_z(s, k) for k, s in enumerate(sends, 1)]))
        results += [summed, to_core(summed, core)]
    return call(final_kernel, shape(tok, width), (idx, keep_rows, over_ctx(send_rows, 1), *results), smem=1)


def general(
    resid, query, key, value, norm_gain, routes, route_gates, segment_ids, w_gate, w_up, w_down
):
    tok_count = resid.shape[0]
    feat_width = resid.shape[1]
    head_count = feat_width // HD
    score_scale = 1.0 / math.sqrt(HD)
    query_pos = lax.axis_index("ctx") * tok_count + jnp.arange(tok_count, dtype=jnp.int32)
    key_segments = lax.all_gather(segment_ids, "ctx", axis=0, tiled=True)
    query_heads = query.reshape(tok_count, head_count, HD)
    start_sums = (
        jnp.zeros((tok_count, feat_width), jnp.float32),
        jnp.zeros((tok_count,), jnp.float32),
    )
    key_piece = lax.all_gather(key, "ctx", axis=0, tiled=True)
    value_piece = lax.all_gather(value, "ctx", axis=0, tiled=True)
    piece_len = key_piece.shape[0]
    block_len = math.gcd(piece_len, 512)
    block_count = piece_len // block_len
    key_blocks = key_piece.reshape(block_count, block_len, head_count, HD)
    value_blocks = value_piece.reshape(block_count, block_len, head_count, HD)

    def advance(state, inputs):
        key_block, value_block, block_id = inputs
        key_first = block_id * block_len

        def compute(current):
            acc_sum, key_total = current
            key_pos = key_first + jnp.arange(block_len, dtype=jnp.int32)
            key_segs = lax.dynamic_slice_in_dim(key_segments, key_first, block_len, 0)
            visible = jnp.logical_and(
                key_segs[None, :] == segment_ids[:, None], key_pos[None, :] <= query_pos[:, None]
            ).astype(jnp.float32)
            scores = (
                jnp.einsum(
                    "thd,shd->hts", query_heads, key_block, preferred_element_type=jnp.float32
                )
                * score_scale
            )
            weights = (jax.nn.silu(scores) * visible[None]).astype(jnp.bfloat16)
            summed = jnp.einsum(
                "hts,shd->thd", weights, value_block, preferred_element_type=jnp.float32
            )
            return (
                acc_sum + summed.reshape(tok_count, feat_width),
                key_total + jnp.sum(visible, axis=1),
            )

        last_key_seg = lax.dynamic_slice_in_dim(key_segments, key_first + block_len - 1, 1, 0)[0]
        reached = jnp.logical_and(key_first <= query_pos[-1], last_key_seg >= segment_ids[0])
        state = lax.cond(reached, compute, lambda current: current, state)
        return (state, None)

    block_ids = jnp.arange(block_count, dtype=jnp.int32)
    result, unused = lax.scan(advance, start_sums, (key_blocks, value_blocks, block_ids))
    acc_sum, key_total = result
    attended = acc_sum / jnp.sqrt(key_total)[:, None]
    hand_state = (resid.astype(jnp.float32) + attended).astype(jnp.bfloat16)
    hand_f32 = hand_state.astype(jnp.float32)
    square_sums = lax.psum(jnp.sum(hand_f32 * hand_f32, axis=1), ("tp", "sub"))
    normed = (
        hand_f32 * lax.rsqrt(square_sums / D + EPS)[:, None] * norm_gain.astype(jnp.float32)
    ).astype(jnp.bfloat16)
    ctx_count = lax.axis_size("ctx")
    expert_count = ctx_count // 2
    capacity = block_slots(ctx_count, tok_count)
    slot_total = expert_count * capacity
    recv_total = ctx_count * capacity
    flat_routes = routes.reshape(-1)
    onehot = (flat_routes[:, None] == jnp.arange(expert_count, dtype=jnp.int32)[None, :]).astype(
        jnp.int32
    )
    slot_rank = jnp.sum((jnp.cumsum(onehot, axis=0) - 1) * onehot, axis=1)
    slot_index = flat_routes * capacity + slot_rank
    position = jnp.arange(tok_count * TOPK, dtype=jnp.int32) // TOPK
    slot_source = jnp.full((slot_total,), tok_count, jnp.int32).at[slot_index].set(position)
    gate_local = w_gate[0]
    up_local = w_up[0]
    down_local = w_down[0]
    gathered = lax.all_gather(normed, ("tp", "sub"), axis=1, tiled=True)
    padded = jnp.concatenate([gathered, jnp.zeros((1, gathered.shape[1]), gathered.dtype)], axis=0)
    filled = padded[slot_source].reshape(expert_count, capacity, gathered.shape[1])
    arrived = lax.all_to_all(
        jnp.repeat(filled, 2, axis=0), "ctx", split_axis=0, concat_axis=0, tiled=True
    ).reshape(recv_total, gathered.shape[1])
    gate_sum = jnp.dot(arrived, gate_local, preferred_element_type=jnp.float32)
    up_sum = jnp.dot(arrived, up_local, preferred_element_type=jnp.float32)
    hidden = (jax.nn.silu(gate_sum) * up_sum).astype(jnp.bfloat16)
    down_rows_out = jnp.dot(
        lax.all_gather(hidden, ("tp", "sub"), axis=1, tiled=True),
        down_local,
        preferred_element_type=jnp.float32,
    ).astype(jnp.bfloat16)
    returned = lax.all_to_all(
        down_rows_out.reshape(ctx_count, capacity, feat_width),
        "ctx",
        split_axis=0,
        concat_axis=0,
        tiled=True,
    )
    combined = jnp.sum(
        returned.reshape(expert_count, 2, capacity, feat_width).astype(jnp.float32), axis=1
    ).reshape(slot_total, feat_width)
    picked = combined[slot_index].reshape(tok_count, TOPK, feat_width)
    mixed = hand_f32 + jnp.sum(route_gates[:, :, None] * picked, axis=1)
    return mixed.astype(jnp.bfloat16)


def block_slots(ctx, tok):
    return min(tok, max(2, tok * 10 // ctx))


def fits(mesh, resid):
    ctx, tp = mesh.shape["ctx"], mesh.shape["tp"]
    heads = resid.shape[1] // tp // HD
    tok = resid.shape[0] // mesh.shape["groups"] // ctx
    slots = ctx // 4 * block_slots(ctx, tok)
    whole = heads == ctx and 2 * tok == LANES and slots % 16 == 0
    return tp == 2 and mesh.shape["sub"] == 1 and whole and ctx >= 8 and ctx & (ctx - 1) == 0


def solution(mesh):
    placed = (
        P(("groups", "ctx"), ("tp", "sub")),
        P(("groups", "ctx"), ("tp", "sub")),
        P(("groups", "ctx"), ("tp", "sub")),
        P(("groups", "ctx"), ("tp", "sub")),
        P(("tp", "sub")),
        P(("groups", "ctx"), None),
        P(("groups", "ctx"), None),
        P(("groups", "ctx")),
        P("ctx", None, ("tp", "sub")),
        P("ctx", None, ("tp", "sub")),
        P("ctx", None, ("tp", "sub")),
    )

    def step(resid, *rest):
        per_device = heads_over_ctx if fits(mesh, resid) else general
        return jax.shard_map(
            per_device,
            mesh=mesh,
            in_specs=placed,
            out_specs=P(("groups", "ctx"), ("tp", "sub")),
            check_vma=False,
        )(resid, *rest)

    return step
```
